256 devices in a mesh: ent: 128 (over z, x, y), grp: 2 (over core).
Axes of the slice: x: 4, y: 4, z: 8, core: 2. Of those that a mesh axis runs over, the one named last changes fastest.
Arguments:
- slab: float32 [294912, 800], P(('ent', 'grp')), may hold values from -42 to 42
- slab_owner: int32 [294912, 1], P(('ent', 'grp')), may hold values from 0 to 127; in each aligned block of 1152 rows (0 to 1151, 1152 to 2303, ...) at most 18 rows name the same one
- slab_row: int32 [294912], P(('ent', 'grp')), may hold values from 0 to 511
- rel_slab: float32 [32768, 800], P(('ent', 'grp')), may hold values from -1.8 to 1.8
- rel_owner: int32 [32768, 1], P(('ent', 'grp')), may hold values from 0 to 127; in each aligned block of 128 rows (0 to 127, 128 to 255, ...) at most 4 rows name the same one
- rel_row: int32 [32768], P(('ent', 'grp')), may hold values from 0 to 115
- heads: int32 [131072], P(('ent', 'grp')), may hold values from 0 to 127
- tails: int32 [131072], P(('ent', 'grp')), may hold values from 0 to 127
- rels: int32 [131072], P(('ent', 'grp')), may hold values from 0 to 127
- weights: float32 [131072], P(('ent', 'grp')), may hold values from 0.5 to 2
Outputs:
- ent_grad: float32 [65536, 800], P('ent', 'grp')
- rel_grad: float32 [14848, 800], P('ent', 'grp')
The draws below stay inside these ranges and needn't reach their ends.
Inputs may be any that keep to these rules, and one draw needn't show every extreme that they name: `slab_owner`: in the 1152 rows of one device no owner is named by more than 18 rows, a bound that some block reaches. `rel_owner`: in the 128 rows of one device no owner is named by more than 4 rows, a bound that some block reaches.
All inputs are finite; a program needn't handle non-finite values.
Results may differ from the reference program's by a relative error of at most 0.0003.
Values sent between devices are 32-bit elements; how exact they have to be, the bound alone decides.
A program may use at most 128 MiB of HBM per device.

```python
import math
import jax
import jax.numpy as jnp
import numpy as np
from jax import lax

K = 400
NEG = 1024
SPANS = 2
EB = 256
TOUCHED = 128
RSLAB = 128
ROWS_DEV = 512
REL_DEV = 116
SLAB = 1152
CAP = 18
RCAP = 4
EDGES = 512
ENTITIES = 65536
RELS = 14848
N_ENT = 128
N_GRP = 2
DEVICES = 256


def draw_slab(key, part):
    key = jax.random.fold_in(key, 7)
    base_key, scale_key = jax.random.split(key, 2)
    rows_all = DEVICES * SLAB
    position = jnp.arange(rows_all, dtype=jnp.int32) % SLAB
    touched = (position < TOUCHED)[:, None]
    spread = jnp.exp(jax.random.uniform(scale_key, (rows_all, 1), jnp.float32) * jnp.log(10.0))
    scales = jnp.where(touched, 0.3 * spread, 0.03 * spread)
    values = jnp.clip(jax.random.normal(base_key, (rows_all, 2 * K), jnp.float32), -4.0, 4.0)
    return values * scales


def touch_ends(result, key, low, high):
    extent = result.shape
    place = [jax.random.randint(jax.random.fold_in(key, axis), (), 0, extent[axis]) for axis in range(len(extent))]
    result = result.at[tuple(place)].set(low)
    longest = extent.index(max(extent))
    place[longest] = (place[longest] + 1) % extent[longest]
    return result.at[tuple(place)].set(high)


def shard_levels(key, dims, cuts, low, high):
    def one(dim, blocks):
        steps = jax.random.uniform(jax.random.fold_in(jax.random.fold_in(key, 6), dim), (blocks,), jnp.float32, low / len(cuts), high / len(cuts))
        return jnp.repeat(jnp.exp(steps), dims[dim] // blocks).reshape((-1,) + (1,) * (len(dims) - dim - 1))

    gain = one(*cuts[0])
    for cut in cuts[1:]:
        gain = gain * one(*cut)
    return gain


def assign_block(stream_key, own, number, rows, count, top, bound, skew):
    ranking = jax.random.permutation(stream_key, count)
    heavy_load, usual = portions_of(count, rows * top, bound, skew, True), portions_of(count, rows * top, bound, skew, False)
    places = jnp.arange(count)

    def named(lengths, turn):
        used = int((lengths > 0).sum())
        fixed = max(1, used // 4)
        passed = fixed + (places - fixed + turn * (used - fixed)) % max(1, count - fixed)
        return jnp.zeros((count,), jnp.int32).at[ranking[jnp.where(places < fixed, places, passed)]].set(jnp.asarray(lengths, jnp.int32))

    lengths = jnp.where(number % 4 == 0, named(heavy_load, number // 4), named(usual, number - number // 4 - 1))
    mixed = jax.random.permutation(jax.random.fold_in(own, 3), count)
    donor, sink = mixed[0:count // 2 * 2:2], mixed[1:count // 2 * 2:2]
    slack = jnp.minimum(lengths[donor] - 1, bound - lengths[sink]) // 2
    slack = jnp.where((donor == ranking[0]) | (sink == ranking[0]) | (lengths[sink] == 0), 0, jnp.maximum(slack, 0))
    passed = jax.random.randint(jax.random.fold_in(own, 4), (count // 2,), 0, 1 << 20) % (slack + 1)
    lengths = lengths.at[donor].add(-passed).at[sink].add(passed)
    members = jnp.searchsorted(jnp.cumsum(lengths), jnp.arange(rows * top), side="right").astype(jnp.int32)
    table = members.reshape(top, rows).T
    table = table[jax.random.permutation(jax.random.fold_in(own, 1), rows)]
    turn = jax.random.randint(jax.random.fold_in(own, 2), (rows, 1), 0, top)
    return jnp.take_along_axis(table, (jnp.arange(top)[None, :] + turn) % top, axis=1)


def portions_of(amount, total, bound, skew, full):
    loads = [(1 << 20) // math.isqrt(grade ** skew) + 1 for grade in range(1, amount + 1)]
    largest = bound if full else min(bound, max(-(-total // amount), total * loads[0] // sum(loads)))
    least = 1 if total - largest >= amount - 1 else 0
    given, rest = [largest] + [least] * (amount - 1), total - largest - least * (amount - 1)
    while rest > 0:
        free = [i for i in range(1, amount) if given[i] < largest] or [i for i in range(1, amount) if given[i] < bound]
        pool, budget = sum([loads[i] for i in free]), rest
        for i in free:
            extra = min(bound - given[i], max(1, budget * loads[i] // pool), rest)
            given[i] = given[i] + extra
            rest = rest - extra
    return np.array(given)


def scatter_about(key, shape, scale, limit, pieces=(), kind=jnp.bfloat16):
    drawn = scale * jax.random.normal(key, shape, jnp.float32)
    if pieces:
        drawn = drawn * shard_levels(key, shape, pieces, -0.22, 0.18)
    return jnp.clip(drawn, -limit, limit).astype(kind)


def setup_inputs(seed: int = 0) -> dict:
    seeds = jax.random.split(jax.random.key(seed), 11)
    slab = draw_slab(jax.random.fold_in(seeds[10], 71), 0)
    slab_owner_keys = jax.random.split(jax.random.fold_in(seeds[1], 1), (DEVICES * SLAB) // SLAB)
    slab_owner_turns = jax.random.permutation(jax.random.fold_in(seeds[1], 3), (DEVICES * SLAB) // SLAB)
    slab_owner = jax.vmap(lambda own, number: assign_block(jax.random.fold_in(seeds[1], 2), own, number, SLAB, N_ENT, 1, CAP, 2))(slab_owner_keys, slab_owner_turns).reshape((DEVICES * SLAB, 1))
    slab_row = touch_ends(jax.random.randint(seeds[2], (DEVICES * SLAB,), 0, ROWS_DEV), jax.random.fold_in(seeds[2], 1), 0, ROWS_DEV - 1).astype(jnp.int32)
    rel_slab = scatter_about(seeds[3], (DEVICES * RSLAB, 2 * K), 0.3, 1.8, ((0, 256),), jnp.float32)
    rel_owner_keys = jax.random.split(jax.random.fold_in(seeds[4], 1), (DEVICES * RSLAB) // RSLAB)
    rel_owner_turns = jax.random.permutation(jax.random.fold_in(seeds[4], 3), (DEVICES * RSLAB) // RSLAB)
    rel_owner = jax.vmap(lambda own, number: assign_block(jax.random.fold_in(seeds[4], 2), own, number, RSLAB, N_ENT, 1, RCAP, 2))(rel_owner_keys, rel_owner_turns).reshape((DEVICES * RSLAB, 1))
    rel_row = touch_ends(jax.random.randint(seeds[5], (DEVICES * RSLAB,), 0, REL_DEV), jax.random.fold_in(seeds[5], 1), 0, REL_DEV - 1).astype(jnp.int32)
    heads = touch_ends(jax.random.randint(seeds[6], (DEVICES * EDGES,), 0, TOUCHED), jax.random.fold_in(seeds[6], 1), 0, TOUCHED - 1).astype(jnp.int32)
    tails = touch_ends(jax.random.randint(seeds[7], (DEVICES * EDGES,), 0, TOUCHED), jax.random.fold_in(seeds[7], 1), 0, TOUCHED - 1).astype(jnp.int32)
    rels = touch_ends(jax.random.randint(seeds[8], (DEVICES * EDGES,), 0, RSLAB), jax.random.fold_in(seeds[8], 1), 0, RSLAB - 1).astype(jnp.int32)
    weights = jnp.clip(jnp.exp(math.log(2.0) - 1.3862944 * jax.random.uniform(seeds[9], (DEVICES * EDGES,), jnp.float32) ** shard_levels(seeds[9], (DEVICES * EDGES,), ((0, 256),), -0.2, 0.2)), 0.5, 2.0)
    return {"slab": slab, "slab_owner": slab_owner, "slab_row": slab_row, "rel_slab": rel_slab, "rel_owner": rel_owner, "rel_row": rel_row, "heads": heads, "tails": tails, "rels": rels, "weights": weights}


highest = lax.Precision.HIGHEST


def complex_product(left, right, complex_width):
    left_real, left_imag = left[:, :complex_width], left[:, complex_width:]
    right_real, right_imag = right[:, :complex_width], right[:, complex_width:]
    return jnp.concatenate([left_real * right_real - left_imag * right_imag,
                            left_real * right_imag + left_imag * right_real], axis=1)


def conj_product(grads, other, complex_width):
    grad_real, grad_imag = grads[:, :complex_width], grads[:, complex_width:]
    other_real, other_imag = other[:, :complex_width], other[:, complex_width:]
    return jnp.concatenate([grad_real * other_real + grad_imag * other_imag,
                            grad_imag * other_real - grad_real * other_imag], axis=1)


def pair_grads(slabs, rel_slabs, head_ids, tail_ids, rel_ids, edge_weights):
    half_neg = NEG // 2
    slab_grad = jnp.zeros_like(slabs)
    relation_grad = jnp.zeros_like(rel_slabs)
    for block_index in range(SPANS):
        neg_start = TOUCHED + block_index * half_neg
        negatives = jnp.concatenate([slabs[0, neg_start:neg_start + half_neg],
                                     slabs[1, neg_start:neg_start + half_neg]], axis=0)
        neg_grad = jnp.zeros((NEG, 2 * K), jnp.float32)
        for core in range(2):
            head_take = head_ids[core, block_index]
            tail_take = tail_ids[core, block_index]
            rel_take = rel_ids[core, block_index]
            edge_weight = edge_weights[core, block_index]
            head_rows = slabs[core][head_take]
            tail_rows = slabs[core][tail_take]
            relation_rows = rel_slabs[core][rel_take]
            queries = complex_product(head_rows, relation_rows, K)
            positive = jnp.sum(queries * tail_rows, axis=1)
            scores = jnp.dot(queries, negatives.T, precision=highest)
            peak = jnp.maximum(jnp.max(scores, axis=1), positive)
            partition = jnp.exp(positive - peak) + jnp.sum(jnp.exp(scores - peak[:, None]), axis=1)
            grad_pos = edge_weight * (jnp.exp(positive - peak) / partition - 1.0)
            grad_neg = edge_weight[:, None] * jnp.exp(scores - peak[:, None]) / partition[:, None]
            query_grad = grad_pos[:, None] * tail_rows + jnp.dot(grad_neg, negatives, precision=highest)
            neg_grad = neg_grad + jnp.dot(grad_neg.T, queries, precision=highest)
            slab_grad = slab_grad.at[core, head_take].add(conj_product(query_grad, relation_rows, K))
            slab_grad = slab_grad.at[core, tail_take].add(grad_pos[:, None] * queries)
            relation_grad = relation_grad.at[core, rel_take].add(conj_product(query_grad, head_rows, K))
        slab_grad = slab_grad.at[0, neg_start:neg_start + half_neg].add(neg_grad[:half_neg])
        slab_grad = slab_grad.at[1, neg_start:neg_start + half_neg].add(neg_grad[half_neg:])
    return slab_grad, relation_grad


def reference(slab, slab_owner, slab_row, rel_slab, rel_owner, rel_row, heads, tails, rels, weights):
    columns = 2 * K
    slabs = slab.reshape(N_ENT, N_GRP, SLAB, columns)
    rel_slabs = rel_slab.reshape(N_ENT, N_GRP, RSLAB, columns)
    slab_index = (slab_owner[:, 0] * ROWS_DEV + slab_row).astype(jnp.int32).reshape(N_ENT, N_GRP * SLAB)
    rel_index = (rel_owner[:, 0] * REL_DEV + rel_row).astype(jnp.int32).reshape(N_ENT, N_GRP * RSLAB)
    head_ids = heads.reshape(N_ENT, N_GRP, SPANS, EB)
    tail_ids = tails.reshape(N_ENT, N_GRP, SPANS, EB)
    rel_ids = rels.reshape(N_ENT, N_GRP, SPANS, EB)
    edge_weights = weights.reshape(N_ENT, N_GRP, SPANS, EB)

    def owner_step(totals, ent_index):
        ent_total, rel_total = totals
        slab_grad, relation_grad = pair_grads(slabs[ent_index], rel_slabs[ent_index], head_ids[ent_index],
                                              tail_ids[ent_index], rel_ids[ent_index], edge_weights[ent_index])
        ent_total = ent_total.at[slab_index[ent_index]].add(slab_grad.reshape(N_GRP * SLAB, columns))
        rel_total = rel_total.at[rel_index[ent_index]].add(relation_grad.reshape(N_GRP * RSLAB, columns))
        return (ent_total, rel_total), None

    start_totals = (jnp.zeros((ENTITIES, columns), jnp.float32), jnp.zeros((RELS, columns), jnp.float32))
    (ent_grad, rel_grad), unused = lax.scan(owner_step, start_totals, jnp.arange(N_ENT, dtype=jnp.int32))
    return ent_grad, rel_grad
```

```python
import jax
import jax.numpy as jnp
from jax import lax
from jax.experimental import pallas as pl
from jax.experimental.pallas import tpu as pltpu
from jax.sharding import PartitionSpec as P

K = 400
HALF = 512
W = 2 * HALF
EB = 256
SPANS = 2
EDGES = EB * SPANS
TOUCHED = 128
NEGS = 512
SLAB = 1152
RSLAB = 128
ROWS = SLAB + RSLAB
ROWS_DEV = 512
REL_DEV = 116
NZ, NX, NY = 8, 4, 4
CLASSES = NX * NY
CAP, RCAP = 18, 4
SLOTS = CAP + RCAP
CSLOTS = SLOTS * NZ
PEERS = 2 * CLASSES
DEPTH = PEERS * SLOTS
TABLE = 640
CHUNKS = 3
REM = K - 128 * CHUNKS
GW = 2 * 128 * CHUNKS
MiB = 2**20

F32 = jnp.float32
BF = jnp.bfloat16
MESH = pl.DeviceIdType.MESH


def split2(x):
    hi = x.astype(BF)
    return hi, (x - hi.astype(F32)).astype(BF)


def split3(x):
    hi = x.astype(BF)
    rest = x - hi.astype(F32)
    mid = rest.astype(BF)
    return hi, mid, (rest - mid.astype(F32)).astype(BF)


def dot_nn(a, b):
    return lax.dot_general(a, b, (((1,), (0,)), ((), ())), preferred_element_type=F32)


def dot_nt(a, b):
    return lax.dot_general(a, b, (((1,), (1,)), ((), ())), preferred_element_type=F32)


def rows_of(i, n):
    return pl.ds(pl.multiple_of(i * n, n), n)


def local_kernel(slab, rel, hc, tc, rc, hr, tr, rr, wc, ghi, glo,
                 pad, tabs, nparts, hbuf, rbuf, tbuf, pos, qown, qoth, qparts, scores, stat_own, stat_oth,
                 mown, gnb, qg_out, qg_in, qg_own, terms, sends, recvs):
    ent, grp = lax.axis_index("ent"), lax.axis_index("grp")
    peer = (ent, 1 - grp)
    barrier = pltpu.get_barrier_semaphore()
    pl.semaphore_signal(barrier, inc=1, device_id=peer, device_id_type=MESH)

    def remote(src, dst, i):
        return pltpu.make_async_remote_copy(src, dst, sends.at[i], recvs.at[i], device_id=peer, device_id_type=MESH)

    pad[...] = jnp.zeros_like(pad)

    def padded(x):
        pad[:, 0:K] = x[:, 0:K]
        pad[:, HALF:HALF + K] = x[:, K:2 * K]
        return pad[...]

    for i, source in enumerate((slab, rel)):
        for j, part in enumerate(split3(padded(source[0:128, :]))):
            tabs[i, j] = part

    lane128 = lax.broadcasted_iota(jnp.int32, (128, 128), 1)

    def gathered(idx, i, rows):
        onehot = jnp.where(idx[rows, :] == lane128, 1.0, 0.0).astype(BF)
        return dot_nn(onehot, tabs[i, 0]) + dot_nn(onehot, tabs[i, 1]) + dot_nn(onehot, tabs[i, 2])

    @pl.loop(0, EDGES // 128)
    def _(i):
        rows = rows_of(i, 128)
        h = gathered(hc, 0, rows)
        r = gathered(rc, 1, rows)
        hbuf[rows, :] = h
        rbuf[rows, :] = r
        hre, him, rre, rim = h[:, :HALF], h[:, HALF:], r[:, :HALF], r[:, HALF:]
        qown[rows, 0:HALF] = hre * rre - him * rim
        qown[rows, HALF:W] = hre * rim + him * rre

    pl.semaphore_wait(barrier, 1)
    q_copy = remote(qown, qoth, 0)
    q_copy.start()

    @pl.loop(0, 2 * NEGS // 128)
    def _(i):
        x = slab[pl.ds(pl.multiple_of(TOUCHED + i * 128, 128), 128), :]
        for j, part in enumerate(split3(padded(x))):
            nparts[j, rows_of(i, 128), :] = part

    @pl.loop(0, EDGES // 128)
    def _(i):
        rows = rows_of(i, 128)
        t = gathered(tc, 0, rows)
        tbuf[rows, :] = t
        q = qown[rows, :]
        pos[rows, :] = jnp.sum(q * t, axis=1, keepdims=True)
        place = pl.ds(pl.multiple_of((i // 2) * (2 * EB) + (i % 2) * 128, 128), 128)
        for j, part in enumerate(split3(q)):
            qparts[j, place, :] = part

    def score(b, first):
        for i in range(2):
            rows = pl.ds(b * 2 * EB + first + i * 128, 128)
            q = [qparts[j, rows, :] for j in range(3)]
            n = [nparts[j, pl.ds(b * NEGS, NEGS), :] for j in range(3)]
            small = dot_nt(q[0], n[2]) + dot_nt(q[2], n[0]) + dot_nt(q[1], n[1])
            scores[rows, :] = (small + (dot_nt(q[0], n[1]) + dot_nt(q[1], n[0]))) + dot_nt(q[0], n[0])

    for b in range(SPANS):
        score(b, 0)
    q_copy.wait()

    @pl.loop(0, EDGES // 128)
    def _(i):
        place = pl.ds(pl.multiple_of((i // 2) * (2 * EB) + EB + (i % 2) * 128, 128), 128)
        for j, part in enumerate(split3(qoth[rows_of(i, 128), :])):
            qparts[j, place, :] = part

    for b in range(SPANS):
        score(b, EB)

    lane = lax.broadcasted_iota(jnp.int32, (EB, 128), 1)
    for b in range(SPANS):
        for own in range(2):
            rows = pl.ds(b * 2 * EB + (1 - own) * EB, EB)
            s = scores[rows, :]
            m = jnp.max(s, axis=1, keepdims=True)
            if own:
                p = pos[pl.ds(b * EB, EB), :]
                m = jnp.maximum(m, p)
            e = jnp.exp(s - m)
            total = jnp.sum(e, axis=1, keepdims=True)
            weight = jnp.zeros_like(total)
            if own:
                total = total + jnp.exp(p - m)
                weight = wc[pl.ds(b * EB, EB), :]
            scores[rows, :] = e
            stat_own[rows, :] = jnp.where(lane == 0, m, jnp.where(lane == 1, total, weight))
    stat_copy = remote(stat_own, stat_oth, 1)
    stat_copy.start()
    stat_copy.wait()

    qg_copies = []
    for b in range(SPANS):
        for own in range(2):
            rows = pl.ds(b * 2 * EB + (1 - own) * EB, EB)
            theirs = pl.ds(b * 2 * EB + own * EB, EB)
            a, o = stat_own[rows, :], stat_oth[theirs, :]
            m1, l1, m2, l2 = a[:, 0:1], a[:, 1:2], o[:, 0:1], o[:, 1:2]
            w = a[:, 2:3] if own else o[:, 2:3]
            peak = jnp.maximum(m1, m2)
            f1 = jnp.exp(m1 - peak)
            total = l1 * f1 + l2 * jnp.exp(m2 - peak)
            scale = w / total
            if own:
                mown[pl.ds(b * EB, EB), :] = w * (jnp.exp(pos[pl.ds(b * EB, EB), :] - peak) / total - 1.0)
            gn = scores[rows, :] * (f1 * scale)
            scores[rows, :] = gn
            hi, lo = split2(gn)
            negs = pl.ds(b * NEGS, NEGS)
            part = dot_nn(hi, nparts[1, negs, :]) + dot_nn(lo, nparts[0, negs, :]) + dot_nn(hi, nparts[0, negs, :])
            if own:
                qg_own[pl.ds(b * EB, EB), :] = part
            else:
                qg_out[pl.ds(b * EB, EB), :] = part
                copy = remote(qg_out.at[pl.ds(b * EB, EB)], qg_in.at[pl.ds(b * EB, EB)], 2 + b)
                copy.start()
                qg_copies.append(copy)

    def put(rows, value):
        for k in range(CHUNKS):
            for g in range(2):
                lanes = pl.ds((2 * k + g) * 128, 128)
                hi, lo = split2(value[:, g * HALF + 128 * k:g * HALF + 128 * (k + 1)])
                ghi[rows, lanes] = hi
                glo[rows, lanes] = lo
        rest = value[:, HALF - 128:HALF] + pltpu.roll(value[:, W - 128:W], REM, 1)
        hi = rest.astype(BF).astype(F32)
        lo = (rest - hi).astype(BF).astype(F32)
        ghi[rows, pl.ds(GW, 128)] = (hi + pltpu.roll(lo, 2 * REM, 1)).astype(BF)

    for b in range(SPANS):
        gnt = jnp.transpose(scores[pl.ds(b * 2 * EB, 2 * EB), :])
        for j, part in enumerate(split2(gnt)):
            gnb[j] = part

        @pl.loop(0, NEGS // 128)
        def _(i):
            hi, lo = gnb[0, rows_of(i, 128), :], gnb[1, rows_of(i, 128), :]
            edges = pl.ds(b * 2 * EB, 2 * EB)
            value = dot_nn(hi, qparts[1, edges, :]) + dot_nn(lo, qparts[0, edges, :]) + dot_nn(hi, qparts[0, edges, :])
            put(pl.ds(pl.multiple_of(TOUCHED + b * NEGS + i * 128, 128), 128), value)

    for copy in qg_copies:
        copy.wait()

    @pl.loop(0, EDGES // 128)
    def _(i):
        rows = rows_of(i, 128)
        gp = mown[rows, :]
        g = gp * tbuf[rows, :] + (qg_own[rows, :] + qg_in[rows, :])
        h, r = hbuf[rows, :], rbuf[rows, :]
        gre, gim = g[:, :HALF], g[:, HALF:]
        for n, other in ((0, r), (2, h)):
            ore, oim = other[:, :HALF], other[:, HALF:]
            for half, value in enumerate((gre * ore + gim * oim, gim * ore - gre * oim)):
                hi, lo = split2(value)
                terms[2 * n, rows, half * HALF:(half + 1) * HALF] = hi
                terms[2 * n + 1, rows, half * HALF:(half + 1) * HALF] = lo
        hi, lo = split2(gp * qown[rows, :])
        terms[2, rows, :] = hi
        terms[3, rows, :] = lo

    row128 = lax.broadcasted_iota(jnp.int32, (128, EDGES), 0)

    def spread(idx, n):
        onehot = jnp.where(idx[...] == row128, 1.0, 0.0).astype(BF)
        return dot_nn(onehot, terms[2 * n + 1]) + dot_nn(onehot, terms[2 * n])

    put(pl.ds(0, 128), spread(hr, 0) + spread(tr, 1))
    put(pl.ds(SLAB, 128), spread(rr, 2))


def offsets(j):
    return j // NY, j % NY


def route_kernel(ghi, glo, owner, target, ent_out, rel_out,
                 kpos, ids_send, ids_recv, perm, place, sbuf, srem, rbuf, rrem, xrem,
                 tables, tab_rem, plus, minus, plus_rem, minus_rem,
                 ids_ss, ids_rs, s_ss, s_rs, own_sem, p_ss, p_rs, m_ss, m_rs):
    ent, grp = lax.axis_index("ent"), lax.axis_index("grp")
    z, c = ent // CLASSES, ent % CLASSES
    x, y = c // NY, c % NY

    def class_at(j):
        dx, dy = j // NY, j % NY
        return ((x + dx) % NX) * NY + (y + dy) % NY

    def peer(j, f):
        return (z * CLASSES + class_at(j), (grp + f) % 2)

    def chip_z(dz):
        return (((z + dz) % NZ) * CLASSES + c, grp)

    barrier = pltpu.get_barrier_semaphore()

    @pl.loop(0, CLASSES)
    def _(j):
        @pl.when(j > 0)
        def _():
            pl.semaphore_signal(barrier, inc=1, device_id=peer(j, 0), device_id_type=MESH)
        pl.semaphore_signal(barrier, inc=1, device_id=peer(j, 1), device_id_type=MESH)

    pl.semaphore_signal(barrier, inc=1, device_id=chip_z(1), device_id_type=MESH)
    pl.semaphore_signal(barrier, inc=1, device_id=chip_z(NZ - 1), device_id_type=MESH)

    own = owner[...]
    oclass, oz = own % CLASSES, own // CLASSES
    orow = oclass * NZ + oz
    onehot = jnp.where(lax.broadcasted_iota(jnp.int32, (128, ROWS), 0) == orow, 1.0, 0.0)
    for start, size, first in ((0, SLAB, 0), (SLAB, RSLAB, CAP)):
        part = onehot[:, start:start + size]
        upper = lax.broadcasted_iota(jnp.int32, (size, size), 0) <= lax.broadcasted_iota(jnp.int32, (size, size), 1)
        count = dot_nn(part.astype(BF), jnp.where(upper, 1.0, 0.0).astype(BF))
        kpos[:, start:start + size] = jnp.sum(part * count, axis=0, keepdims=True) + (first - 1.0)
    kth = kpos[...].astype(jnp.int32)
    slot = oclass * CSLOTS + kth * NZ + oz

    kth_hot = jnp.where(lax.broadcasted_iota(jnp.int32, (128, ROWS), 0) == kth, 1.0, 0.0).astype(BF)
    number = target[...] + 1
    high = ((number // 16) * 16).astype(F32)
    low = (number % 16).astype(F32)
    ids = dot_nt((onehot * high).astype(BF), kth_hot) + dot_nt((onehot * low).astype(BF), kth_hot)
    ids_send[...] = ids.astype(jnp.int32) - 1

    pl.semaphore_wait(barrier, PEERS - 1 + 2)

    def ids_copy(j, f):
        return pltpu.make_async_remote_copy(
            ids_send.at[pl.ds(pl.multiple_of(class_at(j) * NZ, NZ), NZ)], ids_recv.at[j * 2 + f],
            ids_ss.at[j * 2 + f], ids_rs.at[j * 2 + f], device_id=peer(j, f), device_id_type=MESH)

    def for_peers(act):
        @pl.loop(0, CLASSES)
        def _(j):
            @pl.when(j > 0)
            def _():
                act(j, 0)
            act(j, 1)

    for_peers(lambda j, f: ids_copy(j, f).start())
    ids_recv[0] = ids_send[pl.ds(pl.multiple_of(c * NZ, NZ), NZ), :]

    def chunk_copy(k, j, f):
        g = (grp + f) % 2
        return pltpu.make_async_remote_copy(
            sbuf.at[k, g, pl.ds(pl.multiple_of(class_at(j) * CSLOTS, CSLOTS), CSLOTS)],
            rbuf.at[k, pl.ds(pl.multiple_of((j * 2 + f) * CSLOTS, CSLOTS), CSLOTS)],
            s_ss.at[k, j * 2 + f], s_rs.at[k, j * 2 + f], device_id=peer(j, f), device_id_type=MESH)

    def own_copy(k):
        return pltpu.make_async_copy(
            sbuf.at[k, grp, pl.ds(pl.multiple_of(c * CSLOTS, CSLOTS), CSLOTS)], rbuf.at[k, pl.ds(0, CSLOTS)], own_sem.at[k])

    def rem_copy(j, f):
        g = (grp + f) % 2
        return pltpu.make_async_remote_copy(
            srem.at[class_at(j), g], rrem.at[j * 2 + f],
            s_ss.at[CHUNKS, j * 2 + f], s_rs.at[CHUNKS, j * 2 + f], device_id=peer(j, f), device_id_type=MESH)

    def own_rem():
        return pltpu.make_async_copy(srem.at[c, grp], rrem.at[0], own_sem.at[CHUNKS])

    slot_row = lax.broadcasted_iota(jnp.int32, (CSLOTS, ROWS), 0)

    def send_chunk(k):
        @pl.loop(0, CLASSES)
        def _(j):
            cls = class_at(j)
            rows = pl.ds(pl.multiple_of(cls * CSLOTS, CSLOTS), CSLOTS)
            if k == 0:
                perm[rows, :] = jnp.where(slot_row == slot - cls * CSLOTS, 1.0, 0.0).astype(BF)
            lanes = pl.ds(k * 256, 256)
            value = dot_nn(perm[rows, :], glo[:, lanes]) + dot_nn(perm[rows, :], ghi[:, lanes])
            sbuf[k, 0, rows, :] = value[:, :128]
            sbuf[k, 1, rows, :] = value[:, 128:]

            @pl.when(j > 0)
            def _():
                chunk_copy(k, j, 0).start()
            chunk_copy(k, j, 1).start()
        own_copy(k).start()

    def send_rem():
        @pl.loop(0, CLASSES)
        def _(j):
            cls = class_at(j)
            rows = pl.ds(pl.multiple_of(cls * CSLOTS, CSLOTS), CSLOTS)
            value = jnp.transpose(dot_nn(perm[rows, :], ghi[:, pl.ds(GW, 128)]))
            value = value[0:2 * REM, :] + value[2 * REM:4 * REM, :]
            srem[cls, 0, :, 0:CSLOTS] = value[0:REM, :]
            srem[cls, 1, :, 0:CSLOTS] = value[REM:2 * REM, :]

            @pl.when(j > 0)
            def _():
                rem_copy(j, 0).start()
            rem_copy(j, 1).start()
        own_rem().start()

    def wait_chunk(k):
        if k < CHUNKS:
            for_peers(lambda j, f: chunk_copy(k, j, f).wait_recv())
            own_copy(k).wait()
        else:
            for_peers(lambda j, f: rem_copy(j, f).wait_recv())
            own_rem().wait()

    def ring_copy(k, s, sign, o):
        buf, ss, rs = (plus, p_ss, p_rs) if sign > 0 else (minus, m_ss, m_rs)
        if k < CHUNKS:
            src, dst = tables.at[k, o], buf.at[k, s]
            if s == 0:
                half = pl.ds(0 if sign > 0 else TABLE // 2, TABLE // 2)
                src, dst = src.at[half], dst.at[half]
        else:
            buf = plus_rem if sign > 0 else minus_rem
            src, dst = tab_rem.at[o], buf.at[s]
            if s == 0:
                half = pl.ds(0 if sign > 0 else REM // 2, REM // 2)
                src, dst = src.at[half], dst.at[half]
        return pltpu.make_async_remote_copy(src, dst, ss.at[k, s], rs.at[k, s], device_id=chip_z(sign % NZ), device_id_type=MESH)

    def ring_start(k, s):
        ring_copy(k, s, 1, (z + 4 - s) % NZ).start()
        ring_copy(k, s, -1, (z + 4 + s) % NZ).start()

    def ring_finish(k, s):
        for sign in (1, -1):
            ring_copy(k, s, sign, (z + sign * (3 - s) + NZ) % NZ).wait_recv()
            if s == 3:
                continue
            o = (z + sign * (3 - s) + NZ) % NZ
            if k < CHUNKS:
                buf = plus if sign > 0 else minus
                half = pl.ds(0, TABLE) if s else pl.ds(0 if sign > 0 else TABLE // 2, TABLE // 2)
                tables[k, o, half, :] = tables[k, o, half, :] + buf[k, s, half, :]
            else:
                buf = plus_rem if sign > 0 else minus_rem
                half = pl.ds(0, REM) if s else pl.ds(0 if sign > 0 else REM // 2, REM // 2)
                tab_rem[o, half, :] = tab_rem[o, half, :] + buf[s, half, :]

    def build_place():
        for_peers(lambda j, f: ids_copy(j, f).wait_recv())
        got = jnp.concatenate([ids_recv[s][:, 0:SLOTS] for s in range(PEERS)], axis=1)
        row = lax.broadcasted_iota(jnp.int32, (TABLE, DEPTH), 0)
        for o in range(NZ):
            place[o] = jnp.where(row == got[o:o + 1, :], 1.0, 0.0).astype(BF)

    def add_up(k):
        if k < CHUNKS:
            for o in range(NZ):
                hi, lo = split2(rbuf[k, pl.ds(o, DEPTH, stride=NZ), :])
                value = dot_nn(place[o], jnp.concatenate([hi, lo], axis=1))
                tables[k, o] = value[:, :128] + value[:, 128:]
        else:
            xrem[...] = jnp.zeros_like(xrem)
            for s in range(PEERS):
                xrem[pl.ds(s * CSLOTS, CSLOTS), 0:REM] = jnp.transpose(rrem[s])[0:CSLOTS, :]
            total = jnp.zeros((TABLE, 256), F32)
            for o in range(NZ):
                value = xrem[pl.ds(o, DEPTH, stride=NZ), :]
                value = pltpu.roll(value, REM * o, 1) if o else value
                hi, lo = split2(value)
                total = total + dot_nn(place[o], jnp.concatenate([hi, lo], axis=1))
            total = jnp.transpose(total[:, :128] + total[:, 128:])
            for o in range(NZ):
                tab_rem[o] = total[o * REM:(o + 1) * REM, :]

    for k in range(CHUNKS):
        send_chunk(k)
    send_rem()
    build_place()
    for k in range(CHUNKS + 1):
        wait_chunk(k)
        add_up(k)
        ring_start(k, 0)
        for s in range(4):
            ring_finish(k, s)
            if s < 3:
                ring_start(k, s + 1)
        if k < CHUNKS:
            total = tables[k, z] + (plus[k, 3] + minus[k, 3])
            lanes = pl.ds(k * 128, 128)
        else:
            total = jnp.transpose(tab_rem[z] + (plus_rem[3] + minus_rem[3]))
            lanes = pl.ds(k * 128, REM)
        ent_out[:, lanes] = total[0:ROWS_DEV, :]
        rel_out[:, lanes] = total[ROWS_DEV:ROWS_DEV + REL_DEV, :]

    for_peers(lambda j, f: ids_copy(j, f).wait_send())
    for k in range(CHUNKS):
        for_peers(lambda j, f: chunk_copy(k, j, f).wait_send())
    for_peers(lambda j, f: rem_copy(j, f).wait_send())
    for k in range(CHUNKS + 1):
        for s in range(4):
            ring_copy(k, s, 1, (z + 4 - s) % NZ).wait_send()
            ring_copy(k, s, -1, (z + 4 + s) % NZ).wait_send()


def vmem():
    return pl.BlockSpec(memory_space=pltpu.VMEM)


def local_call(*args):
    dma = pltpu.SemaphoreType.DMA
    return pl.pallas_call(
        local_kernel,
        out_shape=(jax.ShapeDtypeStruct((ROWS, GW + 128), BF), jax.ShapeDtypeStruct((ROWS, GW), BF)),
        in_specs=[vmem()] * len(args),
        out_specs=(vmem(), vmem()),
        scratch_shapes=[
            pltpu.VMEM((128, W), F32),
            pltpu.VMEM((2, 3, 128, W), BF),
            pltpu.VMEM((3, 2 * NEGS, W), BF),
            pltpu.VMEM((EDGES, W), F32),
            pltpu.VMEM((EDGES, W), F32),
            pltpu.VMEM((EDGES, W), F32),
            pltpu.VMEM((EDGES, 1), F32),
            pltpu.VMEM((EDGES, W), F32),
            pltpu.VMEM((EDGES, W), F32),
            pltpu.VMEM((3, 2 * EDGES, W), BF),
            pltpu.VMEM((2 * EDGES, NEGS), F32),
            pltpu.VMEM((2 * EDGES, 128), F32),
            pltpu.VMEM((2 * EDGES, 128), F32),
            pltpu.VMEM((EDGES, 1), F32),
            pltpu.VMEM((2, NEGS, 2 * EB), BF),
            pltpu.VMEM((EDGES, W), F32),
            pltpu.VMEM((EDGES, W), F32),
            pltpu.VMEM((EDGES, W), F32),
            pltpu.VMEM((6, EDGES, W), BF),
            dma((4,)), dma((4,)),
        ],
        compiler_params=pltpu.CompilerParams(collective_id=0, has_side_effects=True, vmem_limit_bytes=60 * MiB),
        name="local",
    )(*args)


def route_call(*args):
    dma = pltpu.SemaphoreType.DMA
    return pl.pallas_call(
        route_kernel,
        out_shape=(jax.ShapeDtypeStruct((ROWS_DEV, K), F32), jax.ShapeDtypeStruct((REL_DEV, K), F32)),
        in_specs=[vmem()] * len(args),
        out_specs=(vmem(), vmem()),
        scratch_shapes=[
            pltpu.VMEM((1, ROWS), F32),
            pltpu.VMEM((128, 128), jnp.int32),
            pltpu.VMEM((PEERS, NZ, 128), jnp.int32),
            pltpu.VMEM((CLASSES * CSLOTS, ROWS), BF),
            pltpu.VMEM((NZ, TABLE, DEPTH), BF),
            pltpu.VMEM((CHUNKS, 2, CLASSES * CSLOTS, 128), F32),
            pltpu.VMEM((CLASSES, 2, REM, 256), F32),
            pltpu.VMEM((CHUNKS, PEERS * CSLOTS, 128), F32),
            pltpu.VMEM((PEERS, REM, 256), F32),
            pltpu.VMEM((PEERS * CSLOTS, 128), F32),
            pltpu.VMEM((CHUNKS, NZ, TABLE, 128), F32),
            pltpu.VMEM((NZ, REM, TABLE), F32),
            pltpu.VMEM((CHUNKS, 4, TABLE, 128), F32),
            pltpu.VMEM((CHUNKS, 4, TABLE, 128), F32),
            pltpu.VMEM((4, REM, TABLE), F32),
            pltpu.VMEM((4, REM, TABLE), F32),
            dma((PEERS,)), dma((PEERS,)),
            dma((CHUNKS + 1, PEERS)), dma((CHUNKS + 1, PEERS)), dma((CHUNKS + 1,)),
            dma((CHUNKS + 1, 4)), dma((CHUNKS + 1, 4)), dma((CHUNKS + 1, 4)), dma((CHUNKS + 1, 4)),
        ],
        compiler_params=pltpu.CompilerParams(collective_id=1, has_side_effects=True, vmem_limit_bytes=63 * MiB),
        name="route",
    )(*args)


def body(slab, slab_owner, slab_row, rel_slab, rel_owner, rel_row, heads, tails, rels, weights):
    column = [v.reshape(EDGES, 1) for v in (heads, tails, rels)]
    row = [v.reshape(1, EDGES) for v in (heads, tails, rels)]
    ghi, glo = local_call(slab, rel_slab, *column, *row, weights.reshape(EDGES, 1))
    owner = jnp.concatenate([slab_owner[:, 0], rel_owner[:, 0]]).reshape(1, ROWS)
    target = jnp.concatenate([slab_row, rel_row + ROWS_DEV]).reshape(1, ROWS)
    return route_call(ghi, glo, owner, target)


def solution(mesh):
    split = P(("ent", "grp"))
    wide = P(("ent", "grp"), None)
    in_specs = (wide, wide, split, wide, wide, split, split, split, split, split)
    out_specs = (P("ent", "grp"), P("ent", "grp"))
    return jax.shard_map(body, mesh=mesh, in_specs=in_specs, out_specs=out_specs, check_vma=False)
```

```python
import jax
import jax.numpy as jnp
from jax import lax
from jax.experimental import pallas as pl
from jax.experimental.pallas import tpu as pltpu
from jax.sharding import PartitionSpec as P

K = 400
HALF = 512
W = 2 * HALF
EB = 256
SPANS = 2
EDGES = EB * SPANS
TOUCHED = 128
NEGS = 512
SLAB = 1152
RSLAB = 128
ROWS = SLAB + RSLAB
ROWS_DEV = 512
REL_DEV = 116
NZ, NX, NY = 8, 4, 4
CLASSES = NX * NY
CAP, RCAP = 18, 4
SLOTS = CAP + RCAP
CSLOTS = SLOTS * NZ
PEERS = 2 * CLASSES
DEPTH = PEERS * SLOTS
TABLE = 640
RSLOTS = 24
WITH_REM = 1
TABLE_REM = 736
CHUNKS = 3
REM = K - 128 * CHUNKS
GW = 2 * 128 * CHUNKS
MiB = 2**20

F32 = jnp.float32
BF = jnp.bfloat16
MESH = pl.DeviceIdType.MESH


def split2(x):
    hi = x.astype(BF)
    return hi, (x - hi.astype(F32)).astype(BF)


def split3(x):
    hi = x.astype(BF)
    rest = x - hi.astype(F32)
    mid = rest.astype(BF)
    return hi, mid, (rest - mid.astype(F32)).astype(BF)


def dot_nn(a, b):
    return lax.dot_general(a, b, (((1,), (0,)), ((), ())), preferred_element_type=F32)


def dot_nt(a, b):
    return lax.dot_general(a, b, (((1,), (1,)), ((), ())), preferred_element_type=F32)


def rows_of(i, n):
    return pl.ds(pl.multiple_of(i * n, n), n)


def local_kernel(slab, rel, hr, tr, rr, weights, slab_owner, slab_row, rel_owner, rel_row, ghi, glo, slots, ids,
                 ints, kpos, zmask, tabs, nparts, hbuf, rbuf, tbuf, pos, qown, qoth, qparts, scores, stat_own, stat_oth,
                 mown, gnb, qg_out, qg_in, qg_own, terms, sends, recvs):
    ent, grp = lax.axis_index("ent"), lax.axis_index("grp")
    peer = (ent, 1 - grp)
    barrier = pltpu.get_barrier_semaphore()
    pl.semaphore_signal(barrier, inc=1, device_id=peer, device_id_type=MESH)

    def remote(src, dst, i):
        return pltpu.make_async_remote_copy(src, dst, sends.at[i], recvs.at[i], device_id=peer, device_id_type=MESH)

    def store_parts(ref, lanes, source):
        for start, first in ((0, 0), (K, HALF)):
            for j, part in enumerate(split3(source[start:start + K, :])):
                ref[j, first:first + K, lanes] = part
                ref[j, first + K:first + HALF, lanes] = jnp.zeros((HALF - K, part.shape[1]), BF)

    for i, source in enumerate((slab, rel)):
        store_parts(tabs.at[i], pl.ds(0, 128), source[:, 0:128])

    sub128 = lax.broadcasted_iota(jnp.int32, (128, 128), 0)

    def gathered(idx, i, rows):
        onehot = jnp.transpose(jnp.where(idx[:, rows] == sub128, 1.0, 0.0)).astype(BF)
        return dot_nt(onehot, tabs[i, 0]) + dot_nt(onehot, tabs[i, 1]) + dot_nt(onehot, tabs[i, 2])

    @pl.loop(0, EDGES // 128)
    def _(i):
        rows = rows_of(i, 128)
        h = gathered(hr, 0, rows)
        r = gathered(rr, 1, rows)
        hbuf[rows, :] = h
        rbuf[rows, :] = r
        hre, him, rre, rim = h[:, :HALF], h[:, HALF:], r[:, :HALF], r[:, HALF:]
        qown[rows, 0:HALF] = hre * rre - him * rim
        qown[rows, HALF:W] = hre * rim + him * rre

    pl.semaphore_wait(barrier, 1)
    q_copy = remote(qown, qoth, 0)
    q_copy.start()

    @pl.loop(0, 2 * NEGS // 128)
    def _(i):
        x = slab[:, pl.ds(pl.multiple_of(TOUCHED + i * 128, 128), 128)]
        store_parts(nparts, rows_of(i, 128), x)

    for n, (first, second) in enumerate(((slab_owner, rel_owner), (slab_row, rel_row))):
        ints[n:n + 1, 0:SLAB] = first[...]
        ints[n:n + 1, SLAB:ROWS] = second[...] + n * ROWS_DEV
    own = ints[0:1, :]
    oclass, oz = own % CLASSES, own // CLASSES
    owner_row = lax.broadcasted_iota(jnp.int32, (128, ROWS), 0)
    onehot = jnp.where(owner_row == oclass * NZ + oz, 1.0, 0.0)
    for start, size, offset in ((0, SLAB, 0), (SLAB, RSLAB, CAP)):
        part = onehot[:, start:start + size]
        upper = lax.broadcasted_iota(jnp.int32, (size, size), 0) <= lax.broadcasted_iota(jnp.int32, (size, size), 1)
        count = dot_nn(part.astype(BF), jnp.where(upper, 1.0, 0.0).astype(BF))
        kpos[:, start:start + size] = jnp.sum(part * count, axis=0, keepdims=True) + (offset - 1.0)
    kth = kpos[...].astype(jnp.int32)
    slots[0:1, :] = oclass * CSLOTS + kth * NZ + oz
    slots[1:2, :] = oclass * RSLOTS + kth
    for i in range(ROWS // 128):
        zmask[pl.ds(i * 128, 128), :] = jnp.transpose(jnp.where(oz[:, i * 128:(i + 1) * 128] == sub128 // REM, 1.0, 0.0))
    kth_hot = jnp.where(owner_row == kth, 1.0, 0.0).astype(BF)
    number = ints[1:2, :] + 1
    high = ((number // 16) * 16).astype(F32)
    low = (number % 16).astype(F32)
    ids[...] = (dot_nt((onehot * high).astype(BF), kth_hot) + dot_nt((onehot * low).astype(BF), kth_hot)).astype(jnp.int32) - 1

    @pl.loop(0, EDGES // 128)
    def _(i):
        rows = rows_of(i, 128)
        t = gathered(tr, 0, rows)
        tbuf[rows, :] = t
        q = qown[rows, :]
        pos[rows, :] = jnp.sum(q * t, axis=1, keepdims=True)
        place = pl.ds(pl.multiple_of((i // 2) * (2 * EB) + (i % 2) * 128, 128), 128)
        for j, part in enumerate(split3(q)):
            qparts[j, place, :] = part

    def score(b, first):
        for i in range(2):
            rows = pl.ds(b * 2 * EB + first + i * 128, 128)
            q = [qparts[j, rows, :] for j in range(3)]
            n = [nparts[j, :, pl.ds(b * NEGS, NEGS)] for j in range(3)]
            small = dot_nn(q[0], n[2]) + dot_nn(q[2], n[0]) + dot_nn(q[1], n[1])
            scores[rows, :] = (small + (dot_nn(q[0], n[1]) + dot_nn(q[1], n[0]))) + dot_nn(q[0], n[0])

    for b in range(SPANS):
        score(b, 0)
    q_copy.wait()

    @pl.loop(0, EDGES // 128)
    def _(i):
        place = pl.ds(pl.multiple_of((i // 2) * (2 * EB) + EB + (i % 2) * 128, 128), 128)
        for j, part in enumerate(split3(qoth[rows_of(i, 128), :])):
            qparts[j, place, :] = part

    for b in range(SPANS):
        score(b, EB)

    lane = lax.broadcasted_iota(jnp.int32, (EB, 128), 1)
    for b in range(SPANS):
        for own in range(2):
            rows = pl.ds(b * 2 * EB + (1 - own) * EB, EB)
            s = scores[rows, :]
            m = jnp.max(s, axis=1, keepdims=True)
            if own:
                p = pos[pl.ds(b * EB, EB), :]
                m = jnp.maximum(m, p)
            e = jnp.exp(s - m)
            total = jnp.sum(e, axis=1, keepdims=True)
            weight = jnp.zeros_like(total)
            if own:
                total = total + jnp.exp(p - m)
                weight = jnp.transpose(jnp.broadcast_to(weights[:, b * EB:(b + 1) * EB], (128, EB)))[:, 0:1]
            scores[rows, :] = e
            stat_own[rows, :] = jnp.where(lane == 0, m, jnp.where(lane == 1, total, weight))
    stat_copy = remote(stat_own, stat_oth, 1)
    stat_copy.start()
    stat_copy.wait()

    qg_copies = []
    for b in range(SPANS):
        for own in range(2):
            rows = pl.ds(b * 2 * EB + (1 - own) * EB, EB)
            theirs = pl.ds(b * 2 * EB + own * EB, EB)
            a, o = stat_own[rows, :], stat_oth[theirs, :]
            m1, l1, m2, l2 = a[:, 0:1], a[:, 1:2], o[:, 0:1], o[:, 1:2]
            w = a[:, 2:3] if own else o[:, 2:3]
            peak = jnp.maximum(m1, m2)
            f1 = jnp.exp(m1 - peak)
            total = l1 * f1 + l2 * jnp.exp(m2 - peak)
            scale = w / total
            if own:
                mown[pl.ds(b * EB, EB), :] = w * (jnp.exp(pos[pl.ds(b * EB, EB), :] - peak) / total - 1.0)
            gn = scores[rows, :] * (f1 * scale)
            scores[rows, :] = gn
            hi, lo = split2(gn)
            negs = pl.ds(b * NEGS, NEGS)
            part = dot_nt(hi, nparts[1, :, negs]) + dot_nt(lo, nparts[0, :, negs]) + dot_nt(hi, nparts[0, :, negs])
            if own:
                qg_own[pl.ds(b * EB, EB), :] = part
            else:
                qg_out[pl.ds(b * EB, EB), :] = part
                copy = remote(qg_out.at[pl.ds(b * EB, EB)], qg_in.at[pl.ds(b * EB, EB)], 2 + b)
                copy.start()
                qg_copies.append(copy)

    def put(rows, value):
        for k in range(CHUNKS):
            for g in range(2):
                lanes = pl.ds((2 * k + g) * 128, 128)
                hi, lo = split2(value[:, g * HALF + 128 * k:g * HALF + 128 * (k + 1)])
                ghi[rows, lanes] = hi
                glo[rows, lanes] = lo
        for g in range(2):
            rest = value[:, g * HALF + 128 * CHUNKS:(g + 1) * HALF]
            for shift in (REM, 2 * REM, 4 * REM):
                rest = rest + pltpu.roll(rest, shift, 1)
            hi, lo = split2(rest * zmask[rows, :])
            lanes = pl.ds(GW + g * 128, 128)
            ghi[rows, lanes] = hi
            glo[rows, lanes] = lo

    for b in range(SPANS):
        gnt = jnp.transpose(scores[pl.ds(b * 2 * EB, 2 * EB), :])
        for j, part in enumerate(split2(gnt)):
            gnb[j] = part

        @pl.loop(0, NEGS // 128)
        def _(i):
            hi, lo = gnb[0, rows_of(i, 128), :], gnb[1, rows_of(i, 128), :]
            edges = pl.ds(b * 2 * EB, 2 * EB)
            value = dot_nn(hi, qparts[1, edges, :]) + dot_nn(lo, qparts[0, edges, :]) + dot_nn(hi, qparts[0, edges, :])
            put(pl.ds(pl.multiple_of(TOUCHED + b * NEGS + i * 128, 128), 128), value)

    for copy in qg_copies:
        copy.wait()

    @pl.loop(0, EDGES // 128)
    def _(i):
        rows = rows_of(i, 128)
        gp = mown[rows, :]
        g = gp * tbuf[rows, :] + (qg_own[rows, :] + qg_in[rows, :])
        h, r = hbuf[rows, :], rbuf[rows, :]
        gre, gim = g[:, :HALF], g[:, HALF:]
        for n, other in ((0, r), (2, h)):
            ore, oim = other[:, :HALF], other[:, HALF:]
            for half, value in enumerate((gre * ore + gim * oim, gim * ore - gre * oim)):
                hi, lo = split2(value)
                terms[2 * n, rows, half * HALF:(half + 1) * HALF] = hi
                terms[2 * n + 1, rows, half * HALF:(half + 1) * HALF] = lo
        hi, lo = split2(gp * qown[rows, :])
        terms[2, rows, :] = hi
        terms[3, rows, :] = lo

    row128 = lax.broadcasted_iota(jnp.int32, (128, EDGES), 0)

    def spread(idx, n):
        onehot = jnp.where(idx[...] == row128, 1.0, 0.0).astype(BF)
        return dot_nn(onehot, terms[2 * n + 1]) + dot_nn(onehot, terms[2 * n])

    put(pl.ds(0, 128), spread(hr, 0) + spread(tr, 1))
    put(pl.ds(SLAB, 128), spread(rr, 2))


def route_kernel(ghi, glo, slots, ids_send, ent_out, rel_out,
                 ids_recv, perm, sbuf, srem, abuf, arem, rbuf, rrem, xrem,
                 tables, plus, minus,
                 ids_ss, ids_rs, a_ss, a_rs, b_ss, b_rs, own_sem, p_ss, p_rs, m_ss, m_rs):
    ent, grp = lax.axis_index("ent"), lax.axis_index("grp")
    z, c = ent // CLASSES, ent % CLASSES
    x, y = c // NY, c % NY
    first, second = jnp.where(grp == 0, x, y), jnp.where(grp == 0, y, x)

    def chip(dx, dy, dz=0):
        return ((z + dz) % NZ) * CLASSES + ((x + dx) % NX) * NY + (y + dy) % NY

    def plane_peer(j, f):
        return (chip(j // NY, j % NY), (grp + f) % 2)

    def chip_z(dz):
        return (chip(0, 0, dz), grp)

    barrier = pltpu.get_barrier_semaphore()

    @pl.loop(0, CLASSES)
    def _(j):
        @pl.when(j > 0)
        def _():
            pl.semaphore_signal(barrier, inc=1, device_id=plane_peer(j, 0), device_id_type=MESH)
        pl.semaphore_signal(barrier, inc=1, device_id=plane_peer(j, 1), device_id_type=MESH)

    pl.semaphore_signal(barrier, inc=1, device_id=chip_z(1), device_id_type=MESH)
    pl.semaphore_signal(barrier, inc=1, device_id=chip_z(NZ - 1), device_id_type=MESH)

    slot = slots[0:1, :]

    with jax.named_scope("entry"):
        pl.semaphore_wait(barrier, PEERS - 1 + 2)

    def ids_copy(j, f):
        dx, dy = j // NY, j % NY
        cls = ((x + dx) % NX) * NY + (y + dy) % NY
        there = jnp.where((grp + f) % 2 == 0, dy * NX + dx, dx * NY + dy) * 2 + f
        return pltpu.make_async_remote_copy(
            ids_send.at[pl.ds(pl.multiple_of(cls * NZ, NZ), NZ)], ids_recv.at[there],
            ids_ss.at[j * 2 + f], ids_rs.at[there], device_id=plane_peer(j, f), device_id_type=MESH)

    def for_peers(act):
        @pl.loop(0, CLASSES)
        def _(j):
            @pl.when(j > 0)
            def _():
                act(j, 0)
            act(j, 1)

    for_peers(lambda j, f: ids_copy(j, f).start())
    ids_recv[0] = ids_send[pl.ds(pl.multiple_of(c * NZ, NZ), NZ), :]

    def bufs(k):
        if k < CHUNKS:
            return sbuf.at[k], abuf.at[k], rbuf.at[k]
        return srem, arem, rrem

    def leg1(k, g, d):
        s, a, _ = bufs(k)
        f = (grp + g) % 2
        there = (chip(d, 0) if g == 0 else chip(0, d), g)
        return pltpu.make_async_remote_copy(
            s.at[g, ((x if g == 0 else y) + d) % 4], a.at[d, f],
            a_ss.at[k, g, d], a_rs.at[k, d, f], device_id=there, device_id_type=MESH)

    def leg1_pair(k):
        s, a, _ = bufs(k)
        return pltpu.make_async_remote_copy(
            s.at[1 - grp, second], a.at[0, 1],
            a_ss.at[k, 0, 0], a_rs.at[k, 0, 1], device_id=(ent, 1 - grp), device_id_type=MESH)

    def leg1_own(k):
        s, a, _ = bufs(k)
        return pltpu.make_async_copy(s.at[grp, first], a.at[0, 0], own_sem.at[k, 0])

    def leg2(k, d, e):
        _, a, r = bufs(k)
        there = jnp.where(grp == 0, chip(0, e), chip(e, 0))
        return pltpu.make_async_remote_copy(
            a.at[d, :, (second + e) % 4], r.at[e, d],
            b_ss.at[k, e, d], b_rs.at[k, e, d], device_id=(there, grp), device_id_type=MESH)

    def leg2_own(k, d):
        _, a, r = bufs(k)
        return pltpu.make_async_copy(a.at[d, :, second], r.at[0, d], own_sem.at[k, 1 + d])

    def send(k):
        with jax.named_scope("send%d" % k):
            leg1_own(k).start()
            leg1_pair(k).start()
            for d in (1, 3, 2):
                for g in range(2):
                    leg1(k, g, d).start()

    def forward(k):
        with jax.named_scope("forward%d" % k):
            for d in (0, 1, 3, 2):
                if d == 0:
                    leg1_own(k).wait()
                    leg1_pair(k).wait_recv()
                else:
                    for f in range(2):
                        _, a, _ = bufs(k)
                        pltpu.make_async_remote_copy(
                            a.at[d, f], a.at[d, f], a_ss.at[k, 0, d], a_rs.at[k, d, f],
                            device_id=(ent, 1 - grp), device_id_type=MESH).wait_recv()
                for e in (1, 3, 2):
                    leg2(k, d, e).start()
                leg2_own(k, d).start()

    def arrive(k):
        with jax.named_scope("arrive%d" % k):
            for d in range(4):
                leg2_own(k, d).wait()
                for e in (1, 3, 2):
                    leg2(k, d, e).wait_recv()

    slot_row = lax.broadcasted_iota(jnp.int32, (CSLOTS, ROWS), 0)

    def fill(k):
        with jax.named_scope("fill%d" % k):
            @pl.loop(0, CLASSES)
            def _(cls):
                rows = pl.ds(pl.multiple_of(cls * CSLOTS, CSLOTS), CSLOTS)
                cx, cy = cls // NY, cls % NY
                if k == 0:
                    perm[rows, 0:ROWS] = jnp.where(slot_row == slot - cls * CSLOTS, 1.0, 0.0).astype(BF)
                hot = perm[rows, 0:ROWS]
                lanes = pl.ds(k * 256, 256)
                value = dot_nn(hot, glo[:, lanes]) + dot_nn(hot, ghi[:, lanes])
                sbuf[k, 0, cx, cy] = value[:, :128]
                sbuf[k, 1, cy, cx] = value[:, 128:]

    def fill_rem():
        with jax.named_scope("fill_rem"):
            row = lax.broadcasted_iota(jnp.int32, (CLASSES * RSLOTS, ROWS), 0)
            hot = jnp.where(row == slots[1:2, :], 1.0, 0.0).astype(BF)
            lanes = pl.ds(GW, 256)
            value = dot_nn(hot, glo[:, lanes]) + dot_nn(hot, ghi[:, lanes])
            for cls in range(CLASSES):
                part = value[cls * RSLOTS:(cls + 1) * RSLOTS, :]
                srem[0, cls // NY, cls % NY] = part[:, :128]
                srem[1, cls % NY, cls // NY] = part[:, 128:]

    def ring_rows(k):
        return TABLE_REM if k == WITH_REM else TABLE

    def ring_part(k, s, sign, h):
        n = ring_rows(k) // 2
        if s == 0:
            return pl.ds(h * n + (0 if sign > 0 else n // 2), n // 2)
        return pl.ds(h * n, n)

    def ring_copy(k, s, sign, h):
        o = (z + sign * (4 - s) + NZ) % NZ
        ss, rs = (p_ss, p_rs) if sign > 0 else (m_ss, m_rs)
        part = ring_part(k, s, sign, h)
        return pltpu.make_async_remote_copy(
            tables.at[k, o, part], (plus if sign > 0 else minus).at[k, s, part],
            ss.at[k, s, h], rs.at[k, s, h], device_id=chip_z(sign % NZ), device_id_type=MESH)

    def ring_start(k):
        for h in range(2):
            for sign in (1, -1):
                ring_copy(k, 0, sign, h).start()

    def ring_next(k, s):
        with jax.named_scope("ring%d_%d" % (k, s)):
            for h in range(2):
                for sign in (1, -1):
                    ring_copy(k, s, sign, h).wait_recv()
                    if s == 3:
                        continue
                    o = (z + sign * (3 - s) + NZ) % NZ
                    part = ring_part(k, s, sign, h)
                    tables[k, o, part, :] = tables[k, o, part, :] + (plus if sign > 0 else minus)[k, s, part, :]
                    ring_copy(k, s + 1, sign, h).start()
            if s < 3:
                return
            total = tables[k, z, 0:ring_rows(k), :] + (plus[k, 3, 0:ring_rows(k), :] + minus[k, 3, 0:ring_rows(k), :])
            turned = jnp.transpose(total[0:TABLE, :])
            rows = pl.ds(k * 128, 128)
            ent_out[rows, :] = turned[:, 0:ROWS_DEV]
            rel_out[rows, :] = turned[:, ROWS_DEV:ROWS_DEV + REL_DEV]
            if k == WITH_REM:
                rows = pl.ds(CHUNKS * 128, REM)
                for i in range(TABLE // 128):
                    part = total[TABLE + i * REM:TABLE + (i + 1) * REM, :]
                    if i < ROWS_DEV // 128:
                        ent_out[rows, i * 128:(i + 1) * 128] = part
                    else:
                        rel_out[rows, :] = part[:, 0:REL_DEV]

    def place(o):
        return perm[pl.ds((o // 2) * TABLE, TABLE), (o % 2) * 768:(o % 2) * 768 + DEPTH]

    def build_place():
        with jax.named_scope("place"):
            @pl.loop(1, PEERS)
            def _(n):
                pltpu.make_async_remote_copy(
                    ids_recv.at[n], ids_recv.at[n], ids_ss.at[n], ids_rs.at[n],
                    device_id=(ent, 1 - grp), device_id_type=MESH).wait_recv()
            got = jnp.concatenate([ids_recv[n][:, 0:SLOTS] for n in range(PEERS)], axis=1)
            row = lax.broadcasted_iota(jnp.int32, (TABLE, DEPTH), 0)
            for o in range(NZ):
                perm[pl.ds((o // 2) * TABLE, TABLE), (o % 2) * 768:(o % 2) * 768 + DEPTH] = jnp.where(
                    row == got[o:o + 1, :], 1.0, 0.0).astype(BF)

    def add_up(k):
        with jax.named_scope("add%d" % k):
            flat = rbuf.at[k].reshape(PEERS * CSLOTS, 128)
            for o in range(NZ):
                hi, lo = split2(flat[pl.ds(o, DEPTH, stride=NZ), :])
                value = dot_nn(place(o), jnp.concatenate([hi, lo], axis=1))
                tables[k, o, 0:TABLE, :] = value[:, :128] + value[:, 128:]
            ring_start(k)

    def add_up_rem():
        with jax.named_scope("add_rem"):
            for e in range(4):
                for d in range(4):
                    for f in range(2):
                        n = (e * 4 + d) * 2 + f
                        xrem[pl.ds(n * SLOTS, SLOTS), :] = rrem[e, d, f][0:SLOTS, :]
            group = lax.broadcasted_iota(jnp.int32, (DEPTH, 128), 1) // REM
            total = jnp.zeros((TABLE, 256), F32)
            for o in range(NZ):
                hi, lo = split2(jnp.where(group == o, xrem[...], 0.0))
                total = total + dot_nn(place(o), jnp.concatenate([hi, lo], axis=1))
            total = jnp.transpose(total[:, :128] + total[:, 128:])
            for o in range(NZ):
                for i in range(TABLE // 128):
                    tables[WITH_REM, o, TABLE + i * REM:TABLE + (i + 1) * REM, :] = total[o * REM:(o + 1) * REM, i * 128:(i + 1) * 128]
                tables[WITH_REM, o, TABLE + 5 * REM:TABLE_REM, :] = jnp.zeros((TABLE_REM - TABLE - 5 * REM, 128), F32)

    rem = CHUNKS
    fill(0)
    send(0)
    fill_rem()
    send(rem)
    fill(1)
    forward(0)
    send(1)
    forward(rem)
    fill(2)
    build_place()
    arrive(0)
    add_up(0)
    arrive(rem)
    add_up_rem()
    ring_next(0, 0)
    forward(1)
    send(2)
    ring_next(0, 1)
    ring_next(0, 2)
    arrive(1)
    add_up(1)
    ring_next(0, 3)
    ring_next(1, 0)
    forward(2)
    ring_next(1, 1)
    ring_next(1, 2)
    arrive(2)
    add_up(2)
    ring_next(1, 3)
    for s in range(4):
        ring_next(2, s)

    with jax.named_scope("drain"):
        for_peers(lambda j, f: ids_copy(j, f).wait_send())
        for k in range(CHUNKS + 1):
            leg1_pair(k).wait_send()
            for d in (1, 2, 3):
                for g in range(2):
                    leg1(k, g, d).wait_send()
            for d in range(4):
                for e in (1, 2, 3):
                    leg2(k, d, e).wait_send()
        for k in range(CHUNKS):
            for s in range(4):
                for h in range(2):
                    ring_copy(k, s, 1, h).wait_send()
                    ring_copy(k, s, -1, h).wait_send()


def vmem():
    return pl.BlockSpec(memory_space=pltpu.VMEM)


def local_call(*args):
    dma = pltpu.SemaphoreType.DMA
    return pl.pallas_call(
        local_kernel,
        out_shape=(jax.ShapeDtypeStruct((ROWS, GW + 256), BF), jax.ShapeDtypeStruct((ROWS, GW + 256), BF),
                   jax.ShapeDtypeStruct((2, ROWS), jnp.int32), jax.ShapeDtypeStruct((128, 128), jnp.int32)),
        in_specs=[vmem()] * len(args),
        out_specs=(vmem(),) * 4,
        scratch_shapes=[
            pltpu.VMEM((2, ROWS), jnp.int32),
            pltpu.VMEM((1, ROWS), F32),
            pltpu.VMEM((ROWS, 128), F32),
            pltpu.VMEM((2, 3, W, 128), BF),
            pltpu.VMEM((3, W, 2 * NEGS), BF),
            pltpu.VMEM((EDGES, W), F32),
            pltpu.VMEM((EDGES, W), F32),
            pltpu.VMEM((EDGES, W), F32),
            pltpu.VMEM((EDGES, 1), F32),
            pltpu.VMEM((EDGES, W), F32),
            pltpu.VMEM((EDGES, W), F32),
            pltpu.VMEM((3, 2 * EDGES, W), BF),
            pltpu.VMEM((2 * EDGES, NEGS), F32),
            pltpu.VMEM((2 * EDGES, 128), F32),
            pltpu.VMEM((2 * EDGES, 128), F32),
            pltpu.VMEM((EDGES, 1), F32),
            pltpu.VMEM((2, NEGS, 2 * EB), BF),
            pltpu.VMEM((EDGES, W), F32),
            pltpu.VMEM((EDGES, W), F32),
            pltpu.VMEM((EDGES, W), F32),
            pltpu.VMEM((6, EDGES, W), BF),
            dma((4,)), dma((4,)),
        ],
        compiler_params=pltpu.CompilerParams(collective_id=0, has_side_effects=True, vmem_limit_bytes=60 * MiB),
        name="local",
    )(*args)


def route_call(*args):
    dma = pltpu.SemaphoreType.DMA
    return pl.pallas_call(
        route_kernel,
        out_shape=(jax.ShapeDtypeStruct((K, ROWS_DEV), F32), jax.ShapeDtypeStruct((K, REL_DEV), F32)),
        in_specs=[vmem()] * len(args),
        out_specs=(vmem(), vmem()),
        scratch_shapes=[
            pltpu.VMEM((PEERS, NZ, 128), jnp.int32),
            pltpu.VMEM((CLASSES * CSLOTS, 1536), BF),
            pltpu.VMEM((CHUNKS, 2, 4, 4, CSLOTS, 128), F32),
            pltpu.VMEM((2, 4, 4, RSLOTS, 128), F32),
            pltpu.VMEM((CHUNKS, 4, 2, 4, CSLOTS, 128), F32),
            pltpu.VMEM((4, 2, 4, RSLOTS, 128), F32),
            pltpu.VMEM((CHUNKS, 4, 4, 2, CSLOTS, 128), F32),
            pltpu.VMEM((4, 4, 2, RSLOTS, 128), F32),
            pltpu.VMEM((DEPTH, 128), F32),
            pltpu.VMEM((CHUNKS, NZ, TABLE_REM, 128), F32),
            pltpu.VMEM((CHUNKS, 4, TABLE_REM, 128), F32),
            pltpu.VMEM((CHUNKS, 4, TABLE_REM, 128), F32),
            dma((PEERS,)), dma((PEERS,)),
            dma((CHUNKS + 1, 2, 4)), dma((CHUNKS + 1, 4, 2)), dma((CHUNKS + 1, 4, 4)), dma((CHUNKS + 1, 4, 4)),
            dma((CHUNKS + 1, 5)),
            dma((CHUNKS, 4, 2)), dma((CHUNKS, 4, 2)), dma((CHUNKS, 4, 2)), dma((CHUNKS, 4, 2)),
        ],
        compiler_params=pltpu.CompilerParams(collective_id=1, has_side_effects=True, vmem_limit_bytes=63 * MiB),
        name="route",
    )(*args)


def body(slab, slab_owner, slab_row, rel_slab, rel_owner, rel_row, heads, tails, rels, weights):
    rows = [v.reshape(1, EDGES) for v in (heads, tails, rels, weights)]
    places = [v.reshape(1, v.size) for v in (slab_owner, slab_row, rel_owner, rel_row)]
    ent_grad, rel_grad = route_call(*local_call(slab.T, rel_slab.T, *rows, *places))
    return ent_grad.T, rel_grad.T


def solution(mesh):
    split = P(("ent", "grp"))
    wide = P(("ent", "grp"), None)
    in_specs = (wide, wide, split, wide, wide, split, split, split, split, split)
    out_specs = (P("ent", "grp"), P("ent", "grp"))
    return jax.shard_map(body, mesh=mesh, in_specs=in_specs, out_specs=out_specs, check_vma=False)
```

```python
import jax
import jax.numpy as jnp
from jax import lax
from jax.experimental import pallas as pl
from jax.experimental.pallas import tpu as pltpu
from jax.sharding import PartitionSpec as P

K = 400
HALF = 512
W = 2 * HALF
EB = 256
SPANS = 2
EDGES = EB * SPANS
TOUCHED = 128
NEGS = 512
SLAB = 1152
RSLAB = 128
ROWS = SLAB + RSLAB
ROWS_DEV = 512
REL_DEV = 116
NZ, NX, NY = 8, 4, 4
CLASSES = NX * NY
CAP, RCAP = 18, 4
SLOTS = CAP + RCAP
CSLOTS = SLOTS * NZ
PEERS = 2 * CLASSES
DEPTH = PEERS * SLOTS
TABLE = 640
RSLOTS = 24
WITH_REM = 1
TABLE_REM = 736
CHUNKS = 3
REM = K - 128 * CHUNKS
GW = 2 * 128 * (CHUNKS - 1)
MiB = 2**20

F32 = jnp.float32
BF = jnp.bfloat16
MESH = pl.DeviceIdType.MESH


def split2(x):
    hi = x.astype(BF)
    return hi, (x - hi.astype(F32)).astype(BF)


def split3(x):
    hi = x.astype(BF)
    rest = x - hi.astype(F32)
    mid = rest.astype(BF)
    return hi, mid, (rest - mid.astype(F32)).astype(BF)


def dot_nn(a, b):
    return lax.dot_general(a, b, (((1,), (0,)), ((), ())), preferred_element_type=F32)


def dot_nt(a, b):
    return lax.dot_general(a, b, (((1,), (1,)), ((), ())), preferred_element_type=F32)


def rows_of(i, n):
    return pl.ds(pl.multiple_of(i * n, n), n)


def tile(k, g):
    return slice(256 * k + 128 * g, 256 * k + 128 * (g + 1))


def local_kernel(slab, rel, hr, tr, rr, weights, slab_owner, slab_row, rel_owner, rel_row, ghi, glo, slots, ids, landed,
                 ints, kpos, zmask, tabs, nparts, hbuf, rbuf, tbuf, pos, qown, qoth, qparts, scores, stat_own, stat_oth,
                 mown, gnp, gnb, qg_out, terms, first_g, sbuf, sends, recvs, l_ss, l_rs, own_sem):
    ent, grp = lax.axis_index("ent"), lax.axis_index("grp")
    peer = (ent, 1 - grp)
    z, c = ent // CLASSES, ent % CLASSES
    x, y = c // NY, c % NY

    def chip(dx, dy):
        return z * CLASSES + ((x + dx) % NX) * NY + (y + dy) % NY

    barrier = pltpu.get_barrier_semaphore()
    pl.semaphore_signal(barrier, inc=1, device_id=peer, device_id_type=MESH)
    for d in (1, 2, 3):
        sender = jnp.where(grp == 0, chip(-d + NX, 0), chip(0, -d + NY))
        for core in range(2):
            pl.semaphore_signal(barrier, inc=1, device_id=(sender, core), device_id_type=MESH)

    def remote(src, dst, i):
        return pltpu.make_async_remote_copy(src, dst, sends.at[i], recvs.at[i], device_id=peer, device_id_type=MESH)

    def store_parts(ref, lanes, source, split):
        for g in range(2):
            for k in range(CHUNKS + 1):
                size = 128 if k < CHUNKS else REM
                start, first = g * K + 128 * k, 256 * k + 128 * g
                for j, part in enumerate(split(source[start:start + size, :])):
                    ref[j, first:first + size, lanes] = part
                    if size < 128:
                        ref[j, first + size:first + 128, lanes] = jnp.zeros((128 - size, part.shape[1]), BF)

    for i, source in enumerate((slab, rel)):
        store_parts(tabs.at[i], pl.ds(0, 128), source[:, 0:128], split3)

    sub128 = lax.broadcasted_iota(jnp.int32, (128, 128), 0)
    sub256 = lax.broadcasted_iota(jnp.int32, (128, EB), 0)

    def gathered(idx, i, rows):
        onehot = jnp.transpose(jnp.where(idx[:, rows] == sub256, 1.0, 0.0)).astype(BF)
        return dot_nt(onehot, tabs[i, 0]) + dot_nt(onehot, tabs[i, 1]) + dot_nt(onehot, tabs[i, 2])

    @pl.loop(0, SPANS)
    def _(i):
        rows = rows_of(i, EB)
        h = gathered(hr, 0, rows)
        r = gathered(rr, 1, rows)
        hbuf[rows, :] = h
        rbuf[rows, :] = r
        for k in range(CHUNKS + 1):
            hre, him, rre, rim = h[:, tile(k, 0)], h[:, tile(k, 1)], r[:, tile(k, 0)], r[:, tile(k, 1)]
            qown[rows, tile(k, 0)] = hre * rre - him * rim
            qown[rows, tile(k, 1)] = hre * rim + him * rre

    pl.semaphore_wait(barrier, 7)
    q_copy = remote(qown, qoth, 0)
    q_copy.start()

    @pl.loop(0, 2 * NEGS // 128)
    def _(i):
        x = slab[:, pl.ds(pl.multiple_of(TOUCHED + i * 128, 128), 128)]
        store_parts(nparts, rows_of(i, 128), x, split2)

    for n, (first, second) in enumerate(((slab_owner, rel_owner), (slab_row, rel_row))):
        ints[n:n + 1, 0:SLAB] = first[...]
        ints[n:n + 1, SLAB:ROWS] = second[...] + n * ROWS_DEV
    own = ints[0:1, :]
    oclass, oz = own % CLASSES, own // CLASSES
    owner_row = lax.broadcasted_iota(jnp.int32, (128, ROWS), 0)
    onehot = jnp.where(owner_row == oclass * NZ + oz, 1.0, 0.0)
    for start, size, offset in ((0, SLAB, 0), (SLAB, RSLAB, CAP)):
        part = onehot[:, start:start + size]
        upper = lax.broadcasted_iota(jnp.int32, (size, size), 0) <= lax.broadcasted_iota(jnp.int32, (size, size), 1)
        count = dot_nn(part.astype(BF), jnp.where(upper, 1.0, 0.0).astype(BF))
        kpos[:, start:start + size] = jnp.sum(part * count, axis=0, keepdims=True) + (offset - 1.0)
    kth = kpos[...].astype(jnp.int32)
    slots[0:1, :] = oclass * CSLOTS + kth * NZ + oz
    slots[1:2, :] = oclass * RSLOTS + kth
    for i in range(ROWS // 128):
        zmask[pl.ds(i * 128, 128), :] = jnp.transpose(jnp.where(oz[:, i * 128:(i + 1) * 128] == sub128 // REM, 1.0, 0.0))
    kth_hot = jnp.where(owner_row == kth, 1.0, 0.0).astype(BF)
    number = ints[1:2, :] + 1
    high = ((number // 16) * 16).astype(F32)
    low = (number % 16).astype(F32)
    ids[...] = (dot_nt((onehot * high).astype(BF), kth_hot) + dot_nt((onehot * low).astype(BF), kth_hot)).astype(jnp.int32) - 1

    @pl.loop(0, SPANS)
    def _(i):
        rows = rows_of(i, EB)
        t = gathered(tr, 0, rows)
        tbuf[rows, :] = t
        q = qown[rows, :]
        pos[rows, :] = jnp.sum(q * t, axis=1, keepdims=True)
        place = pl.ds(pl.multiple_of(i * (2 * EB), EB), EB)
        for j, part in enumerate(split2(q)):
            qparts[j, place, :] = part

    def score(b, first):
        rows = pl.ds(b * 2 * EB + first, EB)
        negs = pl.ds(b * NEGS, NEGS)
        q, n = [qparts[j, rows, :] for j in range(2)], [nparts[j, :, negs] for j in range(2)]
        scores[rows, :] = (dot_nn(q[0], n[1]) + dot_nn(q[1], n[0])) + dot_nn(q[0], n[0])

    for b in range(SPANS):
        score(b, 0)
    q_copy.wait()

    @pl.loop(0, EDGES // 128)
    def _(i):
        place = pl.ds(pl.multiple_of((i // 2) * (2 * EB) + EB + (i % 2) * 128, 128), 128)
        for j, part in enumerate(split2(qoth[rows_of(i, 128), :])):
            qparts[j, place, :] = part

    for b in range(SPANS):
        score(b, EB)

    lane = lax.broadcasted_iota(jnp.int32, (EB, 128), 1)
    for b in range(SPANS):
        for own in range(2):
            rows = pl.ds(b * 2 * EB + (1 - own) * EB, EB)
            s = scores[rows, :]
            m = jnp.max(s, axis=1, keepdims=True)
            if own:
                p = pos[pl.ds(b * EB, EB), :]
                m = jnp.maximum(m, p)
            e = jnp.exp(s - m)
            total = jnp.sum(e, axis=1, keepdims=True)
            weight = jnp.zeros_like(total)
            if own:
                total = total + jnp.exp(p - m)
                weight = jnp.transpose(jnp.broadcast_to(weights[:, b * EB:(b + 1) * EB], (128, EB)))[:, 0:1]
            scores[rows, :] = e
            stat_own[rows, :] = jnp.where(lane == 0, m, jnp.where(lane == 1, total, weight))
    stat_copy = remote(stat_own, stat_oth, 1)
    stat_copy.start()
    stat_copy.wait()

    for b in range(SPANS):
        for own in range(2):
            rows = pl.ds(b * 2 * EB + (1 - own) * EB, EB)
            theirs = pl.ds(b * 2 * EB + own * EB, EB)
            a, o = stat_own[rows, :], stat_oth[theirs, :]
            m1, l1, m2, l2 = a[:, 0:1], a[:, 1:2], o[:, 0:1], o[:, 1:2]
            w = a[:, 2:3] if own else o[:, 2:3]
            peak = jnp.maximum(m1, m2)
            f1 = jnp.exp(m1 - peak)
            total = l1 * f1 + l2 * jnp.exp(m2 - peak)
            if own:
                mown[pl.ds(b * EB, EB), :] = w * (jnp.exp(pos[pl.ds(b * EB, EB), :] - peak) / total - 1.0)
            gn = scores[rows, :] * (f1 * (w / total))
            scores[rows, :] = gn
            for j, part in enumerate(split2(gn)):
                gnp[j, rows, :] = part
        gnt = jnp.transpose(scores[pl.ds(b * 2 * EB, 2 * EB), :])
        for j, part in enumerate(split2(gnt)):
            gnb[b, j] = part

    def put(rows, value, chunks):
        for n, k in enumerate(chunks):
            for g in range(2):
                part = value[:, tile(n, g)]
                if k == CHUNKS:
                    for shift in (REM, 2 * REM, 4 * REM):
                        part = part + pltpu.roll(part, shift, 1)
                    part = part * zmask[rows, :]
                hi, lo = split2(part)
                if k == 0:
                    first_g[0, rows, tile(0, g)] = hi
                    first_g[1, rows, tile(0, g)] = lo
                else:
                    ghi[rows, tile(k - 1, g)] = hi
                    glo[rows, tile(k - 1, g)] = lo

    row128 = lax.broadcasted_iota(jnp.int32, (128, EDGES), 0)
    qg_in = qoth

    def gradients(group, chunks):
        start, size = 256 * chunks[0], 256 * len(chunks)
        lanes = pl.ds(start, size)

        def query_part(b, own):
            rows, negs = pl.ds(b * 2 * EB + (1 - own) * EB, EB), pl.ds(b * NEGS, NEGS)
            hi, lo = gnp[0, rows, :], gnp[1, rows, :]
            n0, n1 = nparts[0, lanes, negs], nparts[1, lanes, negs]
            return dot_nt(hi, n1) + dot_nt(lo, n0) + dot_nt(hi, n0)

        copies = []
        for b in range(SPANS):
            rows = pl.ds(b * EB, EB)
            qg_out[rows, lanes] = query_part(b, 0)
            copies.append(remote(qg_out.at[rows, lanes], qg_in.at[rows, lanes], 2 + 2 * group + b))
            copies[-1].start()
        for b in range(SPANS):
            rows = pl.ds(b * EB, EB)
            tbuf[rows, lanes] = mown[rows, :] * tbuf[rows, lanes] + query_part(b, 1)
        for b in range(SPANS):
            edges = pl.ds(b * 2 * EB, 2 * EB)

            @pl.loop(0, NEGS // 256)
            def _(i):
                hi, lo = gnb[b, 0, rows_of(i, 256), :], gnb[b, 1, rows_of(i, 256), :]
                q0, q1 = qparts[0, edges, lanes], qparts[1, edges, lanes]
                value = dot_nn(hi, q1) + dot_nn(lo, q0) + dot_nn(hi, q0)
                put(pl.ds(pl.multiple_of(TOUCHED + b * NEGS + i * 256, 128), 256), value, chunks)
        for copy in copies:
            copy.wait()

        def spread(idx, other):
            @pl.loop(0, EDGES // 128)
            def _(i):
                rows = rows_of(i, 128)
                for n, k in enumerate(chunks):
                    if other is None:
                        values = [mown[rows, :] * qown[rows, tile(k, g)] for g in range(2)]
                    else:
                        gre, gim = (tbuf[rows, tile(k, g)] + qg_in[rows, tile(k, g)] for g in range(2))
                        ore, oim = other[rows, tile(k, 0)], other[rows, tile(k, 1)]
                        values = [gre * ore + gim * oim, gim * ore - gre * oim]
                    for g in range(2):
                        hi, lo = split2(values[g])
                        terms[0, rows, tile(n, g)] = hi
                        terms[1, rows, tile(n, g)] = lo
            onehot = jnp.where(idx[...] == row128, 1.0, 0.0).astype(BF)
            return dot_nn(onehot, terms[1, :, 0:size]) + dot_nn(onehot, terms[0, :, 0:size])

        head = spread(hr, rbuf)
        put(pl.ds(0, 128), head + spread(tr, None), chunks)
        put(pl.ds(SLAB, 128), spread(rr, hbuf), chunks)

    gradients(0, (0,))

    slot_row = lax.broadcasted_iota(jnp.int32, (4 * CSLOTS, ROWS), 0)

    def leg1(g, d):
        f = (grp + g) % 2
        there = (chip(d, 0) if g == 0 else chip(0, d), g)
        return pltpu.make_async_remote_copy(
            sbuf.at[g, ((x if g == 0 else y) + d) % 4], landed.at[d, f],
            l_ss.at[g, d], l_rs.at[d, f], device_id=there, device_id_type=MESH)

    pair = pltpu.make_async_remote_copy(
        sbuf.at[1 - grp, jnp.where(grp == 0, y, x)], landed.at[0, 1], l_ss.at[0, 0], l_rs.at[0, 1],
        device_id=peer, device_id_type=MESH)
    own_copy = pltpu.make_async_copy(sbuf.at[grp, jnp.where(grp == 0, x, y)], landed.at[0, 0], own_sem)
    for d in (1, 3, 2, 0):
        cx = (x + d) % 4
        hot = jnp.where(slot_row == slots[0:1, :] - cx * (4 * CSLOTS), 1.0, 0.0).astype(BF)
        value = dot_nn(hot, first_g[1]) + dot_nn(hot, first_g[0])
        for cy in range(4):
            sbuf[0, cx, cy] = value[cy * CSLOTS:(cy + 1) * CSLOTS, :128]
            sbuf[1, cy, cx] = value[cy * CSLOTS:(cy + 1) * CSLOTS, 128:]
        if d:
            leg1(0, d).start()
    for d in (1, 3, 2):
        leg1(1, d).start()
    pair.start()
    own_copy.start()

    gradients(1, tuple(range(1, CHUNKS + 1)))

    own_copy.wait()
    pair.wait()
    for d in (1, 2, 3):
        for g in range(2):
            leg1(g, d).wait_send()
            pltpu.make_async_remote_copy(
                sbuf.at[0, 0], landed.at[d, g], l_ss.at[0, d], l_rs.at[d, g], device_id=peer, device_id_type=MESH).wait_recv()


def route_kernel(ghi, glo, slots, ids_send, landed, ent_out, rel_out,
                 ids_recv, perm, sbuf, srem, abuf, arem, rbuf, rrem, xrem,
                 tables, plus, minus,
                 ids_ss, ids_rs, a_ss, a_rs, b_ss, b_rs, own_sem, p_ss, p_rs, m_ss, m_rs):
    ent, grp = lax.axis_index("ent"), lax.axis_index("grp")
    z, c = ent // CLASSES, ent % CLASSES
    x, y = c // NY, c % NY
    first, second = jnp.where(grp == 0, x, y), jnp.where(grp == 0, y, x)

    def chip(dx, dy, dz=0):
        return ((z + dz) % NZ) * CLASSES + ((x + dx) % NX) * NY + (y + dy) % NY

    def plane_peer(j, f):
        return (chip(j // NY, j % NY), (grp + f) % 2)

    def chip_z(dz):
        return (chip(0, 0, dz), grp)

    barrier = pltpu.get_barrier_semaphore()

    @pl.loop(0, CLASSES)
    def _(j):
        @pl.when(j > 0)
        def _():
            pl.semaphore_signal(barrier, inc=1, device_id=plane_peer(j, 0), device_id_type=MESH)
        pl.semaphore_signal(barrier, inc=1, device_id=plane_peer(j, 1), device_id_type=MESH)

    pl.semaphore_signal(barrier, inc=1, device_id=chip_z(1), device_id_type=MESH)
    pl.semaphore_signal(barrier, inc=1, device_id=chip_z(NZ - 1), device_id_type=MESH)

    slot = slots[0:1, :]

    def ids_copy(j, f):
        dx, dy = j // NY, j % NY
        cls = ((x + dx) % NX) * NY + (y + dy) % NY
        there = jnp.where((grp + f) % 2 == 0, dy * NX + dx, dx * NY + dy) * 2 + f
        return pltpu.make_async_remote_copy(
            ids_send.at[pl.ds(pl.multiple_of(cls * NZ, NZ), NZ)], ids_recv.at[there],
            ids_ss.at[j * 2 + f], ids_rs.at[there], device_id=plane_peer(j, f), device_id_type=MESH)

    def for_peers(act):
        @pl.loop(0, CLASSES)
        def _(j):
            @pl.when(j > 0)
            def _():
                act(j, 0)
            act(j, 1)

    def send_ids():
        for_peers(lambda j, f: ids_copy(j, f).start())
        ids_recv[0] = ids_send[pl.ds(pl.multiple_of(c * NZ, NZ), NZ), :]

    def bufs(k):
        if k == 0:
            return None, landed, rbuf.at[0]
        if k < CHUNKS:
            return sbuf.at[k - 1], abuf.at[k - 1], rbuf.at[k]
        return srem, arem, rrem

    def leg1(k, g, d):
        s, a, _ = bufs(k)
        f = (grp + g) % 2
        there = (chip(d, 0) if g == 0 else chip(0, d), g)
        return pltpu.make_async_remote_copy(
            s.at[g, ((x if g == 0 else y) + d) % 4], a.at[d, f],
            a_ss.at[k, g, d], a_rs.at[k, d, f], device_id=there, device_id_type=MESH)

    def leg1_pair(k):
        s, a, _ = bufs(k)
        return pltpu.make_async_remote_copy(
            s.at[1 - grp, second], a.at[0, 1],
            a_ss.at[k, 0, 0], a_rs.at[k, 0, 1], device_id=(ent, 1 - grp), device_id_type=MESH)

    def leg1_own(k):
        s, a, _ = bufs(k)
        return pltpu.make_async_copy(s.at[grp, first], a.at[0, 0], own_sem.at[k, 0])

    def leg2(k, d, e):
        _, a, r = bufs(k)
        there = jnp.where(grp == 0, chip(0, e), chip(e, 0))
        return pltpu.make_async_remote_copy(
            a.at[d, :, (second + e) % 4], r.at[e, d],
            b_ss.at[k, e, d], b_rs.at[k, e, d], device_id=(there, grp), device_id_type=MESH)

    def leg2_own(k, d):
        _, a, r = bufs(k)
        return pltpu.make_async_copy(a.at[d, :, second], r.at[0, d], own_sem.at[k, 1 + d])

    def send(k):
        with jax.named_scope("send%d" % k):
            leg1_own(k).start()
            leg1_pair(k).start()
            for d in (1, 3, 2):
                for g in range(2):
                    leg1(k, g, d).start()

    def forward(k):
        with jax.named_scope("forward%d" % k):
            for d in (0, 1, 3, 2):
                if k == 0:
                    pass
                elif d == 0:
                    leg1_own(k).wait()
                    leg1_pair(k).wait_recv()
                else:
                    for f in range(2):
                        _, a, _ = bufs(k)
                        pltpu.make_async_remote_copy(
                            a.at[d, f], a.at[d, f], a_ss.at[k, 0, d], a_rs.at[k, d, f],
                            device_id=(ent, 1 - grp), device_id_type=MESH).wait_recv()
                for e in (1, 3, 2):
                    leg2(k, d, e).start()
                leg2_own(k, d).start()

    def arrive(k):
        with jax.named_scope("arrive%d" % k):
            for d in range(4):
                leg2_own(k, d).wait()
                for e in (1, 3, 2):
                    leg2(k, d, e).wait_recv()

    slot_row = lax.broadcasted_iota(jnp.int32, (4 * CSLOTS, ROWS), 0)

    def fill(k, cx):
        with jax.named_scope("fill%d" % k):
            rows = pl.ds(pl.multiple_of(cx * (4 * CSLOTS), 4 * CSLOTS), 4 * CSLOTS)
            if k == 1:
                perm[rows, 0:ROWS] = jnp.where(slot_row == slot - cx * (4 * CSLOTS), 1.0, 0.0).astype(BF)
            hot = perm[rows, 0:ROWS]
            lanes = pl.ds((k - 1) * 256, 256)
            value = dot_nn(hot, glo[:, lanes]) + dot_nn(hot, ghi[:, lanes])
            for cy in range(4):
                sbuf[k - 1, 0, cx, cy] = value[cy * CSLOTS:(cy + 1) * CSLOTS, :128]
                sbuf[k - 1, 1, cy, cx] = value[cy * CSLOTS:(cy + 1) * CSLOTS, 128:]

    def fill_all(k):
        @pl.loop(0, 4)
        def _(cx):
            fill(k, cx)

    def fill_rem():
        with jax.named_scope("fill_rem"):
            row = lax.broadcasted_iota(jnp.int32, (CLASSES * RSLOTS, ROWS), 0)
            hot = jnp.where(row == slots[1:2, :], 1.0, 0.0).astype(BF)
            lanes = pl.ds(GW, 256)
            value = dot_nn(hot, glo[:, lanes]) + dot_nn(hot, ghi[:, lanes])
            for cls in range(CLASSES):
                part = value[cls * RSLOTS:(cls + 1) * RSLOTS, :]
                srem[0, cls // NY, cls % NY] = part[:, :128]
                srem[1, cls % NY, cls // NY] = part[:, 128:]

    def ring_rows(k):
        return TABLE_REM if k == WITH_REM else TABLE

    def ring_part(k, s, sign, h):
        n = ring_rows(k) // 2
        if s == 0:
            return pl.ds(h * n + (0 if sign > 0 else n // 2), n // 2)
        return pl.ds(h * n, n)

    def ring_copy(k, s, sign, h):
        o = (z + sign * (4 - s) + NZ) % NZ
        ss, rs = (p_ss, p_rs) if sign > 0 else (m_ss, m_rs)
        part = ring_part(k, s, sign, h)
        return pltpu.make_async_remote_copy(
            tables.at[k, o, part], (plus if sign > 0 else minus).at[k, s, part],
            ss.at[k, s, h], rs.at[k, s, h], device_id=chip_z(sign % NZ), device_id_type=MESH)

    def ring_start(k):
        for h in range(2):
            for sign in (1, -1):
                ring_copy(k, 0, sign, h).start()

    def ring_next(k, s):
        with jax.named_scope("ring%d_%d" % (k, s)):
            for h in range(2):
                for sign in (1, -1):
                    ring_copy(k, s, sign, h).wait_recv()
                    if s == 3:
                        continue
                    o = (z + sign * (3 - s) + NZ) % NZ
                    part = ring_part(k, s, sign, h)
                    tables[k, o, part, :] = tables[k, o, part, :] + (plus if sign > 0 else minus)[k, s, part, :]
                    ring_copy(k, s + 1, sign, h).start()
            if s < 3:
                return
            total = tables[k, z, 0:ring_rows(k), :] + (plus[k, 3, 0:ring_rows(k), :] + minus[k, 3, 0:ring_rows(k), :])
            turned = jnp.transpose(total[0:TABLE, :])
            rows = pl.ds(k * 128, 128)
            ent_out[rows, :] = turned[:, 0:ROWS_DEV]
            rel_out[rows, :] = turned[:, ROWS_DEV:ROWS_DEV + REL_DEV]
            if k == WITH_REM:
                rows = pl.ds(CHUNKS * 128, REM)
                for i in range(TABLE // 128):
                    part = total[TABLE + i * REM:TABLE + (i + 1) * REM, :]
                    if i < ROWS_DEV // 128:
                        ent_out[rows, i * 128:(i + 1) * 128] = part
                    else:
                        rel_out[rows, :] = part[:, 0:REL_DEV]

    def place(o):
        return pl.ds(pl.multiple_of((o // 2) * TABLE, TABLE), TABLE), pl.ds(pl.multiple_of((o % 2) * 768, 768), DEPTH)

    def build_place():
        with jax.named_scope("place"):
            @pl.loop(1, PEERS)
            def _(n):
                pltpu.make_async_remote_copy(
                    ids_recv.at[n], ids_recv.at[n], ids_ss.at[n], ids_rs.at[n],
                    device_id=(ent, 1 - grp), device_id_type=MESH).wait_recv()
            got = jnp.concatenate([ids_recv[n][:, 0:SLOTS] for n in range(PEERS)], axis=1)
            row = lax.broadcasted_iota(jnp.int32, (TABLE, DEPTH), 0)
            for o in range(NZ):
                perm[place(o)] = jnp.where(row == got[o:o + 1, :], 1.0, 0.0).astype(BF)

    def add_up(k):
        with jax.named_scope("add%d" % k):
            flat = rbuf.at[k].reshape(PEERS * CSLOTS, 128)
            for n in (4, 3, 5, 2, 6, 1, 7, 0):
                o = (z + n) % NZ
                hi, lo = split2(flat[pl.ds(o, DEPTH, stride=NZ), :])
                value = dot_nn(perm[place(o)], jnp.concatenate([hi, lo], axis=1))
                tables[k, o, 0:TABLE, :] = value[:, :128] + value[:, 128:]
                if n == 4:
                    ring_start(k)

    def add_up_rem():
        with jax.named_scope("add_rem"):
            for e in range(4):
                for d in range(4):
                    for f in range(2):
                        n = (e * 4 + d) * 2 + f
                        xrem[pl.ds(n * SLOTS, SLOTS), :] = rrem[e, d, f][0:SLOTS, :]
            group = lax.broadcasted_iota(jnp.int32, (DEPTH, 128), 1) // REM
            total = jnp.zeros((TABLE, 256), F32)
            for o in range(NZ):
                hi, lo = split2(jnp.where(group == o, xrem[...], 0.0))
                total = total + dot_nn(perm[place(o)], jnp.concatenate([hi, lo], axis=1))
            total = jnp.transpose(total[:, :128] + total[:, 128:])
            for o in range(NZ):
                for i in range(TABLE // 128):
                    tables[WITH_REM, o, TABLE + i * REM:TABLE + (i + 1) * REM, :] = total[o * REM:(o + 1) * REM, i * 128:(i + 1) * 128]
                tables[WITH_REM, o, TABLE + 5 * REM:TABLE_REM, :] = jnp.zeros((TABLE_REM - TABLE - 5 * REM, 128), F32)

    rem = CHUNKS
    pl.semaphore_wait(barrier, PEERS - 1 + 2)
    forward(0)
    send_ids()
    fill_rem()
    send(rem)
    for d in (1, 3, 2, 0):
        fill(1, (x + d) % 4)
        if d:
            leg1(1, 0, d).start()
    leg1_own(1).start()
    leg1_pair(1).start()
    for d in (1, 3, 2):
        leg1(1, 1, d).start()
    fill_all(2)
    build_place()
    arrive(0)
    add_up(0)
    forward(rem)
    ring_next(0, 0)
    forward(1)
    send(2)
    ring_next(0, 1)
    arrive(rem)
    add_up_rem()
    ring_next(0, 2)
    arrive(1)
    add_up(1)
    ring_next(0, 3)
    ring_next(1, 0)
    forward(2)
    ring_next(1, 1)
    ring_next(1, 2)
    arrive(2)
    add_up(2)
    ring_next(1, 3)
    for s in range(4):
        ring_next(2, s)

    with jax.named_scope("drain"):
        for_peers(lambda j, f: ids_copy(j, f).wait_send())
        for k in range(CHUNKS + 1):
            if k:
                leg1_pair(k).wait_send()
                for d in (1, 2, 3):
                    for g in range(2):
                        leg1(k, g, d).wait_send()
            for d in range(4):
                for e in (1, 2, 3):
                    leg2(k, d, e).wait_send()
        for k in range(CHUNKS):
            for s in range(4):
                for h in range(2):
                    ring_copy(k, s, 1, h).wait_send()
                    ring_copy(k, s, -1, h).wait_send()


def vmem():
    return pl.BlockSpec(memory_space=pltpu.VMEM)


def local_call(*args):
    dma = pltpu.SemaphoreType.DMA
    return pl.pallas_call(
        local_kernel,
        out_shape=(jax.ShapeDtypeStruct((ROWS, GW + 256), BF), jax.ShapeDtypeStruct((ROWS, GW + 256), BF),
                   jax.ShapeDtypeStruct((2, ROWS), jnp.int32), jax.ShapeDtypeStruct((128, 128), jnp.int32),
                   jax.ShapeDtypeStruct((4, 2, 4, CSLOTS, 128), F32)),
        in_specs=[vmem()] * len(args),
        out_specs=(vmem(),) * 4 + (pl.BlockSpec(memory_space=pl.ANY),),
        scratch_shapes=[
            pltpu.VMEM((2, ROWS), jnp.int32),
            pltpu.VMEM((1, ROWS), F32),
            pltpu.VMEM((ROWS, 128), F32),
            pltpu.VMEM((2, 3, W, 128), BF),
            pltpu.VMEM((2, W, 2 * NEGS), BF),
            pltpu.VMEM((EDGES, W), F32),
            pltpu.VMEM((EDGES, W), F32),
            pltpu.VMEM((EDGES, W), F32),
            pltpu.VMEM((EDGES, 1), F32),
            pltpu.VMEM((EDGES, W), F32),
            pltpu.VMEM((EDGES, W), F32),
            pltpu.VMEM((2, 2 * EDGES, W), BF),
            pltpu.VMEM((2 * EDGES, NEGS), F32),
            pltpu.VMEM((2 * EDGES, 128), F32),
            pltpu.VMEM((2 * EDGES, 128), F32),
            pltpu.VMEM((EDGES, 1), F32),
            pltpu.VMEM((2, 2 * EDGES, NEGS), BF),
            pltpu.VMEM((SPANS, 2, NEGS, 2 * EB), BF),
            pltpu.VMEM((EDGES, W), F32),
            pltpu.VMEM((2, EDGES, 256 * CHUNKS), BF),
            pltpu.VMEM((2, ROWS, 256), BF),
            pltpu.VMEM((2, 4, 4, CSLOTS, 128), F32),
            dma((6,)), dma((6,)), dma((2, 4)), dma((4, 2)), dma,
        ],
        compiler_params=pltpu.CompilerParams(collective_id=0, has_side_effects=True, vmem_limit_bytes=60 * MiB),
        name="local",
    )(*args)


def route_call(*args):
    dma = pltpu.SemaphoreType.DMA
    return pl.pallas_call(
        route_kernel,
        out_shape=(jax.ShapeDtypeStruct((K, ROWS_DEV), F32), jax.ShapeDtypeStruct((K, REL_DEV), F32)),
        in_specs=[vmem()] * (len(args) - 1) + [pl.BlockSpec(memory_space=pl.ANY)],
        out_specs=(vmem(), vmem()),
        scratch_shapes=[
            pltpu.VMEM((PEERS, NZ, 128), jnp.int32),
            pltpu.VMEM((CLASSES * CSLOTS, 1536), BF),
            pltpu.VMEM((CHUNKS - 1, 2, 4, 4, CSLOTS, 128), F32),
            pltpu.VMEM((2, 4, 4, RSLOTS, 128), F32),
            pltpu.VMEM((CHUNKS - 1, 4, 2, 4, CSLOTS, 128), F32),
            pltpu.VMEM((4, 2, 4, RSLOTS, 128), F32),
            pltpu.VMEM((CHUNKS, 4, 4, 2, CSLOTS, 128), F32),
            pltpu.VMEM((4, 4, 2, RSLOTS, 128), F32),
            pltpu.VMEM((DEPTH, 128), F32),
            pltpu.VMEM((CHUNKS, NZ, TABLE_REM, 128), F32),
            pltpu.VMEM((CHUNKS, 4, TABLE_REM, 128), F32),
            pltpu.VMEM((CHUNKS, 4, TABLE_REM, 128), F32),
            dma((PEERS,)), dma((PEERS,)),
            dma((CHUNKS + 1, 2, 4)), dma((CHUNKS + 1, 4, 2)), dma((CHUNKS + 1, 4, 4)), dma((CHUNKS + 1, 4, 4)),
            dma((CHUNKS + 1, 5)),
            dma((CHUNKS, 4, 2)), dma((CHUNKS, 4, 2)), dma((CHUNKS, 4, 2)), dma((CHUNKS, 4, 2)),
        ],
        compiler_params=pltpu.CompilerParams(collective_id=1, has_side_effects=True, vmem_limit_bytes=63 * MiB),
        name="route",
    )(*args)


def body(slab, slab_owner, slab_row, rel_slab, rel_owner, rel_row, heads, tails, rels, weights):
    rows = [v.reshape(1, EDGES) for v in (heads, tails, rels, weights)]
    places = [v.reshape(1, v.size) for v in (slab_owner, slab_row, rel_owner, rel_row)]
    ent_grad, rel_grad = route_call(*local_call(slab.T, rel_slab.T, *rows, *places))
    return ent_grad.T, rel_grad.T


def solution(mesh):
    split = P(("ent", "grp"))
    wide = P(("ent", "grp"), None)
    in_specs = (wide, wide, split, wide, wide, split, split, split, split, split)
    out_specs = (P("ent", "grp"), P("ent", "grp"))
    return jax.shard_map(body, mesh=mesh, in_specs=in_specs, out_specs=out_specs, check_vma=False)
```

```python
import jax
import jax.numpy as jnp
from jax import lax
from jax.experimental import pallas as pl
from jax.experimental.pallas import tpu as pltpu
from jax.sharding import PartitionSpec as P

K = 400
HALF = 512
W = 2 * HALF
EB = 256
SPANS = 2
EDGES = EB * SPANS
TOUCHED = 128
NEGS = 512
SLAB = 1152
RSLAB = 128
ROWS = SLAB + RSLAB
ROWS_DEV = 512
REL_DEV = 116
NZ, NX, NY = 8, 4, 4
CLASSES = NX * NY
CAP, RCAP = 18, 4
SLOTS = CAP + RCAP
CSLOTS = SLOTS * NZ
PEERS = 2 * CLASSES
DEPTH = PEERS * SLOTS
TABLE = 640
RSLOTS = 24
WITH_REM = 1
TABLE_REM = 736
CHUNKS = 3
REM = K - 128 * CHUNKS
GW = 256
MiB = 2**20

F32 = jnp.float32
BF = jnp.bfloat16
MESH = pl.DeviceIdType.MESH


def split2(x):
    hi = x.astype(BF)
    return hi, (x - hi.astype(F32)).astype(BF)


def split3(x):
    hi = x.astype(BF)
    rest = x - hi.astype(F32)
    mid = rest.astype(BF)
    return hi, mid, (rest - mid.astype(F32)).astype(BF)


def dot_nn(a, b):
    return lax.dot_general(a, b, (((1,), (0,)), ((), ())), preferred_element_type=F32)


def dot_nt(a, b):
    return lax.dot_general(a, b, (((1,), (1,)), ((), ())), preferred_element_type=F32)


def rows_of(i, n):
    return pl.ds(pl.multiple_of(i * n, n), n)


def tile(k, g):
    return slice(256 * k + 128 * g, 256 * k + 128 * (g + 1))


def local_kernel(slab, rel, hr, tr, rr, weights, slab_owner, slab_row, rel_owner, rel_row, ghi, glo, slots, ids, filled, landed,
                 ints, kpos, zmask, tabs, nparts, hbuf, rbuf, tbuf, pos, qown, qoth, qparts, scores, stat_own, stat_oth,
                 mown, gnp, gnb, qg_out, terms, first_g, perm, sbuf, sends, recvs, l_ss, l_rs, own_sem):
    ent, grp = lax.axis_index("ent"), lax.axis_index("grp")
    peer = (ent, 1 - grp)
    z, c = ent // CLASSES, ent % CLASSES
    x, y = c // NY, c % NY

    def chip(dx, dy):
        return z * CLASSES + ((x + dx) % NX) * NY + (y + dy) % NY

    barrier = pltpu.get_barrier_semaphore()
    pl.semaphore_signal(barrier, inc=1, device_id=peer, device_id_type=MESH)
    for d in (1, 2, 3):
        sender = jnp.where(grp == 0, chip(-d + NX, 0), chip(0, -d + NY))
        for core in range(2):
            pl.semaphore_signal(barrier, inc=1, device_id=(sender, core), device_id_type=MESH)

    def remote(src, dst, i):
        return pltpu.make_async_remote_copy(src, dst, sends.at[i], recvs.at[i], device_id=peer, device_id_type=MESH)

    def store_parts(ref, lanes, source, split):
        for g in range(2):
            for k in range(CHUNKS + 1):
                size = 128 if k < CHUNKS else REM
                start, first = g * K + 128 * k, 256 * k + 128 * g
                for j, part in enumerate(split(source[start:start + size, :])):
                    ref[j, first:first + size, lanes] = part
                    if size < 128:
                        ref[j, first + size:first + 128, lanes] = jnp.zeros((128 - size, part.shape[1]), BF)

    for i, source in enumerate((slab, rel)):
        store_parts(tabs.at[i], pl.ds(0, 128), source[:, 0:128], split3)

    sub128 = lax.broadcasted_iota(jnp.int32, (128, 128), 0)
    sub256 = lax.broadcasted_iota(jnp.int32, (128, EB), 0)

    def gathered(idx, i, rows):
        onehot = jnp.transpose(jnp.where(idx[:, rows] == sub256, 1.0, 0.0)).astype(BF)
        return dot_nt(onehot, tabs[i, 0]) + dot_nt(onehot, tabs[i, 1]) + dot_nt(onehot, tabs[i, 2])

    @pl.loop(0, SPANS)
    def _(i):
        rows = rows_of(i, EB)
        h = gathered(hr, 0, rows)
        r = gathered(rr, 1, rows)
        hbuf[rows, :] = h
        rbuf[rows, :] = r
        for k in range(CHUNKS + 1):
            hre, him, rre, rim = h[:, tile(k, 0)], h[:, tile(k, 1)], r[:, tile(k, 0)], r[:, tile(k, 1)]
            qown[rows, tile(k, 0)] = hre * rre - him * rim
            qown[rows, tile(k, 1)] = hre * rim + him * rre

    pl.semaphore_wait(barrier, 7)
    q_copy = remote(qown, qoth, 0)
    q_copy.start()

    @pl.loop(0, 2 * NEGS // 128)
    def _(i):
        x = slab[:, pl.ds(pl.multiple_of(TOUCHED + i * 128, 128), 128)]
        store_parts(nparts, rows_of(i, 128), x, split2)

    @pl.loop(0, SPANS)
    def _(i):
        rows = rows_of(i, EB)
        t = gathered(tr, 0, rows)
        tbuf[rows, :] = t
        q = qown[rows, :]
        pos[rows, :] = jnp.sum(q * t, axis=1, keepdims=True)
        place = pl.ds(pl.multiple_of(i * (2 * EB), EB), EB)
        for j, part in enumerate(split2(q)):
            qparts[j, place, :] = part

    def score(b, first):
        rows = pl.ds(b * 2 * EB + first, EB)
        negs = pl.ds(b * NEGS, NEGS)
        q, n = [qparts[j, rows, :] for j in range(2)], [nparts[j, :, negs] for j in range(2)]
        scores[rows, :] = (dot_nn(q[0], n[1]) + dot_nn(q[1], n[0])) + dot_nn(q[0], n[0])

    for b in range(SPANS):
        score(b, 0)
    q_copy.wait()

    @pl.loop(0, EDGES // 128)
    def _(i):
        place = pl.ds(pl.multiple_of((i // 2) * (2 * EB) + EB + (i % 2) * 128, 128), 128)
        for j, part in enumerate(split2(qoth[rows_of(i, 128), :])):
            qparts[j, place, :] = part

    for b in range(SPANS):
        score(b, EB)

    lane = lax.broadcasted_iota(jnp.int32, (EB, 128), 1)
    for b in range(SPANS):
        for own in range(2):
            rows = pl.ds(b * 2 * EB + (1 - own) * EB, EB)
            s = scores[rows, :]
            m = jnp.max(s, axis=1, keepdims=True)
            if own:
                p = pos[pl.ds(b * EB, EB), :]
                m = jnp.maximum(m, p)
            e = jnp.exp(s - m)
            total = jnp.sum(e, axis=1, keepdims=True)
            weight = jnp.zeros_like(total)
            if own:
                total = total + jnp.exp(p - m)
                weight = jnp.transpose(jnp.broadcast_to(weights[:, b * EB:(b + 1) * EB], (128, EB)))[:, 0:1]
            scores[rows, :] = e
            stat_own[rows, :] = jnp.where(lane == 0, m, jnp.where(lane == 1, total, weight))
    stat_copy = remote(stat_own, stat_oth, 1)
    stat_copy.start()

    for n, (first, second) in enumerate(((slab_owner, rel_owner), (slab_row, rel_row))):
        ints[n:n + 1, 0:SLAB] = first[...].reshape(1, SLAB)
        ints[n:n + 1, SLAB:ROWS] = second[...].reshape(1, RSLAB) + n * ROWS_DEV
    own = ints[0:1, :]
    oclass, oz = own % CLASSES, own // CLASSES
    owner_row = lax.broadcasted_iota(jnp.int32, (128, ROWS), 0)
    onehot = jnp.where(owner_row == oclass * NZ + oz, 1.0, 0.0)
    for start, size, offset in ((0, SLAB, 0), (SLAB, RSLAB, CAP)):
        part = onehot[:, start:start + size]
        upper = lax.broadcasted_iota(jnp.int32, (size, size), 0) <= lax.broadcasted_iota(jnp.int32, (size, size), 1)
        count = dot_nn(part.astype(BF), jnp.where(upper, 1.0, 0.0).astype(BF))
        kpos[:, start:start + size] = jnp.sum(part * count, axis=0, keepdims=True) + (offset - 1.0)
    kth = kpos[...].astype(jnp.int32)
    slots[0:1, :] = oclass * CSLOTS + kth * NZ + oz
    slots[1:2, :] = oclass * RSLOTS + kth
    for i in range(ROWS // 128):
        zmask[pl.ds(i * 128, 128), :] = jnp.transpose(jnp.where(oz[:, i * 128:(i + 1) * 128] == sub128 // REM, 1.0, 0.0))
    kth_hot = jnp.where(owner_row == kth, 1.0, 0.0).astype(BF)
    number = ints[1:2, :] + 1
    high = ((number // 16) * 16).astype(F32)
    low = (number % 16).astype(F32)
    ids[...] = (dot_nt((onehot * high).astype(BF), kth_hot) + dot_nt((onehot * low).astype(BF), kth_hot)).astype(jnp.int32) - 1

    stat_copy.wait()

    for b in range(SPANS):
        for own in range(2):
            rows = pl.ds(b * 2 * EB + (1 - own) * EB, EB)
            theirs = pl.ds(b * 2 * EB + own * EB, EB)
            a, o = stat_own[rows, :], stat_oth[theirs, :]
            m1, l1, m2, l2 = a[:, 0:1], a[:, 1:2], o[:, 0:1], o[:, 1:2]
            w = a[:, 2:3] if own else o[:, 2:3]
            peak = jnp.maximum(m1, m2)
            f1 = jnp.exp(m1 - peak)
            total = l1 * f1 + l2 * jnp.exp(m2 - peak)
            if own:
                mown[pl.ds(b * EB, EB), :] = w * (jnp.exp(pos[pl.ds(b * EB, EB), :] - peak) / total - 1.0)
            gn = scores[rows, :] * (f1 * (w / total))
            scores[rows, :] = gn
            for j, part in enumerate(split2(gn)):
                gnp[j, rows, :] = part
        gnt = jnp.transpose(scores[pl.ds(b * 2 * EB, 2 * EB), :])
        for j, part in enumerate(split2(gnt)):
            gnb[b, j] = part

    def put(rows, value, chunks):
        for n, k in enumerate(chunks):
            for g in range(2):
                part = value[:, tile(n, g)]
                if k == CHUNKS:
                    for shift in (REM, 2 * REM, 4 * REM):
                        part = part + pltpu.roll(part, shift, 1)
                    part = part * zmask[rows, :]
                hi, lo = split2(part)
                if k < 2:
                    first_g[k, 0, rows, tile(0, g)] = hi
                    first_g[k, 1, rows, tile(0, g)] = lo
                else:
                    ghi[rows, tile(k - 2, g)] = hi
                    glo[rows, tile(k - 2, g)] = lo

    row128 = lax.broadcasted_iota(jnp.int32, (128, EDGES), 0)
    qg_in = qoth

    def gradients(group, chunks):
        start, size = 256 * chunks[0], 256 * len(chunks)
        lanes = pl.ds(start, size)

        def query_part(b, own):
            rows, negs = pl.ds(b * 2 * EB + (1 - own) * EB, EB), pl.ds(b * NEGS, NEGS)
            hi, lo = gnp[0, rows, :], gnp[1, rows, :]
            n0, n1 = nparts[0, lanes, negs], nparts[1, lanes, negs]
            return dot_nt(hi, n1) + dot_nt(lo, n0) + dot_nt(hi, n0)

        copies = []
        for b in range(SPANS):
            rows = pl.ds(b * EB, EB)
            qg_out[rows, lanes] = query_part(b, 0)
            copies.append(remote(qg_out.at[rows, lanes], qg_in.at[rows, lanes], 2 + 2 * group + b))
            copies[-1].start()
        for b in range(SPANS):
            rows = pl.ds(b * EB, EB)
            tbuf[rows, lanes] = mown[rows, :] * tbuf[rows, lanes] + query_part(b, 1)
        for b in range(SPANS):
            edges = pl.ds(b * 2 * EB, 2 * EB)

            @pl.loop(0, NEGS // 256)
            def _(i):
                hi, lo = gnb[b, 0, rows_of(i, 256), :], gnb[b, 1, rows_of(i, 256), :]
                q0, q1 = qparts[0, edges, lanes], qparts[1, edges, lanes]
                value = dot_nn(hi, q1) + dot_nn(lo, q0) + dot_nn(hi, q0)
                put(pl.ds(pl.multiple_of(TOUCHED + b * NEGS + i * 256, 128), 256), value, chunks)
        for copy in copies:
            copy.wait()

        def spread(idx, other):
            @pl.loop(0, EDGES // 128)
            def _(i):
                rows = rows_of(i, 128)
                for n, k in enumerate(chunks):
                    if other is None:
                        values = [mown[rows, :] * qown[rows, tile(k, g)] for g in range(2)]
                    else:
                        gre, gim = (tbuf[rows, tile(k, g)] + qg_in[rows, tile(k, g)] for g in range(2))
                        ore, oim = other[rows, tile(k, 0)], other[rows, tile(k, 1)]
                        values = [gre * ore + gim * oim, gim * ore - gre * oim]
                    for g in range(2):
                        hi, lo = split2(values[g])
                        terms[0, rows, tile(n, g)] = hi
                        terms[1, rows, tile(n, g)] = lo
            onehot = jnp.where(idx[...] == row128, 1.0, 0.0).astype(BF)
            return dot_nn(onehot, terms[1, :, 0:size]) + dot_nn(onehot, terms[0, :, 0:size])

        head = spread(hr, rbuf)
        put(pl.ds(0, 128), head + spread(tr, None), chunks)
        put(pl.ds(SLAB, 128), spread(rr, hbuf), chunks)

    gradients(0, (0,))

    slot_row = lax.broadcasted_iota(jnp.int32, (4 * CSLOTS, ROWS), 0)

    def leg1(g, d):
        f = (grp + g) % 2
        there = (chip(d, 0) if g == 0 else chip(0, d), g)
        return pltpu.make_async_remote_copy(
            sbuf.at[g, ((x if g == 0 else y) + d) % 4], landed.at[d, f],
            l_ss.at[g, d], l_rs.at[d, f], device_id=there, device_id_type=MESH)

    pair = pltpu.make_async_remote_copy(
        sbuf.at[1 - grp, jnp.where(grp == 0, y, x)], landed.at[0, 1], l_ss.at[0, 0], l_rs.at[0, 1],
        device_id=peer, device_id_type=MESH)
    own_copy = pltpu.make_async_copy(sbuf.at[grp, jnp.where(grp == 0, x, y)], landed.at[0, 0], own_sem)
    for d in (1, 3, 2, 0):
        cx = (x + d) % 4
        hot = jnp.where(slot_row == slots[0:1, :] - cx * (4 * CSLOTS), 1.0, 0.0).astype(BF)
        perm[pl.ds(pl.multiple_of(cx * (4 * CSLOTS), 4 * CSLOTS), 4 * CSLOTS), :] = hot
        value = dot_nn(hot, first_g[0, 1]) + dot_nn(hot, first_g[0, 0])
        for cy in range(4):
            sbuf[0, cx, cy] = value[cy * CSLOTS:(cy + 1) * CSLOTS, :128]
            sbuf[1, cy, cx] = value[cy * CSLOTS:(cy + 1) * CSLOTS, 128:]
        if d:
            leg1(0, d).start()
    for d in (1, 3, 2):
        leg1(1, d).start()
    pair.start()
    own_copy.start()

    gradients(1, tuple(range(1, CHUNKS + 1)))

    @pl.loop(0, 4)
    def _(cx):
        hot = perm[pl.ds(pl.multiple_of(cx * (4 * CSLOTS), 4 * CSLOTS), 4 * CSLOTS), :]
        value = dot_nn(hot, first_g[1, 1]) + dot_nn(hot, first_g[1, 0])
        for cy in range(4):
            filled[0, cx, cy] = value[cy * CSLOTS:(cy + 1) * CSLOTS, :128]
            filled[1, cy, cx] = value[cy * CSLOTS:(cy + 1) * CSLOTS, 128:]

    own_copy.wait()
    pair.wait()
    for d in (1, 2, 3):
        for g in range(2):
            leg1(g, d).wait_send()
            pltpu.make_async_remote_copy(
                sbuf.at[0, 0], landed.at[d, g], l_ss.at[0, d], l_rs.at[d, g], device_id=peer, device_id_type=MESH).wait_recv()


def route_kernel(ghi, glo, slots, ids_send, filled, landed, ent_out, rel_out,
                 ids_recv, perm, sbuf, srem, abuf, arem, rbuf, rrem, xrem,
                 tables, plus, minus,
                 ids_ss, ids_rs, a_ss, a_rs, b_ss, b_rs, own_sem, p_ss, p_rs, m_ss, m_rs):
    ent, grp = lax.axis_index("ent"), lax.axis_index("grp")
    z, c = ent // CLASSES, ent % CLASSES
    x, y = c // NY, c % NY
    first, second = jnp.where(grp == 0, x, y), jnp.where(grp == 0, y, x)

    def chip(dx, dy, dz=0):
        return ((z + dz) % NZ) * CLASSES + ((x + dx) % NX) * NY + (y + dy) % NY

    def plane_peer(j, f):
        return (chip(j // NY, j % NY), (grp + f) % 2)

    def chip_z(dz):
        return (chip(0, 0, dz), grp)

    barrier = pltpu.get_barrier_semaphore()

    @pl.loop(0, CLASSES)
    def _(j):
        @pl.when(j > 0)
        def _():
            pl.semaphore_signal(barrier, inc=1, device_id=plane_peer(j, 0), device_id_type=MESH)
        pl.semaphore_signal(barrier, inc=1, device_id=plane_peer(j, 1), device_id_type=MESH)

    pl.semaphore_signal(barrier, inc=1, device_id=chip_z(1), device_id_type=MESH)
    pl.semaphore_signal(barrier, inc=1, device_id=chip_z(NZ - 1), device_id_type=MESH)

    slot = slots[0:1, :]

    def ids_copy(j, f):
        dx, dy = j // NY, j % NY
        cls = ((x + dx) % NX) * NY + (y + dy) % NY
        there = jnp.where((grp + f) % 2 == 0, dy * NX + dx, dx * NY + dy) * 2 + f
        return pltpu.make_async_remote_copy(
            ids_send.at[pl.ds(pl.multiple_of(cls * NZ, NZ), NZ)], ids_recv.at[there],
            ids_ss.at[j * 2 + f], ids_rs.at[there], device_id=plane_peer(j, f), device_id_type=MESH)

    def for_peers(act):
        @pl.loop(0, CLASSES)
        def _(j):
            @pl.when(j > 0)
            def _():
                act(j, 0)
            act(j, 1)

    def send_ids():
        for_peers(lambda j, f: ids_copy(j, f).start())
        ids_recv[0] = ids_send[pl.ds(pl.multiple_of(c * NZ, NZ), NZ), :]

    def bufs(k):
        if k == 0:
            return None, landed, rbuf.at[0]
        if k < CHUNKS:
            return filled if k == 1 else sbuf, abuf.at[k - 1], rbuf.at[k]
        return srem, arem, rrem

    def leg1(k, g, d):
        s, a, _ = bufs(k)
        f = (grp + g) % 2
        there = (chip(d, 0) if g == 0 else chip(0, d), g)
        return pltpu.make_async_remote_copy(
            s.at[g, ((x if g == 0 else y) + d) % 4], a.at[d, f],
            a_ss.at[k, g, d], a_rs.at[k, d, f], device_id=there, device_id_type=MESH)

    def leg1_pair(k):
        s, a, _ = bufs(k)
        return pltpu.make_async_remote_copy(
            s.at[1 - grp, second], a.at[0, 1],
            a_ss.at[k, 0, 0], a_rs.at[k, 0, 1], device_id=(ent, 1 - grp), device_id_type=MESH)

    def leg1_own(k):
        s, a, _ = bufs(k)
        return pltpu.make_async_copy(s.at[grp, first], a.at[0, 0], own_sem.at[k, 0])

    def leg2(k, d, e):
        _, a, r = bufs(k)
        there = jnp.where(grp == 0, chip(0, e), chip(e, 0))
        return pltpu.make_async_remote_copy(
            a.at[d, :, (second + e) % 4], r.at[e, d],
            b_ss.at[k, e, d], b_rs.at[k, e, d], device_id=(there, grp), device_id_type=MESH)

    def leg2_own(k, d):
        _, a, r = bufs(k)
        return pltpu.make_async_copy(a.at[d, :, second], r.at[0, d], own_sem.at[k, 1 + d])

    def send(k):
        with jax.named_scope("send%d" % k):
            leg1_own(k).start()
            leg1_pair(k).start()
            for d in (1, 3, 2):
                for g in range(2):
                    leg1(k, g, d).start()

    def forward(k):
        with jax.named_scope("forward%d" % k):
            for d in (0, 1, 3, 2):
                if k == 0:
                    pass
                elif d == 0:
                    leg1_own(k).wait()
                    leg1_pair(k).wait_recv()
                else:
                    for f in range(2):
                        _, a, _ = bufs(k)
                        pltpu.make_async_remote_copy(
                            a.at[d, f], a.at[d, f], a_ss.at[k, 0, d], a_rs.at[k, d, f],
                            device_id=(ent, 1 - grp), device_id_type=MESH).wait_recv()
                for e in (1, 3, 2):
                    leg2(k, d, e).start()
                leg2_own(k, d).start()

    def arrive(k):
        with jax.named_scope("arrive%d" % k):
            for d in range(4):
                leg2_own(k, d).wait()
                for e in (1, 3, 2):
                    leg2(k, d, e).wait_recv()

    slot_row = lax.broadcasted_iota(jnp.int32, (4 * CSLOTS, ROWS), 0)

    def fill(k, cx):
        with jax.named_scope("fill%d" % k):
            rows = pl.ds(pl.multiple_of(cx * (4 * CSLOTS), 4 * CSLOTS), 4 * CSLOTS)
            if k == 2:
                perm[rows, 0:ROWS] = jnp.where(slot_row == slot - cx * (4 * CSLOTS), 1.0, 0.0).astype(BF)
            hot = perm[rows, 0:ROWS]
            lanes = pl.ds(0, 256)
            value = dot_nn(hot, glo[:, lanes]) + dot_nn(hot, ghi[:, lanes])
            for cy in range(4):
                sbuf[0, cx, cy] = value[cy * CSLOTS:(cy + 1) * CSLOTS, :128]
                sbuf[1, cy, cx] = value[cy * CSLOTS:(cy + 1) * CSLOTS, 128:]

    def fill_all(k):
        @pl.loop(0, 4)
        def _(cx):
            fill(k, cx)

    def fill_rem():
        with jax.named_scope("fill_rem"):
            row = lax.broadcasted_iota(jnp.int32, (CLASSES * RSLOTS, ROWS), 0)
            hot = jnp.where(row == slots[1:2, :], 1.0, 0.0).astype(BF)
            lanes = pl.ds(GW, 256)
            value = dot_nn(hot, glo[:, lanes]) + dot_nn(hot, ghi[:, lanes])
            for cls in range(CLASSES):
                part = value[cls * RSLOTS:(cls + 1) * RSLOTS, :]
                srem[0, cls // NY, cls % NY] = part[:, :128]
                srem[1, cls % NY, cls // NY] = part[:, 128:]

    def ring_rows(k):
        return TABLE_REM if k == WITH_REM else TABLE

    def ring_part(k, s, sign, h):
        n = ring_rows(k) // 2
        if s == 0:
            return pl.ds(h * n + (0 if sign > 0 else n // 2), n // 2)
        return pl.ds(h * n, n)

    def ring_copy(k, s, sign, h):
        o = (z + sign * (4 - s) + NZ) % NZ
        ss, rs = (p_ss, p_rs) if sign > 0 else (m_ss, m_rs)
        part = ring_part(k, s, sign, h)
        return pltpu.make_async_remote_copy(
            tables.at[k, o, part], (plus if sign > 0 else minus).at[k, s, part],
            ss.at[k, s, h], rs.at[k, s, h], device_id=chip_z(sign % NZ), device_id_type=MESH)

    def ring_start(k):
        for h in range(2):
            for sign in (1, -1):
                ring_copy(k, 0, sign, h).start()

    def ring_next(k, s):
        with jax.named_scope("ring%d_%d" % (k, s)):
            for h in range(2):
                for sign in (1, -1):
                    ring_copy(k, s, sign, h).wait_recv()
                    if s == 3:
                        continue
                    o = (z + sign * (3 - s) + NZ) % NZ
                    part = ring_part(k, s, sign, h)
                    tables[k, o, part, :] = tables[k, o, part, :] + (plus if sign > 0 else minus)[k, s, part, :]
                    ring_copy(k, s + 1, sign, h).start()
            if s < 3:
                return
            total = tables[k, z, 0:ring_rows(k), :] + (plus[k, 3, 0:ring_rows(k), :] + minus[k, 3, 0:ring_rows(k), :])
            turned = jnp.transpose(total[0:TABLE, :])
            rows = pl.ds(k * 128, 128)
            ent_out[rows, :] = turned[:, 0:ROWS_DEV]
            rel_out[rows, :] = turned[:, ROWS_DEV:ROWS_DEV + REL_DEV]
            if k == WITH_REM:
                rows = pl.ds(CHUNKS * 128, REM)
                for i in range(TABLE // 128):
                    part = total[TABLE + i * REM:TABLE + (i + 1) * REM, :]
                    if i < ROWS_DEV // 128:
                        ent_out[rows, i * 128:(i + 1) * 128] = part
                    else:
                        rel_out[rows, :] = part[:, 0:REL_DEV]

    def place(o):
        return pl.ds(pl.multiple_of((o // 2) * TABLE, TABLE), TABLE), pl.ds(pl.multiple_of((o % 2) * 768, 768), DEPTH)

    def build_place():
        with jax.named_scope("place"):
            @pl.loop(1, PEERS)
            def _(n):
                pltpu.make_async_remote_copy(
                    ids_recv.at[n], ids_recv.at[n], ids_ss.at[n], ids_rs.at[n],
                    device_id=(ent, 1 - grp), device_id_type=MESH).wait_recv()
            got = jnp.concatenate([ids_recv[n][:, 0:SLOTS] for n in range(PEERS)], axis=1)
            row = lax.broadcasted_iota(jnp.int32, (TABLE, DEPTH), 0)
            for o in range(NZ):
                perm[place(o)] = jnp.where(row == got[o:o + 1, :], 1.0, 0.0).astype(BF)

    def add_up(k):
        with jax.named_scope("add%d" % k):
            flat = rbuf.at[k].reshape(PEERS * CSLOTS, 128)
            for n in (4, 3, 5, 2, 6, 1, 7, 0):
                o = (z + n) % NZ
                hi, lo = split2(flat[pl.ds(o, DEPTH, stride=NZ), :])
                value = dot_nn(perm[place(o)], jnp.concatenate([hi, lo], axis=1))
                tables[k, o, 0:TABLE, :] = value[:, :128] + value[:, 128:]
                if n == 4:
                    ring_start(k)

    def add_up_rem():
        with jax.named_scope("add_rem"):
            for e in range(4):
                for d in range(4):
                    for f in range(2):
                        n = (e * 4 + d) * 2 + f
                        xrem[pl.ds(n * SLOTS, SLOTS), :] = rrem[e, d, f][0:SLOTS, :]
            group = lax.broadcasted_iota(jnp.int32, (DEPTH, 128), 1) // REM
            total = jnp.zeros((TABLE, 256), F32)
            for o in range(NZ):
                hi, lo = split2(jnp.where(group == o, xrem[...], 0.0))
                total = total + dot_nn(perm[place(o)], jnp.concatenate([hi, lo], axis=1))
            total = jnp.transpose(total[:, :128] + total[:, 128:])
            for o in range(NZ):
                for i in range(TABLE // 128):
                    tables[WITH_REM, o, TABLE + i * REM:TABLE + (i + 1) * REM, :] = total[o * REM:(o + 1) * REM, i * 128:(i + 1) * 128]
                tables[WITH_REM, o, TABLE + 5 * REM:TABLE_REM, :] = jnp.zeros((TABLE_REM - TABLE - 5 * REM, 128), F32)

    rem = CHUNKS
    pl.semaphore_wait(barrier, PEERS - 1 + 2)
    for d in range(4):
        leg2(0, d, 1).start()
    send_ids()
    for d in range(4):
        for e in (3, 2):
            leg2(0, d, e).start()
        leg2_own(0, d).start()
    fill_rem()
    send(rem)
    send(1)
    fill_all(2)
    build_place()
    arrive(0)
    add_up(0)
    forward(rem)
    ring_next(0, 0)
    forward(1)
    send(2)
    ring_next(0, 1)
    arrive(rem)
    add_up_rem()
    ring_next(0, 2)
    arrive(1)
    add_up(1)
    ring_next(0, 3)
    ring_next(1, 0)
    forward(2)
    ring_next(1, 1)
    ring_next(1, 2)
    arrive(2)
    add_up(2)
    ring_next(1, 3)
    for s in range(4):
        ring_next(2, s)

    with jax.named_scope("drain"):
        for_peers(lambda j, f: ids_copy(j, f).wait_send())
        for k in range(CHUNKS + 1):
            if k:
                leg1_pair(k).wait_send()
                for d in (1, 2, 3):
                    for g in range(2):
                        leg1(k, g, d).wait_send()
            for d in range(4):
                for e in (1, 2, 3):
                    leg2(k, d, e).wait_send()
        for k in range(CHUNKS):
            for s in range(4):
                for h in range(2):
                    ring_copy(k, s, 1, h).wait_send()
                    ring_copy(k, s, -1, h).wait_send()


def vmem():
    return pl.BlockSpec(memory_space=pltpu.VMEM)


def local_call(*args):
    dma = pltpu.SemaphoreType.DMA
    return pl.pallas_call(
        local_kernel,
        out_shape=(jax.ShapeDtypeStruct((ROWS, GW + 256), BF), jax.ShapeDtypeStruct((ROWS, GW + 256), BF),
                   jax.ShapeDtypeStruct((2, ROWS), jnp.int32), jax.ShapeDtypeStruct((128, 128), jnp.int32),
                   jax.ShapeDtypeStruct((2, 4, 4, CSLOTS, 128), F32), jax.ShapeDtypeStruct((4, 2, 4, CSLOTS, 128), F32)),
        in_specs=[vmem()] * len(args),
        out_specs=(vmem(),) * 5 + (pl.BlockSpec(memory_space=pl.ANY),),
        scratch_shapes=[
            pltpu.VMEM((2, ROWS), jnp.int32),
            pltpu.VMEM((1, ROWS), F32),
            pltpu.VMEM((ROWS, 128), F32),
            pltpu.VMEM((2, 3, W, 128), BF),
            pltpu.VMEM((2, W, 2 * NEGS), BF),
            pltpu.VMEM((EDGES, W), F32),
            pltpu.VMEM((EDGES, W), F32),
            pltpu.VMEM((EDGES, W), F32),
            pltpu.VMEM((EDGES, 1), F32),
            pltpu.VMEM((EDGES, W), F32),
            pltpu.VMEM((EDGES, W), F32),
            pltpu.VMEM((2, 2 * EDGES, W), BF),
            pltpu.VMEM((2 * EDGES, NEGS), F32),
            pltpu.VMEM((2 * EDGES, 128), F32),
            pltpu.VMEM((2 * EDGES, 128), F32),
            pltpu.VMEM((EDGES, 1), F32),
            pltpu.VMEM((2, 2 * EDGES, NEGS), BF),
            pltpu.VMEM((SPANS, 2, NEGS, 2 * EB), BF),
            pltpu.VMEM((EDGES, W), F32),
            pltpu.VMEM((2, EDGES, 256 * CHUNKS), BF),
            pltpu.VMEM((2, 2, ROWS, 256), BF),
            pltpu.VMEM((CLASSES * CSLOTS, ROWS), BF),
            pltpu.VMEM((2, 4, 4, CSLOTS, 128), F32),
            dma((6,)), dma((6,)), dma((2, 4)), dma((4, 2)), dma,
        ],
        compiler_params=pltpu.CompilerParams(collective_id=0, has_side_effects=True, vmem_limit_bytes=63 * MiB),
        name="local",
    )(*args)


def route_call(*args):
    dma = pltpu.SemaphoreType.DMA
    return pl.pallas_call(
        route_kernel,
        out_shape=(jax.ShapeDtypeStruct((K, ROWS_DEV), F32), jax.ShapeDtypeStruct((K, REL_DEV), F32)),
        in_specs=[vmem()] * (len(args) - 2) + [pl.BlockSpec(memory_space=pl.ANY)] * 2,
        out_specs=(vmem(), vmem()),
        scratch_shapes=[
            pltpu.VMEM((PEERS, NZ, 128), jnp.int32),
            pltpu.VMEM((CLASSES * CSLOTS, 1536), BF),
            pltpu.VMEM((2, 4, 4, CSLOTS, 128), F32),
            pltpu.VMEM((2, 4, 4, RSLOTS, 128), F32),
            pltpu.VMEM((CHUNKS - 1, 4, 2, 4, CSLOTS, 128), F32),
            pltpu.VMEM((4, 2, 4, RSLOTS, 128), F32),
            pltpu.VMEM((CHUNKS, 4, 4, 2, CSLOTS, 128), F32),
            pltpu.VMEM((4, 4, 2, RSLOTS, 128), F32),
            pltpu.VMEM((DEPTH, 128), F32),
            pltpu.VMEM((CHUNKS, NZ, TABLE_REM, 128), F32),
            pltpu.VMEM((CHUNKS, 4, TABLE_REM, 128), F32),
            pltpu.VMEM((CHUNKS, 4, TABLE_REM, 128), F32),
            dma((PEERS,)), dma((PEERS,)),
            dma((CHUNKS + 1, 2, 4)), dma((CHUNKS + 1, 4, 2)), dma((CHUNKS + 1, 4, 4)), dma((CHUNKS + 1, 4, 4)),
            dma((CHUNKS + 1, 5)),
            dma((CHUNKS, 4, 2)), dma((CHUNKS, 4, 2)), dma((CHUNKS, 4, 2)), dma((CHUNKS, 4, 2)),
        ],
        compiler_params=pltpu.CompilerParams(collective_id=1, has_side_effects=True, vmem_limit_bytes=63 * MiB),
        name="route",
    )(*args)


def emit_kernel(ent_in, rel_in, ent_out, rel_out):
    ent_out[...] = ent_in[...]
    rel_out[...] = rel_in[...]


def emit_call(ent, rel):
    return pl.pallas_call(
        emit_kernel,
        out_shape=(jax.ShapeDtypeStruct(ent.shape, F32), jax.ShapeDtypeStruct(rel.shape, F32)),
        in_specs=[vmem()] * 2,
        out_specs=(vmem(), vmem()),
        name="emit",
    )(ent, rel)


def body(slab, slab_owner, slab_row, rel_slab, rel_owner, rel_row, heads, tails, rels, weights):
    rows = [v.reshape(1, EDGES) for v in (heads, tails, rels, weights)]
    places = [slab_owner.reshape(1, SLAB), slab_row, rel_owner.reshape(1, RSLAB), rel_row]
    ent_grad, rel_grad = emit_call(*route_call(*local_call(slab.T, rel_slab.T, *rows, *places)))
    return ent_grad.T, rel_grad.T


def solution(mesh):
    split = P(("ent", "grp"))
    wide = P(("ent", "grp"), None)
    in_specs = (wide, wide, split, wide, wide, split, split, split, split, split)
    out_specs = (P("ent", "grp"), P("ent", "grp"))
    return jax.shard_map(body, mesh=mesh, in_specs=in_specs, out_specs=out_specs, check_vma=False)
```

```python
import jax
import jax.numpy as jnp
from jax import lax
from jax.experimental import pallas as pl
from jax.experimental.pallas import tpu as pltpu
from jax.sharding import PartitionSpec as P

K = 400
HALF = 512
W = 2 * HALF
EB = 256
SPANS = 2
EDGES = EB * SPANS
TOUCHED = 128
NEGS = 512
SLAB = 1152
RSLAB = 128
ROWS = SLAB + RSLAB
ROWS_DEV = 512
REL_DEV = 116
NZ, NX, NY = 8, 4, 4
CLASSES = NX * NY
CAP, RCAP = 18, 4
SLOTS = CAP + RCAP
CSLOTS = SLOTS * NZ
PEERS = 2 * CLASSES
DEPTH = PEERS * SLOTS
TABLE = 640
RSLOTS = 24
WITH_REM = 1
TABLE_REM = 736
CHUNKS = 3
REM = K - 128 * CHUNKS
GW = 256
MiB = 2**20

F32 = jnp.float32
BF = jnp.bfloat16
MESH = pl.DeviceIdType.MESH


def split2(x):
    hi = x.astype(BF)
    return hi, (x - hi.astype(F32)).astype(BF)


def dot_nn(a, b):
    return lax.dot_general(a, b, (((1,), (0,)), ((), ())), preferred_element_type=F32)


def dot_nt(a, b):
    return lax.dot_general(a, b, (((1,), (1,)), ((), ())), preferred_element_type=F32)


def rows_of(i, n):
    return pl.ds(pl.multiple_of(i * n, n), n)


def tile(k, g):
    return slice(256 * k + 128 * g, 256 * k + 128 * (g + 1))


def local_kernel(slab, rel, hr, tr, rr, weights, slab_owner, slab_row, rel_owner, rel_row, ghi_out, glo_out, slots, ids, filled_out, landed,
                 ghi, glo, filled, ints, kpos, zmask, tabs, nparts, hbuf, rbuf, tbuf, pos, qown, qoth, qparts, scores, stat_own, stat_oth,
                 mown, gnp, gnb, qg_out, terms, first_g, perm, sbuf, sends, recvs, l_ss, l_rs, own_sem, out_sem):
    ent, grp = lax.axis_index("ent"), lax.axis_index("grp")
    peer = (ent, 1 - grp)
    z, c = ent // CLASSES, ent % CLASSES
    x, y = c // NY, c % NY

    def chip(dx, dy):
        return z * CLASSES + ((x + dx) % NX) * NY + (y + dy) % NY

    barrier = pltpu.get_barrier_semaphore()
    pl.semaphore_signal(barrier, inc=1, device_id=peer, device_id_type=MESH)
    for d in (1, 2, 3):
        sender = jnp.where(grp == 0, chip(-d + NX, 0), chip(0, -d + NY))
        for core in range(2):
            pl.semaphore_signal(barrier, inc=1, device_id=(sender, core), device_id_type=MESH)

    def remote(src, dst, i):
        return pltpu.make_async_remote_copy(src, dst, sends.at[i], recvs.at[i], device_id=peer, device_id_type=MESH)

    def store_parts(ref, lanes, source, split):
        for g in range(2):
            for k in range(CHUNKS + 1):
                size = 128 if k < CHUNKS else REM
                start, first = g * K + 128 * k, 256 * k + 128 * g
                for j, part in enumerate(split(source[start:start + size, :])):
                    ref[j, first:first + size, lanes] = part
                    if size < 128:
                        ref[j, first + size:first + 128, lanes] = jnp.zeros((128 - size, part.shape[1]), BF)

    for i, source in enumerate((slab, rel)):
        store_parts(tabs.at[i], pl.ds(0, 128), source[:, 0:128], split2)

    sub128 = lax.broadcasted_iota(jnp.int32, (128, 128), 0)
    sub256 = lax.broadcasted_iota(jnp.int32, (128, EB), 0)

    def gathered(idx, i, rows):
        onehot = jnp.transpose(jnp.where(idx[:, rows] == sub256, 1.0, 0.0)).astype(BF)
        return dot_nt(onehot, tabs[i, 0]) + dot_nt(onehot, tabs[i, 1])

    @pl.loop(0, SPANS)
    def _(i):
        rows = rows_of(i, EB)
        h = gathered(hr, 0, rows)
        r = gathered(rr, 1, rows)
        hbuf[rows, :] = h
        rbuf[rows, :] = r
        for k in range(CHUNKS + 1):
            hre, him, rre, rim = h[:, tile(k, 0)], h[:, tile(k, 1)], r[:, tile(k, 0)], r[:, tile(k, 1)]
            qown[rows, tile(k, 0)] = hre * rre - him * rim
            qown[rows, tile(k, 1)] = hre * rim + him * rre

    pl.semaphore_wait(barrier, 7)
    q_copy = remote(qown, qoth, 0)
    q_copy.start()

    @pl.loop(0, 2 * NEGS // 128)
    def _(i):
        x = slab[:, pl.ds(pl.multiple_of(TOUCHED + i * 128, 128), 128)]
        store_parts(nparts, rows_of(i, 128), x, split2)

    @pl.loop(0, SPANS)
    def _(i):
        rows = rows_of(i, EB)
        t = gathered(tr, 0, rows)
        tbuf[rows, :] = t
        q = qown[rows, :]
        pos[rows, :] = jnp.sum(q * t, axis=1, keepdims=True)
        place = pl.ds(pl.multiple_of(i * (2 * EB), EB), EB)
        for j, part in enumerate(split2(q)):
            qparts[j, place, :] = part

    def score(b, first):
        rows = pl.ds(b * 2 * EB + first, EB)
        negs = pl.ds(b * NEGS, NEGS)
        q, n = [qparts[j, rows, :] for j in range(2)], [nparts[j, :, negs] for j in range(2)]
        scores[rows, :] = (dot_nn(q[0], n[1]) + dot_nn(q[1], n[0])) + dot_nn(q[0], n[0])

    for b in range(SPANS):
        score(b, 0)
    q_copy.wait()

    @pl.loop(0, EDGES // 128)
    def _(i):
        place = pl.ds(pl.multiple_of((i // 2) * (2 * EB) + EB + (i % 2) * 128, 128), 128)
        for j, part in enumerate(split2(qoth[rows_of(i, 128), :])):
            qparts[j, place, :] = part

    for b in range(SPANS):
        score(b, EB)

    lane = lax.broadcasted_iota(jnp.int32, (EB, 128), 1)
    for b in range(SPANS):
        for own in range(2):
            rows = pl.ds(b * 2 * EB + (1 - own) * EB, EB)
            s = scores[rows, :]
            m = jnp.max(s, axis=1, keepdims=True)
            if own:
                p = pos[pl.ds(b * EB, EB), :]
                m = jnp.maximum(m, p)
            e = jnp.exp(s - m)
            total = jnp.sum(e, axis=1, keepdims=True)
            weight = jnp.zeros_like(total)
            if own:
                total = total + jnp.exp(p - m)
                weight = jnp.transpose(jnp.broadcast_to(weights[:, b * EB:(b + 1) * EB], (128, EB)))[:, 0:1]
            scores[rows, :] = e
            stat_own[rows, :] = jnp.where(lane == 0, m, jnp.where(lane == 1, total, weight))
    stat_copy = remote(stat_own, stat_oth, 1)
    stat_copy.start()

    for n, (first, second) in enumerate(((slab_owner, rel_owner), (slab_row, rel_row))):
        ints[n:n + 1, 0:SLAB] = first[...].reshape(1, SLAB)
        ints[n:n + 1, SLAB:ROWS] = second[...].reshape(1, RSLAB) + n * ROWS_DEV
    own = ints[0:1, :]
    oclass, oz = own % CLASSES, own // CLASSES
    owner_row = lax.broadcasted_iota(jnp.int32, (128, ROWS), 0)
    onehot = jnp.where(owner_row == oclass * NZ + oz, 1.0, 0.0)
    for start, size, offset in ((0, SLAB, 0), (SLAB, RSLAB, CAP)):
        part = onehot[:, start:start + size]
        upper = lax.broadcasted_iota(jnp.int32, (size, size), 0) <= lax.broadcasted_iota(jnp.int32, (size, size), 1)
        count = dot_nn(part.astype(BF), jnp.where(upper, 1.0, 0.0).astype(BF))
        kpos[:, start:start + size] = jnp.sum(part * count, axis=0, keepdims=True) + (offset - 1.0)
    kth = kpos[...].astype(jnp.int32)
    slots[0:1, :] = oclass * CSLOTS + kth * NZ + oz
    slots[1:2, :] = oclass * RSLOTS + kth
    for i in range(ROWS // 128):
        zmask[pl.ds(i * 128, 128), :] = jnp.transpose(jnp.where(oz[:, i * 128:(i + 1) * 128] == sub128 // REM, 1.0, 0.0))
    kth_hot = jnp.where(owner_row == kth, 1.0, 0.0).astype(BF)
    number = ints[1:2, :] + 1
    high = ((number // 16) * 16).astype(F32)
    low = (number % 16).astype(F32)
    ids[...] = (dot_nt((onehot * high).astype(BF), kth_hot) + dot_nt((onehot * low).astype(BF), kth_hot)).astype(jnp.int32) - 1

    stat_copy.wait()

    for b in range(SPANS):
        for own in range(2):
            rows = pl.ds(b * 2 * EB + (1 - own) * EB, EB)
            theirs = pl.ds(b * 2 * EB + own * EB, EB)
            a, o = stat_own[rows, :], stat_oth[theirs, :]
            m1, l1, m2, l2 = a[:, 0:1], a[:, 1:2], o[:, 0:1], o[:, 1:2]
            w = a[:, 2:3] if own else o[:, 2:3]
            peak = jnp.maximum(m1, m2)
            f1 = jnp.exp(m1 - peak)
            total = l1 * f1 + l2 * jnp.exp(m2 - peak)
            if own:
                mown[pl.ds(b * EB, EB), :] = w * (jnp.exp(pos[pl.ds(b * EB, EB), :] - peak) / total - 1.0)
            gn = scores[rows, :] * (f1 * (w / total))
            scores[rows, :] = gn
            for j, part in enumerate(split2(gn)):
                gnp[j, rows, :] = part
        gnt = jnp.transpose(scores[pl.ds(b * 2 * EB, 2 * EB), :])
        for j, part in enumerate(split2(gnt)):
            gnb[b, j] = part

    def put(rows, value, chunks):
        for n, k in enumerate(chunks):
            for g in range(2):
                part = value[:, tile(n, g)]
                if k == CHUNKS:
                    for shift in (REM, 2 * REM, 4 * REM):
                        part = part + pltpu.roll(part, shift, 1)
                    part = part * zmask[rows, :]
                hi, lo = split2(part)
                if k < 2:
                    first_g[k, 0, rows, tile(0, g)] = hi
                    first_g[k, 1, rows, tile(0, g)] = lo
                else:
                    ghi[rows, tile(k - 2, g)] = hi
                    glo[rows, tile(k - 2, g)] = lo

    row128 = lax.broadcasted_iota(jnp.int32, (128, EDGES), 0)
    qg_in = qoth

    def gradients(group, chunks):
        start, size = 256 * chunks[0], 256 * len(chunks)
        lanes = pl.ds(start, size)

        def query_part(b, own):
            rows, negs = pl.ds(b * 2 * EB + (1 - own) * EB, EB), pl.ds(b * NEGS, NEGS)
            hi, lo = gnp[0, rows, :], gnp[1, rows, :]
            n0, n1 = nparts[0, lanes, negs], nparts[1, lanes, negs]
            return dot_nt(hi, n1) + dot_nt(lo, n0) + dot_nt(hi, n0)

        copies = []
        for b in range(SPANS):
            rows = pl.ds(b * EB, EB)
            qg_out[rows, lanes] = query_part(b, 0)
            copies.append(remote(qg_out.at[rows, lanes], qg_in.at[rows, lanes], 2 + 2 * group + b))
            copies[-1].start()
        for b in range(SPANS):
            rows = pl.ds(b * EB, EB)
            tbuf[rows, lanes] = mown[rows, :] * tbuf[rows, lanes] + query_part(b, 1)
        for b in range(SPANS):
            edges = pl.ds(b * 2 * EB, 2 * EB)

            @pl.loop(0, NEGS // 256)
            def _(i):
                hi, lo = gnb[b, 0, rows_of(i, 256), :], gnb[b, 1, rows_of(i, 256), :]
                q0, q1 = qparts[0, edges, lanes], qparts[1, edges, lanes]
                value = dot_nn(hi, q1) + dot_nn(lo, q0) + dot_nn(hi, q0)
                put(pl.ds(pl.multiple_of(TOUCHED + b * NEGS + i * 256, 128), 256), value, chunks)
        for copy in copies:
            copy.wait()

        def spread(idx, other):
            @pl.loop(0, EDGES // 128)
            def _(i):
                rows = rows_of(i, 128)
                for n, k in enumerate(chunks):
                    if other is None:
                        values = [mown[rows, :] * qown[rows, tile(k, g)] for g in range(2)]
                    else:
                        gre, gim = (tbuf[rows, tile(k, g)] + qg_in[rows, tile(k, g)] for g in range(2))
                        ore, oim = other[rows, tile(k, 0)], other[rows, tile(k, 1)]
                        values = [gre * ore + gim * oim, gim * ore - gre * oim]
                    for g in range(2):
                        hi, lo = split2(values[g])
                        terms[0, rows, tile(n, g)] = hi
                        terms[1, rows, tile(n, g)] = lo
            onehot = jnp.where(idx[...] == row128, 1.0, 0.0).astype(BF)
            return dot_nn(onehot, terms[1, :, 0:size]) + dot_nn(onehot, terms[0, :, 0:size])

        head = spread(hr, rbuf)
        put(pl.ds(0, 128), head + spread(tr, None), chunks)
        put(pl.ds(SLAB, 128), spread(rr, hbuf), chunks)

    gradients(0, (0,))

    slot_row = lax.broadcasted_iota(jnp.int32, (4 * CSLOTS, ROWS), 0)

    def leg1(g, d):
        f = (grp + g) % 2
        there = (chip(d, 0) if g == 0 else chip(0, d), g)
        return pltpu.make_async_remote_copy(
            sbuf.at[g, ((x if g == 0 else y) + d) % 4], landed.at[d, f],
            l_ss.at[g, d], l_rs.at[d, f], device_id=there, device_id_type=MESH)

    pair = pltpu.make_async_remote_copy(
        sbuf.at[1 - grp, jnp.where(grp == 0, y, x)], landed.at[0, 1], l_ss.at[0, 0], l_rs.at[0, 1],
        device_id=peer, device_id_type=MESH)
    own_copy = pltpu.make_async_copy(sbuf.at[grp, jnp.where(grp == 0, x, y)], landed.at[0, 0], own_sem)
    for d in (1, 3, 2, 0):
        cx = (x + d) % 4
        hot = jnp.where(slot_row == slots[0:1, :] - cx * (4 * CSLOTS), 1.0, 0.0).astype(BF)
        perm[pl.ds(pl.multiple_of(cx * (4 * CSLOTS), 4 * CSLOTS), 4 * CSLOTS), :] = hot
        value = dot_nn(hot, first_g[0, 1]) + dot_nn(hot, first_g[0, 0])
        for cy in range(4):
            sbuf[0, cx, cy] = value[cy * CSLOTS:(cy + 1) * CSLOTS, :128]
            sbuf[1, cy, cx] = value[cy * CSLOTS:(cy + 1) * CSLOTS, 128:]
        if d:
            leg1(0, d).start()
    for d in (1, 3, 2):
        leg1(1, d).start()
    pair.start()
    own_copy.start()

    gradients(1, tuple(range(1, CHUNKS + 1)))
    outs = [pltpu.make_async_copy(a, b, out_sem.at[n]) for n, (a, b) in enumerate(((ghi, ghi_out), (glo, glo_out)))]
    for copy in outs:
        copy.start()

    def filled_copy(g, cx):
        part = filled.at[0, cx] if g == 0 else filled.at[1, :, cx]
        return pltpu.make_async_copy(part, filled_out.at[0, cx] if g == 0 else filled_out.at[1, :, cx], out_sem.at[2 + 2 * cx + g])

    @pl.loop(0, 4)
    def _(cx):
        hot = perm[pl.ds(pl.multiple_of(cx * (4 * CSLOTS), 4 * CSLOTS), 4 * CSLOTS), :]
        value = dot_nn(hot, first_g[1, 1]) + dot_nn(hot, first_g[1, 0])
        for cy in range(4):
            filled[0, cx, cy] = value[cy * CSLOTS:(cy + 1) * CSLOTS, :128]
            filled[1, cy, cx] = value[cy * CSLOTS:(cy + 1) * CSLOTS, 128:]
        for g in range(2):
            filled_copy(g, cx).start()

    @pl.loop(0, 4)
    def _(cx):
        for g in range(2):
            filled_copy(g, cx).wait()

    for copy in outs:
        copy.wait()
    own_copy.wait()
    pair.wait()
    for d in (1, 2, 3):
        for g in range(2):
            leg1(g, d).wait_send()
            pltpu.make_async_remote_copy(
                sbuf.at[0, 0], landed.at[d, g], l_ss.at[0, d], l_rs.at[d, g], device_id=peer, device_id_type=MESH).wait_recv()


def route_kernel(ghi_in, glo_in, slots, ids_send, filled, landed, ent_out, rel_out,
                 ghi, glo, ids_recv, perm, sbuf, srem, abuf, arem, rbuf, rrem, xrem,
                 tables, plus, minus,
                 ids_ss, ids_rs, a_ss, a_rs, b_ss, b_rs, own_sem, in_sem, p_ss, p_rs, m_ss, m_rs):
    ent, grp = lax.axis_index("ent"), lax.axis_index("grp")
    z, c = ent // CLASSES, ent % CLASSES
    x, y = c // NY, c % NY
    first, second = jnp.where(grp == 0, x, y), jnp.where(grp == 0, y, x)

    def chip(dx, dy, dz=0):
        return ((z + dz) % NZ) * CLASSES + ((x + dx) % NX) * NY + (y + dy) % NY

    def plane_peer(j, f):
        return (chip(j // NY, j % NY), (grp + f) % 2)

    def chip_z(dz):
        return (chip(0, 0, dz), grp)

    ins = [pltpu.make_async_copy(a, b, in_sem.at[n]) for n, (a, b) in enumerate(((ghi_in, ghi), (glo_in, glo)))]
    for copy in ins:
        copy.start()
    barrier = pltpu.get_barrier_semaphore()

    @pl.loop(0, CLASSES)
    def _(j):
        @pl.when(j > 0)
        def _():
            pl.semaphore_signal(barrier, inc=1, device_id=plane_peer(j, 0), device_id_type=MESH)
        pl.semaphore_signal(barrier, inc=1, device_id=plane_peer(j, 1), device_id_type=MESH)

    pl.semaphore_signal(barrier, inc=1, device_id=chip_z(1), device_id_type=MESH)
    pl.semaphore_signal(barrier, inc=1, device_id=chip_z(NZ - 1), device_id_type=MESH)

    slot = slots[0:1, :]

    def ids_copy(j, f):
        dx, dy = j // NY, j % NY
        cls = ((x + dx) % NX) * NY + (y + dy) % NY
        there = jnp.where((grp + f) % 2 == 0, dy * NX + dx, dx * NY + dy) * 2 + f
        return pltpu.make_async_remote_copy(
            ids_send.at[pl.ds(pl.multiple_of(cls * NZ, NZ), NZ)], ids_recv.at[there],
            ids_ss.at[j * 2 + f], ids_rs.at[there], device_id=plane_peer(j, f), device_id_type=MESH)

    def for_peers(act):
        @pl.loop(0, CLASSES)
        def _(j):
            @pl.when(j > 0)
            def _():
                act(j, 0)
            act(j, 1)

    def send_ids():
        for_peers(lambda j, f: ids_copy(j, f).start())
        ids_recv[0] = ids_send[pl.ds(pl.multiple_of(c * NZ, NZ), NZ), :]

    def bufs(k):
        if k == 0:
            return None, landed, rbuf.at[0]
        if k < CHUNKS:
            return filled if k == 1 else sbuf, abuf.at[k - 1], rbuf.at[k]
        return srem, arem, rrem

    def leg1(k, g, d):
        s, a, _ = bufs(k)
        f = (grp + g) % 2
        there = (chip(d, 0) if g == 0 else chip(0, d), g)
        return pltpu.make_async_remote_copy(
            s.at[g, ((x if g == 0 else y) + d) % 4], a.at[d, f],
            a_ss.at[k, g, d], a_rs.at[k, d, f], device_id=there, device_id_type=MESH)

    def leg1_pair(k):
        s, a, _ = bufs(k)
        return pltpu.make_async_remote_copy(
            s.at[1 - grp, second], a.at[0, 1],
            a_ss.at[k, 0, 0], a_rs.at[k, 0, 1], device_id=(ent, 1 - grp), device_id_type=MESH)

    def leg1_own(k):
        s, a, _ = bufs(k)
        return pltpu.make_async_copy(s.at[grp, first], a.at[0, 0], own_sem.at[k, 0])

    def leg2(k, d, e):
        _, a, r = bufs(k)
        there = jnp.where(grp == 0, chip(0, e), chip(e, 0))
        return pltpu.make_async_remote_copy(
            a.at[d, :, (second + e) % 4], r.at[e, d],
            b_ss.at[k, e, d], b_rs.at[k, e, d], device_id=(there, grp), device_id_type=MESH)

    def leg2_own(k, d):
        _, a, r = bufs(k)
        return pltpu.make_async_copy(a.at[d, :, second], r.at[0, d], own_sem.at[k, 1 + d])

    def send(k):
        with jax.named_scope("send%d" % k):
            leg1_own(k).start()
            leg1_pair(k).start()
            for d in (1, 3, 2):
                for g in range(2):
                    leg1(k, g, d).start()

    def forward(k):
        with jax.named_scope("forward%d" % k):
            for d in (0, 1, 3, 2):
                if k == 0:
                    pass
                elif d == 0:
                    leg1_own(k).wait()
                    leg1_pair(k).wait_recv()
                else:
                    for f in range(2):
                        _, a, _ = bufs(k)
                        pltpu.make_async_remote_copy(
                            a.at[d, f], a.at[d, f], a_ss.at[k, 0, d], a_rs.at[k, d, f],
                            device_id=(ent, 1 - grp), device_id_type=MESH).wait_recv()
                for e in (1, 3, 2):
                    leg2(k, d, e).start()
                leg2_own(k, d).start()

    def arrive(k):
        with jax.named_scope("arrive%d" % k):
            for d in range(4):
                leg2_own(k, d).wait()
                for e in (1, 3, 2):
                    leg2(k, d, e).wait_recv()

    slot_row = lax.broadcasted_iota(jnp.int32, (4 * CSLOTS, ROWS), 0)

    def fill(k, cx):
        with jax.named_scope("fill%d" % k):
            rows = pl.ds(pl.multiple_of(cx * (4 * CSLOTS), 4 * CSLOTS), 4 * CSLOTS)
            if k == 2:
                perm[rows, 0:ROWS] = jnp.where(slot_row == slot - cx * (4 * CSLOTS), 1.0, 0.0).astype(BF)
            hot = perm[rows, 0:ROWS]
            lanes = pl.ds(0, 256)
            value = dot_nn(hot, glo[:, lanes]) + dot_nn(hot, ghi[:, lanes])
            for cy in range(4):
                sbuf[0, cx, cy] = value[cy * CSLOTS:(cy + 1) * CSLOTS, :128]
                sbuf[1, cy, cx] = value[cy * CSLOTS:(cy + 1) * CSLOTS, 128:]

    def fill_all(k):
        @pl.loop(0, 4)
        def _(cx):
            fill(k, cx)

    def fill_rem():
        with jax.named_scope("fill_rem"):
            row = lax.broadcasted_iota(jnp.int32, (CLASSES * RSLOTS, ROWS), 0)
            hot = jnp.where(row == slots[1:2, :], 1.0, 0.0).astype(BF)
            lanes = pl.ds(GW, 256)
            value = dot_nn(hot, glo[:, lanes]) + dot_nn(hot, ghi[:, lanes])
            for cls in range(CLASSES):
                part = value[cls * RSLOTS:(cls + 1) * RSLOTS, :]
                srem[0, cls // NY, cls % NY] = part[:, :128]
                srem[1, cls % NY, cls // NY] = part[:, 128:]

    def ring_rows(k):
        return TABLE_REM if k == WITH_REM else TABLE

    def ring_part(k, s, sign, h):
        n = ring_rows(k) // 2
        if s == 0:
            return pl.ds(h * n + (0 if sign > 0 else n // 2), n // 2)
        return pl.ds(h * n, n)

    def ring_copy(k, s, sign, h):
        o = (z + sign * (4 - s) + NZ) % NZ
        ss, rs = (p_ss, p_rs) if sign > 0 else (m_ss, m_rs)
        part = ring_part(k, s, sign, h)
        return pltpu.make_async_remote_copy(
            tables.at[k, o, part], (plus if sign > 0 else minus).at[k, s, part],
            ss.at[k, s, h], rs.at[k, s, h], device_id=chip_z(sign % NZ), device_id_type=MESH)

    def ring_start(k):
        for h in range(2):
            for sign in (1, -1):
                ring_copy(k, 0, sign, h).start()

    def ring_next(k, s):
        with jax.named_scope("ring%d_%d" % (k, s)):
            for h in range(2):
                for sign in (1, -1):
                    ring_copy(k, s, sign, h).wait_recv()
                    if s == 3:
                        continue
                    o = (z + sign * (3 - s) + NZ) % NZ
                    part = ring_part(k, s, sign, h)
                    tables[k, o, part, :] = tables[k, o, part, :] + (plus if sign > 0 else minus)[k, s, part, :]
                    ring_copy(k, s + 1, sign, h).start()
            if s < 3:
                return
            total = tables[k, z, 0:ring_rows(k), :] + (plus[k, 3, 0:ring_rows(k), :] + minus[k, 3, 0:ring_rows(k), :])
            turned = jnp.transpose(total[0:TABLE, :])
            rows = pl.ds(k * 128, 128)
            ent_out[rows, :] = turned[:, 0:ROWS_DEV]
            rel_out[rows, :] = turned[:, ROWS_DEV:ROWS_DEV + REL_DEV]
            if k == WITH_REM:
                rows = pl.ds(CHUNKS * 128, REM)
                for i in range(TABLE // 128):
                    part = total[TABLE + i * REM:TABLE + (i + 1) * REM, :]
                    if i < ROWS_DEV // 128:
                        ent_out[rows, i * 128:(i + 1) * 128] = part
                    else:
                        rel_out[rows, :] = part[:, 0:REL_DEV]

    def place(o):
        return pl.ds(pl.multiple_of((o // 2) * TABLE, TABLE), TABLE), pl.ds(pl.multiple_of((o % 2) * 768, 768), DEPTH)

    def build_place():
        with jax.named_scope("place"):
            @pl.loop(1, PEERS)
            def _(n):
                pltpu.make_async_remote_copy(
                    ids_recv.at[n], ids_recv.at[n], ids_ss.at[n], ids_rs.at[n],
                    device_id=(ent, 1 - grp), device_id_type=MESH).wait_recv()
            got = jnp.concatenate([ids_recv[n][:, 0:SLOTS] for n in range(PEERS)], axis=1)
            row = lax.broadcasted_iota(jnp.int32, (TABLE, DEPTH), 0)
            for o in range(NZ):
                perm[place(o)] = jnp.where(row == got[o:o + 1, :], 1.0, 0.0).astype(BF)

    def add_up(k):
        with jax.named_scope("add%d" % k):
            flat = rbuf.at[k].reshape(PEERS * CSLOTS, 128)
            for n in (4, 3, 5, 2, 6, 1, 7, 0):
                o = (z + n) % NZ
                hi, lo = split2(flat[pl.ds(o, DEPTH, stride=NZ), :])
                value = dot_nn(perm[place(o)], jnp.concatenate([hi, lo], axis=1))
                tables[k, o, 0:TABLE, :] = value[:, :128] + value[:, 128:]
                if n == 4:
                    ring_start(k)

    def add_up_rem():
        with jax.named_scope("add_rem"):
            for e in range(4):
                for d in range(4):
                    for f in range(2):
                        n = (e * 4 + d) * 2 + f
                        xrem[pl.ds(n * SLOTS, SLOTS), :] = rrem[e, d, f][0:SLOTS, :]
            group = lax.broadcasted_iota(jnp.int32, (DEPTH, 128), 1) // REM
            total = jnp.zeros((TABLE, 256), F32)
            for o in range(NZ):
                hi, lo = split2(jnp.where(group == o, xrem[...], 0.0))
                total = total + dot_nn(perm[place(o)], jnp.concatenate([hi, lo], axis=1))
            total = jnp.transpose(total[:, :128] + total[:, 128:])
            for o in range(NZ):
                for i in range(TABLE // 128):
                    tables[WITH_REM, o, TABLE + i * REM:TABLE + (i + 1) * REM, :] = total[o * REM:(o + 1) * REM, i * 128:(i + 1) * 128]
                tables[WITH_REM, o, TABLE + 5 * REM:TABLE_REM, :] = jnp.zeros((TABLE_REM - TABLE - 5 * REM, 128), F32)

    rem = CHUNKS
    pl.semaphore_wait(barrier, PEERS - 1 + 2)
    for d in range(4):
        leg2(0, d, 1).start()
    send_ids()
    for d in range(4):
        for e in (3, 2):
            leg2(0, d, e).start()
        leg2_own(0, d).start()
    for copy in ins:
        copy.wait()
    fill_rem()
    send(rem)
    send(1)
    fill_all(2)
    build_place()
    arrive(0)
    add_up(0)
    forward(rem)
    ring_next(0, 0)
    forward(1)
    send(2)
    ring_next(0, 1)
    arrive(rem)
    add_up_rem()
    ring_next(0, 2)
    arrive(1)
    add_up(1)
    ring_next(0, 3)
    ring_next(1, 0)
    forward(2)
    ring_next(1, 1)
    ring_next(1, 2)
    arrive(2)
    add_up(2)
    ring_next(1, 3)

    def legs_sent(k):
        if k:
            leg1_pair(k).wait_send()
            for d in (1, 2, 3):
                for g in range(2):
                    leg1(k, g, d).wait_send()
        for d in range(4):
            for e in (1, 2, 3):
                leg2(k, d, e).wait_send()

    def ring_sent(k):
        for s in range(4):
            for h in range(2):
                ring_copy(k, s, 1, h).wait_send()
                ring_copy(k, s, -1, h).wait_send()

    for_peers(lambda j, f: ids_copy(j, f).wait_send())
    legs_sent(0)
    ring_next(2, 0)
    legs_sent(1)
    legs_sent(rem)
    ring_sent(0)
    ring_next(2, 1)
    legs_sent(2)
    ring_sent(1)
    ring_next(2, 2)
    ring_next(2, 3)
    ring_sent(2)


def vmem():
    return pl.BlockSpec(memory_space=pltpu.VMEM)


def anywhere():
    return pl.BlockSpec(memory_space=pl.ANY)


def local_call(*args):
    dma = pltpu.SemaphoreType.DMA
    return pl.pallas_call(
        local_kernel,
        out_shape=(jax.ShapeDtypeStruct((ROWS, GW + 256), BF), jax.ShapeDtypeStruct((ROWS, GW + 256), BF),
                   jax.ShapeDtypeStruct((2, ROWS), jnp.int32), jax.ShapeDtypeStruct((128, 128), jnp.int32),
                   jax.ShapeDtypeStruct((2, 4, 4, CSLOTS, 128), F32), jax.ShapeDtypeStruct((4, 2, 4, CSLOTS, 128), F32)),
        in_specs=[vmem()] * len(args),
        out_specs=(anywhere(), anywhere(), vmem(), vmem(), anywhere(), anywhere()),
        scratch_shapes=[
            pltpu.VMEM((ROWS, GW + 256), BF),
            pltpu.VMEM((ROWS, GW + 256), BF),
            pltpu.VMEM((2, 4, 4, CSLOTS, 128), F32),
            pltpu.VMEM((2, ROWS), jnp.int32),
            pltpu.VMEM((1, ROWS), F32),
            pltpu.VMEM((ROWS, 128), F32),
            pltpu.VMEM((2, 2, W, 128), BF),
            pltpu.VMEM((2, W, 2 * NEGS), BF),
            pltpu.VMEM((EDGES, W), F32),
            pltpu.VMEM((EDGES, W), F32),
            pltpu.VMEM((EDGES, W), F32),
            pltpu.VMEM((EDGES, 1), F32),
            pltpu.VMEM((EDGES, W), F32),
            pltpu.VMEM((EDGES, W), F32),
            pltpu.VMEM((2, 2 * EDGES, W), BF),
            pltpu.VMEM((2 * EDGES, NEGS), F32),
            pltpu.VMEM((2 * EDGES, 128), F32),
            pltpu.VMEM((2 * EDGES, 128), F32),
            pltpu.VMEM((EDGES, 1), F32),
            pltpu.VMEM((2, 2 * EDGES, NEGS), BF),
            pltpu.VMEM((SPANS, 2, NEGS, 2 * EB), BF),
            pltpu.VMEM((EDGES, W), F32),
            pltpu.VMEM((2, EDGES, 256 * CHUNKS), BF),
            pltpu.VMEM((2, 2, ROWS, 256), BF),
            pltpu.VMEM((CLASSES * CSLOTS, ROWS), BF),
            pltpu.VMEM((2, 4, 4, CSLOTS, 128), F32),
            dma((6,)), dma((6,)), dma((2, 4)), dma((4, 2)), dma, dma((10,)),
        ],
        compiler_params=pltpu.CompilerParams(collective_id=0, has_side_effects=True, vmem_limit_bytes=63 * MiB),
        name="local",
    )(*args)


def route_call(*args):
    dma = pltpu.SemaphoreType.DMA
    return pl.pallas_call(
        route_kernel,
        out_shape=(jax.ShapeDtypeStruct((K, ROWS_DEV), F32), jax.ShapeDtypeStruct((K, REL_DEV), F32)),
        in_specs=[anywhere(), anywhere(), vmem(), vmem(), anywhere(), anywhere()],
        out_specs=(vmem(), vmem()),
        scratch_shapes=[
            pltpu.VMEM((ROWS, GW + 256), BF),
            pltpu.VMEM((ROWS, GW + 256), BF),
            pltpu.VMEM((PEERS, NZ, 128), jnp.int32),
            pltpu.VMEM((CLASSES * CSLOTS, 1536), BF),
            pltpu.VMEM((2, 4, 4, CSLOTS, 128), F32),
            pltpu.VMEM((2, 4, 4, RSLOTS, 128), F32),
            pltpu.VMEM((CHUNKS - 1, 4, 2, 4, CSLOTS, 128), F32),
            pltpu.VMEM((4, 2, 4, RSLOTS, 128), F32),
            pltpu.VMEM((CHUNKS, 4, 4, 2, CSLOTS, 128), F32),
            pltpu.VMEM((4, 4, 2, RSLOTS, 128), F32),
            pltpu.VMEM((DEPTH, 128), F32),
            pltpu.VMEM((CHUNKS, NZ, TABLE_REM, 128), F32),
            pltpu.VMEM((CHUNKS, 4, TABLE_REM, 128), F32),
            pltpu.VMEM((CHUNKS, 4, TABLE_REM, 128), F32),
            dma((PEERS,)), dma((PEERS,)),
            dma((CHUNKS + 1, 2, 4)), dma((CHUNKS + 1, 4, 2)), dma((CHUNKS + 1, 4, 4)), dma((CHUNKS + 1, 4, 4)),
            dma((CHUNKS + 1, 5)), dma((2,)),
            dma((CHUNKS, 4, 2)), dma((CHUNKS, 4, 2)), dma((CHUNKS, 4, 2)), dma((CHUNKS, 4, 2)),
        ],
        compiler_params=pltpu.CompilerParams(collective_id=1, has_side_effects=True, vmem_limit_bytes=63 * MiB),
        name="route",
    )(*args)


def emit_kernel(ent_in, rel_in, ent_out, rel_out):
    ent_out[...] = ent_in[...]
    rel_out[...] = rel_in[...]


def emit_call(ent, rel):
    return pl.pallas_call(
        emit_kernel,
        out_shape=(jax.ShapeDtypeStruct(ent.shape, F32), jax.ShapeDtypeStruct(rel.shape, F32)),
        in_specs=[vmem()] * 2,
        out_specs=(vmem(), vmem()),
        name="emit",
    )(ent, rel)


def body(slab, slab_owner, slab_row, rel_slab, rel_owner, rel_row, heads, tails, rels, weights):
    rows = [v.reshape(1, EDGES) for v in (heads, tails, rels, weights)]
    places = [slab_owner.reshape(1, SLAB), slab_row, rel_owner.reshape(1, RSLAB), rel_row]
    ent_grad, rel_grad = emit_call(*route_call(*local_call(slab.T, rel_slab.T, *rows, *places)))
    return ent_grad.T, rel_grad.T


def solution(mesh):
    split = P(("ent", "grp"))
    wide = P(("ent", "grp"), None)
    in_specs = (wide, wide, split, wide, wide, split, split, split, split, split)
    out_specs = (P("ent", "grp"), P("ent", "grp"))
    return jax.shard_map(body, mesh=mesh, in_specs=in_specs, out_specs=out_specs, check_vma=False)
```

```python
import jax
import jax.numpy as jnp
from jax import lax
from jax.experimental import pallas as pl
from jax.experimental.pallas import tpu as pltpu
from jax.sharding import PartitionSpec as P

K = 400
HALF = 512
W = 2 * HALF
EB = 256
SPANS = 2
EDGES = EB * SPANS
TOUCHED = 128
NEGS = 512
SLAB = 1152
RSLAB = 128
ROWS = SLAB + RSLAB
ROWS_DEV = 512
REL_DEV = 116
NZ, NX, NY = 8, 4, 4
CLASSES = NX * NY
CAP, RCAP = 18, 4
SLOTS = CAP + RCAP
CSLOTS = SLOTS * NZ
PEERS = 2 * CLASSES
DEPTH = PEERS * SLOTS
TABLE = 640
RSLOTS = 24
WITH_REM = 1
TABLE_REM = 736
CHUNKS = 3
REM = K - 128 * CHUNKS
GW = 256
MiB = 2**20

F32 = jnp.float32
BF = jnp.bfloat16
MESH = pl.DeviceIdType.MESH


def split2(x):
    hi = x.astype(BF)
    return hi, (x - hi.astype(F32)).astype(BF)


def dot_nn(a, b):
    return lax.dot_general(a, b, (((1,), (0,)), ((), ())), preferred_element_type=F32)


def dot_nt(a, b):
    return lax.dot_general(a, b, (((1,), (1,)), ((), ())), preferred_element_type=F32)


def rows_of(i, n):
    return pl.ds(pl.multiple_of(i * n, n), n)


def tile(k, g):
    return slice(256 * k + 128 * g, 256 * k + 128 * (g + 1))


def local_kernel(slab, rel, hr, tr, rr, weights, slab_owner, slab_row, rel_owner, rel_row, ghi_out, glo_out, slots, ids, filled_out, landed,
                 ghi, glo, filled, ints, kpos, zmask, tabs, nparts, hbuf, rbuf, tbuf, pos, qown, qoth, qparts, scores, stat_own, stat_oth,
                 mown, gnp, gnb, qg_out, terms, first_g, perm, sbuf, sends, recvs, l_ss, l_rs, own_sem, out_sem):
    ent, grp = lax.axis_index("ent"), lax.axis_index("grp")
    peer = (ent, 1 - grp)
    z, c = ent // CLASSES, ent % CLASSES
    x, y = c // NY, c % NY

    def chip(dx, dy):
        return z * CLASSES + ((x + dx) % NX) * NY + (y + dy) % NY

    barrier = pltpu.get_barrier_semaphore()
    pl.semaphore_signal(barrier, inc=1, device_id=peer, device_id_type=MESH)
    for d in (1, 2, 3):
        sender = jnp.where(grp == 0, chip(-d + NX, 0), chip(0, -d + NY))
        for core in range(2):
            pl.semaphore_signal(barrier, inc=1, device_id=(sender, core), device_id_type=MESH)

    def remote(src, dst, i):
        return pltpu.make_async_remote_copy(src, dst, sends.at[i], recvs.at[i], device_id=peer, device_id_type=MESH)

    def store_parts(ref, lanes, source, split):
        for g in range(2):
            for k in range(CHUNKS + 1):
                size = 128 if k < CHUNKS else REM
                start, first = g * K + 128 * k, 256 * k + 128 * g
                for j, part in enumerate(split(source[start:start + size, :])):
                    ref[j, first:first + size, lanes] = part
                    if size < 128:
                        ref[j, first + size:first + 128, lanes] = jnp.zeros((128 - size, part.shape[1]), BF)

    for i, source in enumerate((slab, rel)):
        store_parts(tabs.at[i], pl.ds(0, 128), source[:, 0:128], split2)

    sub128 = lax.broadcasted_iota(jnp.int32, (128, 128), 0)
    sub256 = lax.broadcasted_iota(jnp.int32, (128, EB), 0)

    def gathered(idx, i, rows):
        onehot = jnp.transpose(jnp.where(idx[:, rows] == sub256, 1.0, 0.0)).astype(BF)
        return dot_nt(onehot, tabs[i, 0]) + dot_nt(onehot, tabs[i, 1])

    @pl.loop(0, SPANS)
    def _(i):
        rows = rows_of(i, EB)
        h = gathered(hr, 0, rows)
        r = gathered(rr, 1, rows)
        hbuf[rows, :] = h
        rbuf[rows, :] = r
        for k in range(CHUNKS + 1):
            hre, him, rre, rim = h[:, tile(k, 0)], h[:, tile(k, 1)], r[:, tile(k, 0)], r[:, tile(k, 1)]
            qown[rows, tile(k, 0)] = hre * rre - him * rim
            qown[rows, tile(k, 1)] = hre * rim + him * rre

    pl.semaphore_wait(barrier, 7)
    q_copy = remote(qown, qoth, 0)
    q_copy.start()

    @pl.loop(0, 2 * NEGS // 128)
    def _(i):
        x = slab[:, pl.ds(pl.multiple_of(TOUCHED + i * 128, 128), 128)]
        store_parts(nparts, rows_of(i, 128), x, split2)

    @pl.loop(0, SPANS)
    def _(i):
        rows = rows_of(i, EB)
        t = gathered(tr, 0, rows)
        tbuf[rows, :] = t
        q = qown[rows, :]
        pos[rows, :] = jnp.sum(q * t, axis=1, keepdims=True)
        place = pl.ds(pl.multiple_of(i * (2 * EB), EB), EB)
        for j, part in enumerate(split2(q)):
            qparts[j, place, :] = part

    def score(b, first):
        rows = pl.ds(b * 2 * EB + first, EB)
        negs = pl.ds(b * NEGS, NEGS)
        q, n = [qparts[j, rows, :] for j in range(2)], [nparts[j, :, negs] for j in range(2)]
        scores[rows, :] = (dot_nn(q[0], n[1]) + dot_nn(q[1], n[0])) + dot_nn(q[0], n[0])

    for b in range(SPANS):
        score(b, 0)
    q_copy.wait()

    @pl.loop(0, EDGES // 128)
    def _(i):
        place = pl.ds(pl.multiple_of((i // 2) * (2 * EB) + EB + (i % 2) * 128, 128), 128)
        for j, part in enumerate(split2(qoth[rows_of(i, 128), :])):
            qparts[j, place, :] = part

    for b in range(SPANS):
        score(b, EB)

    lane = lax.broadcasted_iota(jnp.int32, (EB, 128), 1)
    for b in range(SPANS):
        for own in range(2):
            rows = pl.ds(b * 2 * EB + (1 - own) * EB, EB)
            s = scores[rows, :]
            m = jnp.max(s, axis=1, keepdims=True)
            if own:
                p = pos[pl.ds(b * EB, EB), :]
                m = jnp.maximum(m, p)
            e = jnp.exp(s - m)
            total = jnp.sum(e, axis=1, keepdims=True)
            weight = jnp.zeros_like(total)
            if own:
                total = total + jnp.exp(p - m)
                weight = jnp.transpose(jnp.broadcast_to(weights[:, b * EB:(b + 1) * EB], (128, EB)))[:, 0:1]
            scores[rows, :] = e
            stat_own[rows, :] = jnp.where(lane == 0, m, jnp.where(lane == 1, total, weight))
    stat_copy = remote(stat_own, stat_oth, 1)
    stat_copy.start()

    for n, (first, second) in enumerate(((slab_owner, rel_owner), (slab_row, rel_row))):
        ints[n:n + 1, 0:SLAB] = first[...].reshape(1, SLAB)
        ints[n:n + 1, SLAB:ROWS] = second[...].reshape(1, RSLAB) + n * ROWS_DEV
    own = ints[0:1, :]
    oclass, oz = own % CLASSES, own // CLASSES
    owner_row = lax.broadcasted_iota(jnp.int32, (128, ROWS), 0)
    onehot = jnp.where(owner_row == oclass * NZ + oz, 1.0, 0.0)
    for start, size, offset in ((0, SLAB, 0), (SLAB, RSLAB, CAP)):
        part = onehot[:, start:start + size]
        upper = lax.broadcasted_iota(jnp.int32, (size, size), 0) <= lax.broadcasted_iota(jnp.int32, (size, size), 1)
        count = dot_nn(part.astype(BF), jnp.where(upper, 1.0, 0.0).astype(BF))
        kpos[:, start:start + size] = jnp.sum(part * count, axis=0, keepdims=True) + (offset - 1.0)
    kth = kpos[...].astype(jnp.int32)
    slots[0:1, :] = oclass * CSLOTS + kth * NZ + oz
    slots[1:2, :] = oclass * RSLOTS + kth
    for i in range(ROWS // 128):
        zmask[pl.ds(i * 128, 128), :] = jnp.transpose(jnp.where(oz[:, i * 128:(i + 1) * 128] == sub128 // REM, 1.0, 0.0))
    kth_hot = jnp.where(owner_row == kth, 1.0, 0.0).astype(BF)
    number = ints[1:2, :] + 1
    high = ((number // 16) * 16).astype(F32)
    low = (number % 16).astype(F32)
    ids[...] = (dot_nt((onehot * high).astype(BF), kth_hot) + dot_nt((onehot * low).astype(BF), kth_hot)).astype(jnp.int32) - 1

    stat_copy.wait()

    for b in range(SPANS):
        for own in range(2):
            rows = pl.ds(b * 2 * EB + (1 - own) * EB, EB)
            theirs = pl.ds(b * 2 * EB + own * EB, EB)
            a, o = stat_own[rows, :], stat_oth[theirs, :]
            m1, l1, m2, l2 = a[:, 0:1], a[:, 1:2], o[:, 0:1], o[:, 1:2]
            w = a[:, 2:3] if own else o[:, 2:3]
            peak = jnp.maximum(m1, m2)
            f1 = jnp.exp(m1 - peak)
            total = l1 * f1 + l2 * jnp.exp(m2 - peak)
            if own:
                mown[pl.ds(b * EB, EB), :] = w * (jnp.exp(pos[pl.ds(b * EB, EB), :] - peak) / total - 1.0)
            gn = scores[rows, :] * (f1 * (w / total))
            scores[rows, :] = gn
            for j, part in enumerate(split2(gn)):
                gnp[j, rows, :] = part
        gnt = jnp.transpose(scores[pl.ds(b * 2 * EB, 2 * EB), :])
        for j, part in enumerate(split2(gnt)):
            gnb[b, j] = part

    def put(rows, value, chunks):
        for n, k in enumerate(chunks):
            for g in range(2):
                part = value[:, tile(n, g)]
                if k == CHUNKS:
                    for shift in (REM, 2 * REM, 4 * REM):
                        part = part + pltpu.roll(part, shift, 1)
                    part = part * zmask[rows, :]
                hi, lo = split2(part)
                if k < 2:
                    first_g[k, 0, rows, tile(0, g)] = hi
                    first_g[k, 1, rows, tile(0, g)] = lo
                else:
                    ghi[rows, tile(k - 2, g)] = hi
                    glo[rows, tile(k - 2, g)] = lo

    row128 = lax.broadcasted_iota(jnp.int32, (128, EDGES), 0)
    qg_in = qoth

    def gradients(group, chunks):
        start, size = 256 * chunks[0], 256 * len(chunks)
        lanes = pl.ds(start, size)

        def query_part(b, own):
            rows, negs = pl.ds(b * 2 * EB + (1 - own) * EB, EB), pl.ds(b * NEGS, NEGS)
            hi, lo = gnp[0, rows, :], gnp[1, rows, :]
            n0, n1 = nparts[0, lanes, negs], nparts[1, lanes, negs]
            return dot_nt(hi, n1) + dot_nt(lo, n0) + dot_nt(hi, n0)

        copies = []
        for b in range(SPANS):
            rows = pl.ds(b * EB, EB)
            qg_out[rows, lanes] = query_part(b, 0)
            copies.append(remote(qg_out.at[rows, lanes], qg_in.at[rows, lanes], 2 + 2 * group + b))
            copies[-1].start()
        for b in range(SPANS):
            rows = pl.ds(b * EB, EB)
            tbuf[rows, lanes] = mown[rows, :] * tbuf[rows, lanes] + query_part(b, 1)
        for b in range(SPANS):
            edges = pl.ds(b * 2 * EB, 2 * EB)

            @pl.loop(0, NEGS // 256)
            def _(i):
                hi, lo = gnb[b, 0, rows_of(i, 256), :], gnb[b, 1, rows_of(i, 256), :]
                q0, q1 = qparts[0, edges, lanes], qparts[1, edges, lanes]
                value = dot_nn(hi, q1) + dot_nn(lo, q0) + dot_nn(hi, q0)
                put(pl.ds(pl.multiple_of(TOUCHED + b * NEGS + i * 256, 128), 256), value, chunks)
        for copy in copies:
            copy.wait()

        def spread(idx, other):
            @pl.loop(0, EDGES // 128)
            def _(i):
                rows = rows_of(i, 128)
                for n, k in enumerate(chunks):
                    if other is None:
                        values = [mown[rows, :] * qown[rows, tile(k, g)] for g in range(2)]
                    else:
                        gre, gim = (tbuf[rows, tile(k, g)] + qg_in[rows, tile(k, g)] for g in range(2))
                        ore, oim = other[rows, tile(k, 0)], other[rows, tile(k, 1)]
                        values = [gre * ore + gim * oim, gim * ore - gre * oim]
                    for g in range(2):
                        hi, lo = split2(values[g])
                        terms[0, rows, tile(n, g)] = hi
                        terms[1, rows, tile(n, g)] = lo
            onehot = jnp.where(idx[...] == row128, 1.0, 0.0).astype(BF)
            return dot_nn(onehot, terms[1, :, 0:size]) + dot_nn(onehot, terms[0, :, 0:size])

        head = spread(hr, rbuf)
        put(pl.ds(0, 128), head + spread(tr, None), chunks)
        put(pl.ds(SLAB, 128), spread(rr, hbuf), chunks)

    gradients(0, (0,))

    slot_row = lax.broadcasted_iota(jnp.int32, (4 * CSLOTS, ROWS), 0)

    def leg1(g, d):
        f = (grp + g) % 2
        there = (chip(d, 0) if g == 0 else chip(0, d), g)
        return pltpu.make_async_remote_copy(
            sbuf.at[g, ((x if g == 0 else y) + d) % 4], landed.at[d, f],
            l_ss.at[g, d], l_rs.at[d, f], device_id=there, device_id_type=MESH)

    pair = pltpu.make_async_remote_copy(
        sbuf.at[1 - grp, jnp.where(grp == 0, y, x)], landed.at[0, 1], l_ss.at[0, 0], l_rs.at[0, 1],
        device_id=peer, device_id_type=MESH)
    own_copy = pltpu.make_async_copy(sbuf.at[grp, jnp.where(grp == 0, x, y)], landed.at[0, 0], own_sem)
    for d in (1, 3, 2, 0):
        cx = (x + d) % 4
        hot = jnp.where(slot_row == slots[0:1, :] - cx * (4 * CSLOTS), 1.0, 0.0).astype(BF)
        perm[pl.ds(pl.multiple_of(cx * (4 * CSLOTS), 4 * CSLOTS), 4 * CSLOTS), :] = hot
        value = dot_nn(hot, first_g[0, 1]) + dot_nn(hot, first_g[0, 0])
        for cy in range(4):
            sbuf[0, cx, cy] = value[cy * CSLOTS:(cy + 1) * CSLOTS, :128]
            sbuf[1, cy, cx] = value[cy * CSLOTS:(cy + 1) * CSLOTS, 128:]
        if d:
            leg1(0, d).start()
    for d in (1, 3, 2):
        leg1(1, d).start()
    pair.start()
    own_copy.start()

    gradients(1, tuple(range(1, CHUNKS + 1)))
    outs = [pltpu.make_async_copy(a, b, out_sem.at[n]) for n, (a, b) in enumerate(((ghi, ghi_out), (glo, glo_out)))]
    for copy in outs:
        copy.start()

    def filled_copy(g, cx):
        part = filled.at[0, cx] if g == 0 else filled.at[1, :, cx]
        return pltpu.make_async_copy(part, filled_out.at[0, cx] if g == 0 else filled_out.at[1, :, cx], out_sem.at[2 + 2 * cx + g])

    @pl.loop(0, 4)
    def _(cx):
        hot = perm[pl.ds(pl.multiple_of(cx * (4 * CSLOTS), 4 * CSLOTS), 4 * CSLOTS), :]
        value = dot_nn(hot, first_g[1, 1]) + dot_nn(hot, first_g[1, 0])
        for cy in range(4):
            filled[0, cx, cy] = value[cy * CSLOTS:(cy + 1) * CSLOTS, :128]
            filled[1, cy, cx] = value[cy * CSLOTS:(cy + 1) * CSLOTS, 128:]
        for g in range(2):
            filled_copy(g, cx).start()

    @pl.loop(0, 4)
    def _(cx):
        for g in range(2):
            filled_copy(g, cx).wait()

    for copy in outs:
        copy.wait()
    own_copy.wait()
    pair.wait()
    for d in (1, 2, 3):
        for g in range(2):
            leg1(g, d).wait_send()
            pltpu.make_async_remote_copy(
                sbuf.at[0, 0], landed.at[d, g], l_ss.at[0, d], l_rs.at[d, g], device_id=peer, device_id_type=MESH).wait_recv()


def route_kernel(ghi_in, glo_in, slots, ids_send, filled, landed, ent_out, rel_out,
                 ghi, glo, ids_recv, perm, sbuf, srem, abuf, arem, rbuf, rrem, xrem,
                 tables, plus, minus,
                 ids_ss, ids_rs, a_ss, a_rs, b_ss, b_rs, own_sem, in_sem, p_ss, p_rs, m_ss, m_rs):
    ent, grp = lax.axis_index("ent"), lax.axis_index("grp")
    z, c = ent // CLASSES, ent % CLASSES
    x, y = c // NY, c % NY
    first, second = jnp.where(grp == 0, x, y), jnp.where(grp == 0, y, x)

    def chip(dx, dy, dz=0):
        return ((z + dz) % NZ) * CLASSES + ((x + dx) % NX) * NY + (y + dy) % NY

    def plane_peer(j, f):
        return (chip(j // NY, j % NY), (grp + f) % 2)

    def chip_z(dz):
        return (chip(0, 0, dz), grp)

    ins = [pltpu.make_async_copy(a, b, in_sem.at[n]) for n, (a, b) in enumerate(((ghi_in, ghi), (glo_in, glo)))]
    for copy in ins:
        copy.start()
    barrier = pltpu.get_barrier_semaphore()

    @pl.loop(0, CLASSES)
    def _(j):
        @pl.when(j > 0)
        def _():
            pl.semaphore_signal(barrier, inc=1, device_id=plane_peer(j, 0), device_id_type=MESH)
        pl.semaphore_signal(barrier, inc=1, device_id=plane_peer(j, 1), device_id_type=MESH)

    pl.semaphore_signal(barrier, inc=1, device_id=chip_z(1), device_id_type=MESH)
    pl.semaphore_signal(barrier, inc=1, device_id=chip_z(NZ - 1), device_id_type=MESH)

    slot = slots[0:1, :]

    def ids_copy(j, f):
        dx, dy = j // NY, j % NY
        cls = ((x + dx) % NX) * NY + (y + dy) % NY
        there = jnp.where((grp + f) % 2 == 0, dy * NX + dx, dx * NY + dy) * 2 + f
        return pltpu.make_async_remote_copy(
            ids_send.at[pl.ds(pl.multiple_of(cls * NZ, NZ), NZ)], ids_recv.at[there],
            ids_ss.at[j * 2 + f], ids_rs.at[there], device_id=plane_peer(j, f), device_id_type=MESH)

    def for_peers(act):
        @pl.loop(0, CLASSES)
        def _(j):
            @pl.when(j > 0)
            def _():
                act(j, 0)
            act(j, 1)

    def send_ids():
        for_peers(lambda j, f: ids_copy(j, f).start())
        ids_recv[0] = ids_send[pl.ds(pl.multiple_of(c * NZ, NZ), NZ), :]

    def bufs(k):
        if k == 0:
            return None, landed, rbuf.at[0]
        if k < CHUNKS:
            return filled if k == 1 else sbuf, abuf.at[k - 1], rbuf.at[k]
        return srem, arem, rrem

    def leg1(k, g, d):
        s, a, _ = bufs(k)
        f = (grp + g) % 2
        there = (chip(d, 0) if g == 0 else chip(0, d), g)
        return pltpu.make_async_remote_copy(
            s.at[g, ((x if g == 0 else y) + d) % 4], a.at[d, f],
            a_ss.at[k, g, d], a_rs.at[k, d, f], device_id=there, device_id_type=MESH)

    def leg1_pair(k):
        s, a, _ = bufs(k)
        return pltpu.make_async_remote_copy(
            s.at[1 - grp, second], a.at[0, 1],
            a_ss.at[k, 0, 0], a_rs.at[k, 0, 1], device_id=(ent, 1 - grp), device_id_type=MESH)

    def leg1_own(k):
        s, a, _ = bufs(k)
        return pltpu.make_async_copy(s.at[grp, first], a.at[0, 0], own_sem.at[k, 0])

    def leg2(k, d, e):
        _, a, r = bufs(k)
        there = jnp.where(grp == 0, chip(0, e), chip(e, 0))
        return pltpu.make_async_remote_copy(
            a.at[d, :, (second + e) % 4], r.at[e, d],
            b_ss.at[k, e, d], b_rs.at[k, e, d], device_id=(there, grp), device_id_type=MESH)

    def leg2_own(k, d):
        _, a, r = bufs(k)
        return pltpu.make_async_copy(a.at[d, :, second], r.at[0, d], own_sem.at[k, 1 + d])

    def send(k):
        with jax.named_scope("send%d" % k):
            leg1_own(k).start()
            leg1_pair(k).start()
            for d in (1, 3, 2):
                for g in range(2):
                    leg1(k, g, d).start()

    def forward(k):
        with jax.named_scope("forward%d" % k):
            for d in (0, 1, 3, 2):
                if k == 0:
                    pass
                elif d == 0:
                    leg1_own(k).wait()
                    leg1_pair(k).wait_recv()
                else:
                    for f in range(2):
                        _, a, _ = bufs(k)
                        pltpu.make_async_remote_copy(
                            a.at[d, f], a.at[d, f], a_ss.at[k, 0, d], a_rs.at[k, d, f],
                            device_id=(ent, 1 - grp), device_id_type=MESH).wait_recv()
                for e in (1, 3, 2):
                    leg2(k, d, e).start()
                leg2_own(k, d).start()

    def arrive(k):
        with jax.named_scope("arrive%d" % k):
            for d in range(4):
                leg2_own(k, d).wait()
                for e in (1, 3, 2):
                    leg2(k, d, e).wait_recv()

    slot_row = lax.broadcasted_iota(jnp.int32, (4 * CSLOTS, ROWS), 0)

    def fill(k, cx):
        with jax.named_scope("fill%d" % k):
            rows = pl.ds(pl.multiple_of(cx * (4 * CSLOTS), 4 * CSLOTS), 4 * CSLOTS)
            if k == 2:
                perm[rows, 0:ROWS] = jnp.where(slot_row == slot - cx * (4 * CSLOTS), 1.0, 0.0).astype(BF)
            hot = perm[rows, 0:ROWS]
            lanes = pl.ds(0, 256)
            value = dot_nn(hot, glo[:, lanes]) + dot_nn(hot, ghi[:, lanes])
            for cy in range(4):
                sbuf[0, cx, cy] = value[cy * CSLOTS:(cy + 1) * CSLOTS, :128]
                sbuf[1, cy, cx] = value[cy * CSLOTS:(cy + 1) * CSLOTS, 128:]

    def fill_all(k):
        @pl.loop(0, 4)
        def _(cx):
            fill(k, cx)

    def fill_rem():
        with jax.named_scope("fill_rem"):
            row = lax.broadcasted_iota(jnp.int32, (CLASSES * RSLOTS, ROWS), 0)
            hot = jnp.where(row == slots[1:2, :], 1.0, 0.0).astype(BF)
            lanes = pl.ds(GW, 256)
            value = dot_nn(hot, glo[:, lanes]) + dot_nn(hot, ghi[:, lanes])
            for cls in range(CLASSES):
                part = value[cls * RSLOTS:(cls + 1) * RSLOTS, :]
                srem[0, cls // NY, cls % NY] = part[:, :128]
                srem[1, cls % NY, cls // NY] = part[:, 128:]

    def ring_rows(k):
        return TABLE_REM if k == WITH_REM else TABLE

    def ring_part(k, s, sign, h):
        n = ring_rows(k) // 2
        if s == 0:
            return pl.ds(h * n + (0 if sign > 0 else n // 2), n // 2)
        return pl.ds(h * n, n)

    def ring_copy(k, s, sign, h):
        o = (z + sign * (4 - s) + NZ) % NZ
        ss, rs = (p_ss, p_rs) if sign > 0 else (m_ss, m_rs)
        part = ring_part(k, s, sign, h)
        return pltpu.make_async_remote_copy(
            tables.at[k, o, part], (plus if sign > 0 else minus).at[k, s, part],
            ss.at[k, s, h], rs.at[k, s, h], device_id=chip_z(sign % NZ), device_id_type=MESH)

    def ring_start(k):
        for h in range(2):
            for sign in (1, -1):
                ring_copy(k, 0, sign, h).start()

    def ring_next(k, s):
        with jax.named_scope("ring%d_%d" % (k, s)):
            for h in range(2):
                for sign in (1, -1):
                    ring_copy(k, s, sign, h).wait_recv()
                    if s == 3:
                        continue
                    o = (z + sign * (3 - s) + NZ) % NZ
                    part = ring_part(k, s, sign, h)
                    tables[k, o, part, :] = tables[k, o, part, :] + (plus if sign > 0 else minus)[k, s, part, :]
                    ring_copy(k, s + 1, sign, h).start()
            if s < 3:
                return
            total = tables[k, z, 0:ring_rows(k), :] + (plus[k, 3, 0:ring_rows(k), :] + minus[k, 3, 0:ring_rows(k), :])
            turned = jnp.transpose(total[0:TABLE, :])
            rows = pl.ds(k * 128, 128)
            ent_out[rows, :] = turned[:, 0:ROWS_DEV]
            rel_out[rows, :] = turned[:, ROWS_DEV:ROWS_DEV + REL_DEV]
            if k == WITH_REM:
                rows = pl.ds(CHUNKS * 128, REM)
                for i in range(TABLE // 128):
                    part = total[TABLE + i * REM:TABLE + (i + 1) * REM, :]
                    if i < ROWS_DEV // 128:
                        ent_out[rows, i * 128:(i + 1) * 128] = part
                    else:
                        rel_out[rows, :] = part[:, 0:REL_DEV]

    def place(o):
        return pl.ds(pl.multiple_of((o // 2) * TABLE, TABLE), TABLE), pl.ds(pl.multiple_of((o % 2) * 768, 768), DEPTH)

    def build_place():
        with jax.named_scope("place"):
            @pl.loop(1, PEERS)
            def _(n):
                pltpu.make_async_remote_copy(
                    ids_recv.at[n], ids_recv.at[n], ids_ss.at[n], ids_rs.at[n],
                    device_id=(ent, 1 - grp), device_id_type=MESH).wait_recv()
            got = jnp.concatenate([ids_recv[n][:, 0:SLOTS] for n in range(PEERS)], axis=1)
            row = lax.broadcasted_iota(jnp.int32, (TABLE, DEPTH), 0)
            for o in range(NZ):
                perm[place(o)] = jnp.where(row == got[o:o + 1, :], 1.0, 0.0).astype(BF)

    def add_up(k):
        with jax.named_scope("add%d" % k):
            flat = rbuf.at[k].reshape(PEERS * CSLOTS, 128)
            for n in (4, 3, 5, 2, 6, 1, 7, 0):
                o = (z + n) % NZ
                hi, lo = split2(flat[pl.ds(o, DEPTH, stride=NZ), :])
                value = dot_nn(perm[place(o)], jnp.concatenate([hi, lo], axis=1))
                tables[k, o, 0:TABLE, :] = value[:, :128] + value[:, 128:]
                if n == 4:
                    ring_start(k)

    def add_up_rem():
        with jax.named_scope("add_rem"):
            for e in range(4):
                for d in range(4):
                    for f in range(2):
                        n = (e * 4 + d) * 2 + f
                        xrem[pl.ds(n * SLOTS, SLOTS), :] = rrem[e, d, f][0:SLOTS, :]
            group = lax.broadcasted_iota(jnp.int32, (DEPTH, 128), 1) // REM
            total = jnp.zeros((TABLE, 256), F32)
            for o in range(NZ):
                hi, lo = split2(jnp.where(group == o, xrem[...], 0.0))
                total = total + dot_nn(perm[place(o)], jnp.concatenate([hi, lo], axis=1))
            total = jnp.transpose(total[:, :128] + total[:, 128:])
            for o in range(NZ):
                for i in range(TABLE // 128):
                    tables[WITH_REM, o, TABLE + i * REM:TABLE + (i + 1) * REM, :] = total[o * REM:(o + 1) * REM, i * 128:(i + 1) * 128]
                tables[WITH_REM, o, TABLE + 5 * REM:TABLE_REM, :] = jnp.zeros((TABLE_REM - TABLE - 5 * REM, 128), F32)

    rem = CHUNKS
    pl.semaphore_wait(barrier, PEERS - 1 + 2)
    for d in range(4):
        leg2(0, d, 1).start()
    send_ids()
    for d in range(4):
        for e in (3, 2):
            leg2(0, d, e).start()
        leg2_own(0, d).start()
    for copy in ins:
        copy.wait()
    fill_rem()
    send(rem)
    send(1)
    fill_all(2)
    build_place()
    arrive(0)
    add_up(0)
    forward(rem)
    ring_next(0, 0)
    forward(1)
    send(2)
    ring_next(0, 1)
    arrive(rem)
    add_up_rem()
    ring_next(0, 2)
    arrive(1)
    add_up(1)
    ring_next(1, 0)
    ring_next(0, 3)
    forward(2)
    ring_next(1, 1)
    ring_next(1, 2)
    arrive(2)
    add_up(2)

    def legs_sent(k):
        if k:
            leg1_pair(k).wait_send()
            for d in (1, 2, 3):
                for g in range(2):
                    leg1(k, g, d).wait_send()
        for d in range(4):
            for e in (1, 2, 3):
                leg2(k, d, e).wait_send()

    def ring_sent(k):
        for s in range(4):
            for h in range(2):
                ring_copy(k, s, 1, h).wait_send()
                ring_copy(k, s, -1, h).wait_send()

    ring_next(2, 0)
    ring_next(1, 3)
    for_peers(lambda j, f: ids_copy(j, f).wait_send())
    legs_sent(0)
    legs_sent(1)
    legs_sent(rem)
    ring_sent(0)
    ring_next(2, 1)
    legs_sent(2)
    ring_sent(1)
    ring_next(2, 2)
    ring_next(2, 3)
    ring_sent(2)


def vmem():
    return pl.BlockSpec(memory_space=pltpu.VMEM)


def anywhere():
    return pl.BlockSpec(memory_space=pl.ANY)


def local_call(*args):
    dma = pltpu.SemaphoreType.DMA
    return pl.pallas_call(
        local_kernel,
        out_shape=(jax.ShapeDtypeStruct((ROWS, GW + 256), BF), jax.ShapeDtypeStruct((ROWS, GW + 256), BF),
                   jax.ShapeDtypeStruct((2, ROWS), jnp.int32), jax.ShapeDtypeStruct((128, 128), jnp.int32),
                   jax.ShapeDtypeStruct((2, 4, 4, CSLOTS, 128), F32), jax.ShapeDtypeStruct((4, 2, 4, CSLOTS, 128), F32)),
        in_specs=[vmem()] * len(args),
        out_specs=(anywhere(), anywhere(), vmem(), vmem(), anywhere(), anywhere()),
        scratch_shapes=[
            pltpu.VMEM((ROWS, GW + 256), BF),
            pltpu.VMEM((ROWS, GW + 256), BF),
            pltpu.VMEM((2, 4, 4, CSLOTS, 128), F32),
            pltpu.VMEM((2, ROWS), jnp.int32),
            pltpu.VMEM((1, ROWS), F32),
            pltpu.VMEM((ROWS, 128), F32),
            pltpu.VMEM((2, 2, W, 128), BF),
            pltpu.VMEM((2, W, 2 * NEGS), BF),
            pltpu.VMEM((EDGES, W), F32),
            pltpu.VMEM((EDGES, W), F32),
            pltpu.VMEM((EDGES, W), F32),
            pltpu.VMEM((EDGES, 1), F32),
            pltpu.VMEM((EDGES, W), F32),
            pltpu.VMEM((EDGES, W), F32),
            pltpu.VMEM((2, 2 * EDGES, W), BF),
            pltpu.VMEM((2 * EDGES, NEGS), F32),
            pltpu.VMEM((2 * EDGES, 128), F32),
            pltpu.VMEM((2 * EDGES, 128), F32),
            pltpu.VMEM((EDGES, 1), F32),
            pltpu.VMEM((2, 2 * EDGES, NEGS), BF),
            pltpu.VMEM((SPANS, 2, NEGS, 2 * EB), BF),
            pltpu.VMEM((EDGES, W), F32),
            pltpu.VMEM((2, EDGES, 256 * CHUNKS), BF),
            pltpu.VMEM((2, 2, ROWS, 256), BF),
            pltpu.VMEM((CLASSES * CSLOTS, ROWS), BF),
            pltpu.VMEM((2, 4, 4, CSLOTS, 128), F32),
            dma((6,)), dma((6,)), dma((2, 4)), dma((4, 2)), dma, dma((10,)),
        ],
        compiler_params=pltpu.CompilerParams(collective_id=0, has_side_effects=True, vmem_limit_bytes=63 * MiB),
        name="local",
    )(*args)


def route_call(*args):
    dma = pltpu.SemaphoreType.DMA
    return pl.pallas_call(
        route_kernel,
        out_shape=(jax.ShapeDtypeStruct((K, ROWS_DEV), F32), jax.ShapeDtypeStruct((K, REL_DEV), F32)),
        in_specs=[anywhere(), anywhere(), vmem(), vmem(), anywhere(), anywhere()],
        out_specs=(vmem(), vmem()),
        scratch_shapes=[
            pltpu.VMEM((ROWS, GW + 256), BF),
            pltpu.VMEM((ROWS, GW + 256), BF),
            pltpu.VMEM((PEERS, NZ, 128), jnp.int32),
            pltpu.VMEM((CLASSES * CSLOTS, 1536), BF),
            pltpu.VMEM((2, 4, 4, CSLOTS, 128), F32),
            pltpu.VMEM((2, 4, 4, RSLOTS, 128), F32),
            pltpu.VMEM((CHUNKS - 1, 4, 2, 4, CSLOTS, 128), F32),
            pltpu.VMEM((4, 2, 4, RSLOTS, 128), F32),
            pltpu.VMEM((CHUNKS, 4, 4, 2, CSLOTS, 128), F32),
            pltpu.VMEM((4, 4, 2, RSLOTS, 128), F32),
            pltpu.VMEM((DEPTH, 128), F32),
            pltpu.VMEM((CHUNKS, NZ, TABLE_REM, 128), F32),
            pltpu.VMEM((CHUNKS, 4, TABLE_REM, 128), F32),
            pltpu.VMEM((CHUNKS, 4, TABLE_REM, 128), F32),
            dma((PEERS,)), dma((PEERS,)),
            dma((CHUNKS + 1, 2, 4)), dma((CHUNKS + 1, 4, 2)), dma((CHUNKS + 1, 4, 4)), dma((CHUNKS + 1, 4, 4)),
            dma((CHUNKS + 1, 5)), dma((2,)),
            dma((CHUNKS, 4, 2)), dma((CHUNKS, 4, 2)), dma((CHUNKS, 4, 2)), dma((CHUNKS, 4, 2)),
        ],
        compiler_params=pltpu.CompilerParams(collective_id=1, has_side_effects=True, vmem_limit_bytes=63 * MiB),
        name="route",
    )(*args)


def emit_kernel(ent_in, rel_in, ent_out, rel_out):
    ent_out[...] = ent_in[...]
    rel_out[...] = rel_in[...]


def emit_call(ent, rel):
    return pl.pallas_call(
        emit_kernel,
        out_shape=(jax.ShapeDtypeStruct(ent.shape, F32), jax.ShapeDtypeStruct(rel.shape, F32)),
        in_specs=[vmem()] * 2,
        out_specs=(vmem(), vmem()),
        name="emit",
    )(ent, rel)


def body(slab, slab_owner, slab_row, rel_slab, rel_owner, rel_row, heads, tails, rels, weights):
    rows = [v.reshape(1, EDGES) for v in (heads, tails, rels, weights)]
    places = [slab_owner.reshape(1, SLAB), slab_row, rel_owner.reshape(1, RSLAB), rel_row]
    ent_grad, rel_grad = emit_call(*route_call(*local_call(slab.T, rel_slab.T, *rows, *places)))
    return ent_grad.T, rel_grad.T


def solution(mesh):
    split = P(("ent", "grp"))
    wide = P(("ent", "grp"), None)
    in_specs = (wide, wide, split, wide, wide, split, split, split, split, split)
    out_specs = (P("ent", "grp"), P("ent", "grp"))
    return jax.shard_map(body, mesh=mesh, in_specs=in_specs, out_specs=out_specs, check_vma=False)
```
